128 devices in a mesh: az: 32 (over y_lo, x, z), ax: 4 (over y_hi, core).
Axes of the slice: x: 4, y: 4 (y_hi: 2, y_lo: 2; y = y_hi * 2 + y_lo), z: 4, core: 2. Of those that a mesh axis runs over, the one named last changes fastest.
Arguments:
- initial: float32 [512, 64, 512], P('az', 'ax'), may hold values from -6 to 6
- target: float32 [512, 64, 512], P('az', 'ax'), may hold values from -6 to 6
- basis: float32 [16, 64, 512], P(None, 'ax'), may hold values from -0.25 to 0.25
- coefficients: float32 [16], replicated, may hold values from -4 to 4
- blade: float32 [2, 512], P(None, 'az'), may hold values from 0.3 to 3
- offset: int32 [2], replicated, may hold values from 256 to 511, as said below
- extra: int32 [2, 512], P(None, 'az'), may hold values from 0 to 1
- frac: float32 [2, 512], P(None, 'az'), may hold values from 0 to 1
Outputs:
- final_field: float32 [512, 64, 512], P('az', 'ax')
- sensitivity: float32 [512, 64, 512], P('az', 'ax')
- gradient: float32 [16], replicated
- loss: float32 [], replicated
The draws below stay inside these ranges and needn't reach their ends.
Inputs may be any that keep to these rules, and one draw needn't show every extreme that they name: offset[0] lies in 256 to 271; offset[1] is 511.
All inputs are finite; a program needn't handle non-finite values.
Results may differ from the reference program's by a relative error of at most 0.00018.
Values sent between devices are 32-bit elements; how exact they have to be, the bound alone decides.
A program may use at most 64 MiB of HBM per device.

```python
import math
import jax
import jax.numpy as jnp
from jax import lax

AZD = 16
NR = 512
NCOEF = 16
STEPS = 2
NAZ = 512
NAX = 64
RI = 256
CELLS = 16777216


def draw_offset(key, part):
    key = jax.random.fold_in(key, 7)
    drift = jax.random.randint(key, (), 0, AZD, dtype=jnp.int32)
    first = jnp.int32(NAZ // 2) + drift
    last = jnp.int32(NAZ - 1) + 0 * drift
    return jnp.stack([first, last]).astype(jnp.int32)


def place_ends(values, key, low, largest):
    longest = values.shape.index(max(values.shape))
    spots = []
    for shift in (0, 1):
        where = [jax.random.randint(jax.random.fold_in(key, axis), (), 0, length) for axis, length in enumerate(values.shape)]
        where[longest] = (where[longest] + shift) % values.shape[longest]
        spots.append(tuple(where))
    return values.at[spots[0]].set(low).at[spots[1]].set(largest)


def block_scale(key, shape, pieces, smallest, top_value):
    loudness = 1.0
    for dim, shards_of in pieces:
        steps = jax.random.uniform(jax.random.fold_in(jax.random.fold_in(key, 6), dim), (shards_of,), jnp.float32, smallest / len(pieces), top_value / len(pieces))
        loudness = loudness * jnp.repeat(jnp.exp(steps), shape[dim] // shards_of).reshape((-1,) + (1,) * (len(shape) - 1 - dim))
    return loudness


def gaussian(own_key, shape, spread, limit, pieces=(), kind=jnp.bfloat16):
    array = spread * jax.random.normal(own_key, shape, jnp.float32)
    if pieces:
        array = array * block_scale(own_key, shape, pieces, -0.22, 0.18)
    return jnp.clip(array, -limit, limit).astype(kind)


def setup_inputs(seed: int = 0) -> dict:
    splits = jax.random.split(jax.random.key(seed), 9)
    return {
        "initial": gaussian(splits[0], (NAZ, NAX, NR), 1.0, 6.0, ((0, 32), (1, 4)), jnp.float32),
        "target": gaussian(splits[1], (NAZ, NAX, NR), 1.0, 6.0, ((0, 32), (1, 4)), jnp.float32),
        "basis": gaussian(splits[2], (NCOEF, NAX, NR), NR ** -0.5, 0.25, ((1, 4),), jnp.float32),
        "coefficients": gaussian(splits[3], (NCOEF,), 1.0, 4.0, (), jnp.float32),
        "blade": jnp.clip(jnp.exp(math.log(3.0) - 2.3025851 * jax.random.uniform(splits[4], (STEPS, NAZ), jnp.float32) ** block_scale(splits[4], (STEPS, NAZ), ((1, 32),), -0.2, 0.2)), 0.3, 3.0),
        "offset": draw_offset(jax.random.fold_in(splits[8], 71), 0),
        "extra": place_ends(jax.random.randint(splits[6], (STEPS, NAZ), 0, 2), jax.random.fold_in(splits[6], 1), 0, 1).astype(jnp.int32),
        "frac": jnp.clip(1.0 * jax.random.uniform(splits[7], (STEPS, NAZ), jnp.float32) ** block_scale(splits[7], (STEPS, NAZ), ((1, 32),), -0.2, 0.2), 0.0, 1.0),
    }


diffusion = 0.12
advection = 0.2
coupling = 0.12

def radial_term(field):
    padded = jnp.pad(field, ((0, 0), (0, 0), (1, 1)))
    faces = padded[:, :, 1:] - padded[:, :, :-1]
    keep = (jnp.arange(NR + 1, dtype=jnp.int32) != RI).astype(jnp.float32)
    faces = faces * keep
    return faces[:, :, 1:] - faces[:, :, :-1]

def operator(field, step, offset, extra, frac, forward):
    padded = jnp.pad(field, ((0, 0), (1, 1), (0, 0)))
    lower = jnp.roll(field, 1, 0)
    upper = jnp.roll(field, -1, 0)
    lap = upper + lower + padded[:, 2:] + padded[:, :-2] - 4.0 * field + radial_term(field)
    if forward:
        adv = field - lower
    else:
        adv = field - upper
    stator = field[:, :, RI]
    rotor = field[:, :, RI - 1]
    cells = jnp.arange(NAZ, dtype=jnp.int32)
    first = (cells + offset[step] + extra[step]) % NAZ
    second = (first + 1) % NAZ
    weight = frac[step][:, None]
    interp = (1.0 - weight) * stator[first] + weight * stator[second]
    flux = interp - rotor
    back = jnp.zeros((NAZ, NAX), jnp.float32).at[first].add((1.0 - weight) * flux).at[second].add(weight * flux)
    result = diffusion * lap - advection * adv
    result = result.at[:, :, RI - 1].add(coupling * flux)
    result = result.at[:, :, RI].add(-coupling * back)
    return result

def reference(initial, target, basis, coefficients, blade, offset, extra, frac):

    def forward_run(start, coefs):
        profile = jnp.tensordot(coefs, basis, axes=1, precision=lax.Precision.HIGHEST)
        field = start
        for step in range(STEPS):
            source = blade[step][:, None, None] * profile[None]
            field = field + operator(field, step, offset, extra, frac, True) + source
        return field
    final_field, pullback = jax.vjp(forward_run, initial, coefficients)
    misfit = final_field - target
    loss = 0.5 * jnp.sum(misfit * misfit) / CELLS
    sensitivity, coef_grad = pullback(misfit)
    gradient = coef_grad / (NAZ * NAX)
    return (final_field, sensitivity, gradient, loss)
```

```python
import functools

import jax
import jax.numpy as jnp
from jax import lax
from jax.experimental import pallas as pl
from jax.experimental.pallas import tpu as pltpu
from jax.sharding import PartitionSpec as P

MESH = pl.DeviceIdType.MESH
f32 = jnp.float32
HI = lax.Precision.HIGHEST

NA, NX = 32, 4
J, Z, R, M = 16, 16, 512, 16
RI = 256
DIFF, ADV = 0.12, 0.2
COLUMNS = NA * J * NX * Z

NEAR = [(a, c) for a in (-1, 0, 1) for c in (-1, 0, 1) if (a, c) != (0, 0)]
FAR = [(a, c) for a in (14, 15, 16, 17, 18) for c in (-1, 0, 1)]
PARTNERS = FAR + NEAR


def slot_of(a, c):
    return [((x + 8) % NA, y) for x, y in PARTNERS].index(((a + 8) % NA, c))


def lane_iota(shape):
    return lax.broadcasted_iota(jnp.int32, shape, len(shape) - 1)


def row_iota(shape):
    return lax.broadcasted_iota(jnp.int32, shape, len(shape) - 2)


def left(v):
    return pltpu.roll(v, v.shape[-1] - 1, v.ndim - 1)


def right(v):
    return pltpu.roll(v, 1, v.ndim - 1)


def kernel(
    u_h, t_h, basis_h, coef_h, blade_h, off_h, extra_h, frac_h,
    fin, sen, tot,
    x0, u1, l2, l1, tg, bs, bh, prof, m1s, m1r, m2s, m2r, rrs, rrr, bb,
    blade_v, extra_v, frac_v, coef_s, off_s,
    loc, near_ss, near_rs, m_ss, m_rs, side_ss, side_rs, rr_ss, rr_rs,
):
    az, ax = lax.axis_index("az"), lax.axis_index("ax")
    me = az * NX + ax

    def partner(a, c):
        return (lax.rem(az + a + NA, NA), lax.rem(ax + c + NX, NX))

    def ranked(k):
        t = lax.rem(me + k, NA * NX)
        return (t // NX, lax.rem(t, NX))

    barrier = pltpu.get_barrier_semaphore()

    def greet(k, _):
        pl.semaphore_signal(barrier, inc=1, device_id=ranked(k + 1), device_id_type=MESH)
        return 0

    lax.fori_loop(0, NA * NX - 1, greet, 0)

    loads = [
        pltpu.make_async_copy(u_h, x0.at[2:18, 8:24, :], loc.at[0]),
        pltpu.make_async_copy(basis_h, bs, loc.at[1]),
        pltpu.make_async_copy(coef_h, coef_s, loc.at[2]),
        pltpu.make_async_copy(off_h, off_s, loc.at[3]),
        pltpu.make_async_copy(blade_h, blade_v, loc.at[4]),
        pltpu.make_async_copy(extra_h, extra_v, loc.at[5]),
        pltpu.make_async_copy(frac_h, frac_v, loc.at[6]),
        pltpu.make_async_copy(t_h, tg, loc.at[7]),
    ]
    for c in loads:
        c.start()

    m1s[...] = jnp.zeros((24, 128), f32)
    for c in loads:
        c.wait()
    lane = lane_iota((Z, 128))

    def take(j, carry):
        rot, sta = carry
        a = pltpu.roll(x0[j + 2, 8:24, 128:256], j + 1, 1)
        b = pltpu.roll(x0[j + 2, 8:24, 256:384], j + 16, 1)
        return jnp.where(lane == j, a, rot), jnp.where(lane == j + 16, b, sta)

    zero = jnp.zeros((Z, 128), f32)
    rot, sta = lax.fori_loop(0, J, take, (zero, zero))
    m1s[0:16, :] = rot + sta
    m1s[16:18, 0:16] = extra_v[...].astype(f32)
    m1s[18:20, 0:16] = frac_v[...]
    m1s[20:22, 0:16] = blade_v[...]

    def mix(m, acc):
        return acc + coef_s[m] * bs[m]

    prof[8:24, :] = lax.fori_loop(0, M, mix, jnp.zeros((Z, R), f32))

    pl.semaphore_wait(barrier, NA * NX - 1)

    plane_src = {-1: pl.ds(0, 2), 0: pl.ds(0, 16), 1: pl.ds(14, 2)}
    row_src = {-1: pl.ds(0, 2), 0: pl.ds(0, 16), 1: pl.ds(14, 2)}
    plane_dst = {-1: pl.ds(18, 2), 0: pl.ds(2, 16), 1: pl.ds(0, 2)}
    row_dst = {-1: pl.ds(24, 2), 0: pl.ds(8, 16), 1: pl.ds(6, 2)}
    plane_own = {-1: pl.ds(2, 2), 0: pl.ds(2, 16), 1: pl.ds(16, 2)}
    row_own = {-1: pl.ds(8, 2), 0: pl.ds(8, 16), 1: pl.ds(22, 2)}

    def near_copy(src, dst, a, c, n):
        i = NEAR.index((a, c))
        return pltpu.make_async_remote_copy(
            src_ref=src, dst_ref=dst.at[plane_dst[a], row_dst[c], :],
            send_sem=near_ss.at[n, i], recv_sem=near_rs.at[n, i],
            device_id=partner(a, c), device_id_type=MESH,
        )

    def message(src, dst, a, c, n):
        return pltpu.make_async_remote_copy(
            src_ref=src, dst_ref=dst.at[slot_of(-a, -c)],
            send_sem=m_ss.at[n], recv_sem=m_rs.at[n],
            device_id=partner(a, c), device_id_type=MESH,
        )

    first = [near_copy(u_h.at[plane_src[a], row_src[c], :], x0, a, c, 0) for a, c in NEAR]
    far1 = [message(m1s, m1r, a, c, 0) for a, c in PARTNERS]
    side = []
    for i, (c, src, dst) in enumerate(((1, 23, 7), (-1, 8, 24))):
        side.append(pltpu.make_async_remote_copy(
            src_ref=prof.at[pl.ds(src, 1), :], dst_ref=prof.at[pl.ds(dst, 1), :],
            send_sem=side_ss.at[0, i], recv_sem=side_rs.at[0, i],
            device_id=partner(0, c), device_id_type=MESH))
        side.append(pltpu.make_async_remote_copy(
            src_ref=basis_h.at[:, pl.ds(src - 8, 1), :], dst_ref=bh.at[i],
            send_sem=side_ss.at[1, i], recv_sem=side_rs.at[1, i],
            device_id=partner(0, c), device_id_type=MESH))
    for c in far1 + first + side:
        c.start()

    def whole(ref, ss, rs):
        return pltpu.make_async_remote_copy(
            src_ref=ref, dst_ref=ref, send_sem=ss, recv_sem=rs, device_id=partner(0, 1), device_id_type=MESH)

    whole(m1r, m_ss.at[0], m_rs.at[0]).wait_recv()

    lane32 = lane_iota((32, 128))
    lane8 = lane_iota((8, 128))

    def ext_rows(own, ref, a):
        def part(c, lo, hi):
            return own[lo:hi, :] if (a, c) == (0, 0) else ref[slot_of(a, c), lo:hi, :]
        return jnp.concatenate([part(-1, 8, 16), part(0, 0, 16), part(1, 0, 8)], axis=0)

    def gather_cols(own, ref, offsets, ncols):
        cols = [jnp.zeros((32, 128), f32) for _ in range(ncols)]
        for b, a in enumerate(offsets):
            v = ext_rows(own, ref, a)
            here = (lane32 >= 16 * b) & (lane32 < 16 * b + 16)
            for i in range(ncols):
                s = (16 * (b - i)) % 128
                cols[i] = jnp.where(here, pltpu.roll(v, s, 1) if s else v, cols[i])
        return cols

    def gather_meta(offsets):
        out = jnp.zeros((8, 128), f32)
        for b, a in enumerate(offsets):
            v = m1s[16:24, :] if a == 0 else m1r[slot_of(a, 0), 16:24, :]
            here = (lane8 >= 16 * b) & (lane8 < 16 * b + 16)
            out = jnp.where(here, pltpu.roll(v, 16 * b, 1) if b else v, out)
        return out

    near_off, far_off = (-1, 0, 1), (14, 15, 16, 17, 18)
    rot_n, sta_n = gather_cols(m1s, m1r, near_off, 2)
    rot_f, sta_f = gather_cols(m1s, m1r, far_off, 2)
    meta_n, meta_f = gather_meta(near_off), gather_meta(far_off)

    drift = off_s[0] - RI
    rows = row_iota((128, 128))
    lanes = lane_iota((128, 128))

    def weights(meta, base):
        w = meta[2:3, :]
        at = lanes + (drift + base) + meta[0:1, :].astype(jnp.int32)
        return jnp.where(rows == at, 1.0 - w, 0.0) + jnp.where(rows == at + 1, w, 0.0)

    w_n = weights(meta_n, 16)
    w_f = weights(meta_f, -16)

    def opposite(rn, sn, rf, sf):
        flux = jnp.dot(sf, w_n, precision=HI, preferred_element_type=f32) - rn
        fluxf = jnp.dot(sn, w_f, precision=HI, preferred_element_type=f32) - rf
        back = lax.dot_general(fluxf, w_f, (((1,), (1,)), ((), ())), precision=HI, preferred_element_type=f32)
        return flux, back

    def local_weights(meta):
        e, w = meta[1:2, :], meta[3:4, :]
        return (1.0 - e) * (1.0 - w), (1.0 - e) * w + e * (1.0 - w), e * w

    lw_n, lw_f = local_weights(meta_n), local_weights(meta_f)

    def spread(lw, v):
        return lw[0] * right(v) + lw[1] * v + lw[2] * left(v)

    def collect(lw, v):
        return left(lw[0] * v) + lw[1] * v + right(lw[2] * v)

    bl0, bl1 = meta_n[4:5, :], meta_n[5:6, :]
    eb = spread(lw_n, bl0)
    c0 = (1.0 - 2 * DIFF) * bl0 + DIFF * (left(bl0) + right(bl0)) - ADV * (bl0 - right(bl0)) + bl1
    r32 = row_iota((32, 128))
    for i, v in enumerate((bl0, bl1, c0, collect(lw_n, bl0), collect(lw_n, eb), eb)):
        picked = jnp.where(lane32 == r32 + 15, jnp.broadcast_to(v, (32, 128)), 0.0)
        bb[i] = jnp.broadcast_to(jnp.sum(picked, axis=1, keepdims=True), (32, 128))

    def coef(i, q):
        return bb[i, pl.ds(q, 1), :]

    def wide(v):
        return jnp.concatenate([v] * 4, axis=1)

    ri = lane_iota((1, R))
    edge = (ri == RI - 1) | (ri == RI)
    ctr = jnp.where(edge, 1.0 - 5 * DIFF - ADV, 1.0 - 6 * DIFF - ADV).astype(f32)
    up = jnp.where((ri == RI - 1) | (ri == R - 1), 0.0, DIFF).astype(f32)
    dn = jnp.where((ri == RI) | (ri == 0), 0.0, DIFF).astype(f32)

    def stencil(v, strong, weak, vz):
        return ctr * v + up * left(v) + dn * right(v) + DIFF * (vz + weak) + (DIFF + ADV) * strong

    def beside(v):
        return pltpu.roll(v, 1, 0) + pltpu.roll(v, v.shape[0] - 1, 0)

    def put(ref, idx, rows_, v, flux, back, k):
        ln = lane_iota(flux.shape)
        f = jnp.where(ln == 127, pltpu.roll(flux, 127 - k, 1), 0.0)
        b = jnp.where(ln == 0, pltpu.roll(back, lax.rem(128 - k, 128), 1), 0.0)
        ref[idx, rows_, 0:128] = v[:, 0:128]
        ref[idx, rows_, 128:256] = v[:, 128:256] + DIFF * f
        ref[idx, rows_, 256:384] = v[:, 256:384] - DIFF * b
        ref[idx, rows_, 384:512] = v[:, 384:512]

    def seal(ref, n):
        @pl.when(ax == 0)
        def _():
            ref[:, pl.ds(8 - n, n), :] = jnp.zeros((ref.shape[0], n, R), f32)

        @pl.when(ax == NX - 1)
        def _():
            ref[:, pl.ds(24, n), :] = jnp.zeros((ref.shape[0], n, R), f32)

    flux0, back0 = opposite(rot_n, sta_n, rot_f, sta_f)

    for c in first + side:
        c.wait_recv()
    seal(x0, 2)
    ally = slice(0, 32)

    def step_u1(q, _):
        v = x0[q + 1]
        new = stencil(v, x0[q], x0[q + 2], beside(v)) + wide(coef(0, q)) * prof[...]
        put(u1, q, ally, new, flux0, back0, q + 15)
        return 0

    lax.fori_loop(0, 18, step_u1, 0)
    seal(u1, 1)

    def take1(q, carry):
        rot, sta = carry
        a = pltpu.roll(u1[q, 8:24, 128:256], q + 16, 1)
        b = pltpu.roll(u1[q, 8:24, 256:384], q + 15, 1)
        return jnp.where(lane == q + 15, a, rot), jnp.where(lane == q + 15, b, sta)

    rot1, sta1 = lax.fori_loop(0, 18, take1, (zero, zero))
    flux1 = spread(lw_n, sta1) - rot1
    back1 = collect(lw_n, flux1)

    centre = slice(8, 24)

    def step_u2(j, carry):
        ls, qs, ps, a1, a2, a3, cols = carry
        v = u1[j + 1]
        new = stencil(v[8:24], u1[j, 8:24, :], u1[j + 2, 8:24, :], beside(v)[8:24]) + wide(coef(1, j + 1)) * prof[8:24, :]
        put(fin, j, slice(0, 16), new, flux1, back1, j + 16)
        lam = fin[j] - tg[j]
        l2[j + 2, 8:24, :] = lam
        mid1, mid2 = lam[:, 128:256], lam[:, 256:384]
        cols = cols
        for i, (t, l) in enumerate(((mid1, 126), (mid1, 127), (mid2, 0), (mid2, 1))):
            k = j + 16 * i
            cols = jnp.where(lane == k, pltpu.roll(t, lax.rem(k + 128 - l, 128), 1), cols)
        q = j + 1
        return (ls + lam * lam, qs + wide(coef(2, q)) * lam, ps + wide(coef(0, q)) * lam,
                a1 + coef(3, q) * mid2, a2 + coef(4, q) * mid2, a3 + coef(5, q) * mid1, cols)

    big = jnp.zeros((Z, R), f32)
    ls, qs, ps, a1, a2, a3, cols = lax.fori_loop(0, J, step_u2, (big, big, big, zero, zero, zero, zero))
    m2s[...] = cols

    second = [near_copy(l2.at[plane_own[a], row_own[c], :], l2, a, c, 1) for a, c in NEAR]
    far2 = [message(m2s, m2r, a, c, 1) for a, c in PARTNERS]
    for c in far2 + second:
        c.start()

    zr = row_iota((Z, R))
    pz = jnp.where(zr == 0, 0.0, pltpu.roll(ps, 1, 0)) + jnp.where(zr == Z - 1, 0.0, pltpu.roll(ps, Z - 1, 0))
    vv = qs + (ctr - (1.0 - 6 * DIFF - ADV) - 4 * DIFF) * ps + up * left(ps) + dn * right(ps) + DIFF * pz
    at255 = jnp.where(lane == 127, left(a1) - ps[:, 128:256], 0.0)
    at256 = jnp.where(lane == 0, a2 - right(a3), 0.0)
    vv = vv + DIFF * jnp.concatenate([zero, at255, -at256, zero], axis=1)
    top = jnp.where(ax == 0, 0.0, DIFF) * ps[0:1, :]
    bot = jnp.where(ax == NX - 1, 0.0, DIFF) * ps[15:16, :]

    def fold(v):
        v = v[:, 0:128] + v[:, 128:256] + v[:, 256:384] + v[:, 384:512]
        return jnp.sum(v, axis=0, keepdims=True)

    rowsum = []
    for m in range(M):
        rowsum.append(fold(bs[m] * vv) + fold(bh[0, m] * top + bh[1, m] * bot))
    rowsum.append(fold(ls))
    rowsum.append(jnp.zeros((7, 128), f32))
    stack = jnp.concatenate(rowsum, axis=0)
    stack = jnp.broadcast_to(jnp.sum(stack, axis=1, keepdims=True), (24, 128))
    rrs[...] = jnp.sum(jnp.where(row_iota((24, 128)) == lane_iota((24, 128)), stack, 0.0), axis=0, keepdims=True)

    def tell(k, _):
        pltpu.make_async_remote_copy(
            src_ref=rrs, dst_ref=rrr.at[NA * NX - 2 - k], send_sem=rr_ss.at[0], recv_sem=rr_rs.at[0],
            device_id=ranked(k + 1), device_id_type=MESH).start()
        return 0

    lax.fori_loop(0, NA * NX - 1, tell, 0)

    whole(m2r, m_ss.at[1], m_rs.at[1]).wait_recv()
    zrow = row_iota((32, 128))
    inside = ((zrow >= 8) | (ax != 0)) & ((zrow < 24) | (ax != NX - 1))

    def adjoint_cols(cs, lw):
        c254, c255, c256, c257 = [jnp.where(inside, c, 0.0) for c in cs]
        flux = spread(lw, c256) - c255
        back = collect(lw, flux)

        def one(c, out, term):
            return (1.0 - 5 * DIFF - ADV) * c + DIFF * (out + right(c) + beside(c)) + (DIFF + ADV) * left(c) + DIFF * term

        return flux, back, one(c255, c254, flux), one(c256, c257, -back)

    flux_n, back_n, rot_n1, sta_n1 = adjoint_cols(gather_cols(m2s, m2r, near_off, 4), lw_n)
    _, _, rot_f1, sta_f1 = adjoint_cols(gather_cols(m2s, m2r, far_off, 4), lw_f)
    fluxa, backa = opposite(rot_n1[8:24], sta_n1[8:24], rot_f1[8:24], sta_f1[8:24])
    for c in second:
        c.wait_recv()
    seal(l2, 2)

    def step_l1(q, _):
        v = l2[q + 1]
        new = stencil(v, l2[q + 2], l2[q], beside(v))
        put(l1, q, ally, new, flux_n, back_n, q + 15)
        return 0

    lax.fori_loop(0, 18, step_l1, 0)
    seal(l1, 1)

    def step_l0(j, _):
        v = l1[j + 1]
        new = stencil(v[8:24], l1[j + 2, 8:24, :], l1[j, 8:24, :], beside(v)[8:24])
        put(sen, j, slice(0, 16), new, fluxa, backa, j + 16)
        return 0

    lax.fori_loop(0, J, step_l0, 0)

    whole(rrr, rr_ss.at[0], rr_rs.at[0]).wait_recv()
    total = rrs[...] + jnp.sum(rrr[...], axis=0)
    tot[...] = jnp.broadcast_to(total, (8, 128))

    for c in first + side + second:
        c.wait_send()
    whole(m1r, m_ss.at[0], m_rs.at[0]).wait_send()
    whole(m2r, m_ss.at[1], m_rs.at[1]).wait_send()
    whole(rrr, rr_ss.at[0], rr_rs.at[0]).wait_send()


def finish(fin, sen, tot, fin_o, sen_o, grad_o, loss_o, sems):
    a = pltpu.make_async_copy(fin, fin_o, sems.at[0])
    b = pltpu.make_async_copy(sen, sen_o, sems.at[1])
    a.start()
    b.start()
    row = tot[0:1, :]
    grad_o[...] = row[:, 0:M] * (1.0 / COLUMNS)
    loss_o[...] = row[:, M : M + 1] * (0.5 / (COLUMNS * R))
    a.wait()
    b.wait()


def on_device(initial, target, basis, coefficients, blade, offset, extra, frac):
    vm = pl.BlockSpec(memory_space=pltpu.VMEM)
    hbm = pl.BlockSpec(memory_space=pltpu.HBM)
    block = jax.ShapeDtypeStruct((J, Z, R), f32)
    np_ = len(PARTNERS)
    dma = pltpu.SemaphoreType.DMA
    fin, sen, tot = pl.pallas_call(
        kernel,
        out_shape=(block, block, jax.ShapeDtypeStruct((8, 128), f32)),
        in_specs=[hbm] * 8,
        out_specs=(vm, vm, vm),
        scratch_shapes=[
            pltpu.VMEM((20, 32, R), f32), pltpu.VMEM((18, 32, R), f32),
            pltpu.VMEM((20, 32, R), f32), pltpu.VMEM((18, 32, R), f32),
            pltpu.VMEM((J, Z, R), f32), pltpu.VMEM((M, Z, R), f32), pltpu.VMEM((2, M, 1, R), f32),
            pltpu.VMEM((32, R), f32),
            pltpu.VMEM((24, 128), f32), pltpu.VMEM((np_, 24, 128), f32),
            pltpu.VMEM((16, 128), f32), pltpu.VMEM((np_, 16, 128), f32),
            pltpu.VMEM((1, 128), f32), pltpu.VMEM((NA * NX - 1, 1, 128), f32),
            pltpu.VMEM((6, 32, 128), f32),
            pltpu.VMEM((2, J), f32), pltpu.VMEM((2, J), jnp.int32), pltpu.VMEM((2, J), f32),
            pltpu.SMEM((M,), f32), pltpu.SMEM((2,), jnp.int32),
            dma((8,)), dma((2, 8)), dma((2, 8)), dma((2,)), dma((2,)), dma((2, 2)), dma((2, 2)), dma((1,)), dma((1,)),
        ],
        compiler_params=pltpu.CompilerParams(collective_id=0, has_side_effects=True, vmem_limit_bytes=60 * 1024 * 1024),
    )(initial, target, basis, coefficients, blade, offset, extra, frac)
    fin, sen, grad, loss = pl.pallas_call(
        finish,
        out_shape=(block, block, jax.ShapeDtypeStruct((1, M), f32), jax.ShapeDtypeStruct((1, 1), f32)),
        in_specs=[vm] * 3,
        out_specs=(hbm, hbm, vm, vm),
        scratch_shapes=[dma((2,))],
    )(fin, sen, tot)
    return fin, sen, grad.reshape(M), loss.reshape(())


def solution(mesh):
    block = P("az", "ax", None)
    row = P(None, "az")
    return jax.shard_map(
        on_device,
        mesh=mesh,
        in_specs=(block, block, P(None, "ax", None), P(), row, P(), row, row),
        out_specs=(block, block, P(), P()),
        check_vma=False,
    )
```

```python
import functools

import jax
import jax.numpy as jnp
from jax import lax
from jax.experimental import pallas as pl
from jax.experimental.pallas import tpu as pltpu
from jax.sharding import PartitionSpec as P

MESH = pl.DeviceIdType.MESH
f32 = jnp.float32
HI = lax.Precision.HIGHEST

NA, NX = 32, 4
J, Z, R, M = 16, 16, 512, 16
RI = 256
DIFF, ADV = 0.12, 0.2
COLUMNS = NA * J * NX * Z

NEAR = [(a, c) for a in (-1, 0, 1) for c in (-1, 0, 1) if (a, c) != (0, 0)]
FAR = [(a, c) for a in (14, 15, 16, 17, 18) for c in (-1, 0, 1)]
GROUPS = (0, 1, -1)
PARTNERS = {g: [(a, c) for a, c in FAR + NEAR if c == g] for g in GROUPS}
GREETED = FAR + NEAR + [(6, 0), (6, 2), (-6, 0), (-6, 2)]
OTHERS = sorted(
    [(x, y, z, c) for x in range(4) for y in range(4) for z in range(4) for c in range(2) if x + y + z + c],
    key=lambda o: -(sum(v > 0 for v in o[:3]) * 8 + sum(v == 2 for v in o[:3])),
)


def slot_of(a, c):
    return [x % NA for x, _ in PARTNERS[c]].index(a % NA)


def lane_iota(shape):
    return lax.broadcasted_iota(jnp.int32, shape, len(shape) - 1)


def row_iota(shape):
    return lax.broadcasted_iota(jnp.int32, shape, len(shape) - 2)


def left(v):
    return pltpu.roll(v, v.shape[-1] - 1, v.ndim - 1)


def right(v):
    return pltpu.roll(v, 1, v.ndim - 1)


def kernel(
    u_h, t_h, basis_h, coef_h, blade_h, off_h, extra_h, frac_h,
    fin, sen, tot,
    x0, u1, l2, l1, tg, bs, bh, prof, m1s, m1r0, m1rp, m1rm, m2s, m2r0, m2rp, m2rm, rrs, rrr, bb,
    blade_v, extra_v, frac_v, coef_s, off_s,
    loc, near_ss, near_rs, m_ss, m_rs, side_ss, side_rs, rr_ss, rr_rs, ready,
):
    az, ax = lax.axis_index("az"), lax.axis_index("ax")

    def partner(a, c):
        return ((az + a) & (NA - 1), (ax + c) & (NX - 1))

    def guard(c, act):
        if c == 0:
            act()
        else:
            pl.when((ax < NX - 1) if c > 0 else (ax > 0))(act)

    loads = [
        pltpu.make_async_copy(u_h, x0.at[2:18, 8:24, :], loc.at[0]),
        pltpu.make_async_copy(blade_h, blade_v, loc.at[1]),
        pltpu.make_async_copy(extra_h, extra_v, loc.at[2]),
        pltpu.make_async_copy(frac_h, frac_v, loc.at[3]),
        pltpu.make_async_copy(coef_h, coef_s, loc.at[4]),
        pltpu.make_async_copy(off_h, off_s, loc.at[5]),
        pltpu.make_async_copy(basis_h, bs, loc.at[6]),
        pltpu.make_async_copy(t_h, tg, loc.at[7]),
    ]
    for c in loads:
        c.start()

    barrier = pltpu.get_barrier_semaphore()

    for a, c in GREETED:
        pl.semaphore_signal(barrier, inc=1, device_id=partner(a, c), device_id_type=MESH)

    loads[0].wait()
    tile = (8, 128)
    lane8 = lane_iota(tile)

    def take(j, acc):
        for i, (lo, k) in enumerate(((128, 1), (256, 0))):
            for h in range(2):
                at = 16 + 16 * i + 32 * h + j
                acc = jnp.where(lane8 == at, pltpu.roll(x0[j + 2, 8 + 8 * h : 16 + 8 * h, lo : lo + 128], lax.rem(at + k, 128), 1), acc)
        return acc

    taken = lax.fori_loop(0, J, take, jnp.zeros(tile, f32), unroll=True)
    for c in loads[1:4]:
        c.wait()
    m1s[...] = jnp.zeros(tile, f32)
    m1s[0:2, 0:16] = extra_v[...].astype(f32)
    m1s[2:4, 0:16] = frac_v[...]
    m1s[4:6, 0:16] = blade_v[...]
    m1s[...] = m1s[...] + taken

    pl.semaphore_wait(barrier, len(GREETED))
    for a, c in GREETED:
        pl.semaphore_signal(ready, inc=1, device_id=partner(a, c), device_id_type=MESH)

    plane_src = {-1: pl.ds(0, 2), 0: pl.ds(0, 16), 1: pl.ds(14, 2)}
    row_src = {-1: pl.ds(0, 2), 0: pl.ds(0, 16), 1: pl.ds(14, 2)}
    plane_dst = {-1: pl.ds(18, 2), 0: pl.ds(2, 16), 1: pl.ds(0, 2)}
    row_dst = {-1: pl.ds(24, 2), 0: pl.ds(8, 16), 1: pl.ds(6, 2)}
    plane_own = {-1: pl.ds(2, 2), 0: pl.ds(2, 16), 1: pl.ds(16, 2)}
    row_own = {-1: pl.ds(8, 2), 0: pl.ds(8, 16), 1: pl.ds(22, 2)}

    def near_copy(src, dst, a, c, n):
        i = NEAR.index((a, c))
        return pltpu.make_async_remote_copy(
            src_ref=src, dst_ref=dst.at[plane_dst[a], row_dst[c], :],
            send_sem=near_ss.at[n, i], recv_sem=near_rs.at[n, i],
            device_id=partner(a, c), device_id_type=MESH,
        )

    def message(src, dst, a, c, n):
        return pltpu.make_async_remote_copy(
            src_ref=src, dst_ref=dst[-c].at[slot_of(-a, -c)],
            send_sem=m_ss.at[n, c + 1], recv_sem=m_rs.at[n, 1 - c],
            device_id=partner(a, c), device_id_type=MESH,
        )

    def near_group(c):
        return sorted((n for n in NEAR if n[1] == c), key=lambda n: -abs(n[0]))

    def send_all(near_of, src, dst, n, c):
        def act():
            for a, _ in near_group(c):
                near_of(a, c).start()
            for a, _ in PARTNERS[c]:
                message(src, dst, a, c, n).start()
        guard(c, act)

    m1g = {0: m1r0, 1: m1rp, -1: m1rm}
    m2g = {0: m2r0, 1: m2rp, -1: m2rm}

    def near1(a, c):
        return near_copy(u_h.at[plane_src[a], row_src[c], :], x0, a, c, 0)

    for c in GROUPS:
        send_all(near1, m1s, m1g, 0, c)

    for c in loads[4:]:
        c.wait()

    def mix(m, acc):
        return acc + coef_s[m] * bs[m]

    prof[8:24, :] = lax.fori_loop(0, M, mix, jnp.zeros((Z, R), f32), unroll=4)

    def side(c):
        i, src, dst = (0, 23, 7) if c > 0 else (1, 8, 24)
        return (
            pltpu.make_async_remote_copy(
                src_ref=prof.at[pl.ds(src, 1), :], dst_ref=prof.at[pl.ds(dst, 1), :],
                send_sem=side_ss.at[0, i], recv_sem=side_rs.at[0, i],
                device_id=partner(0, c), device_id_type=MESH),
            pltpu.make_async_remote_copy(
                src_ref=basis_h.at[:, pl.ds(src - 8, 1), :], dst_ref=bh.at[i],
                send_sem=side_ss.at[1, i], recv_sem=side_rs.at[1, i],
                device_id=partner(0, c), device_id_type=MESH),
        )

    for c in (1, -1):
        def act(c=c):
            for copy in side(c):
                copy.start()
        guard(c, act)

    def whole(ref, ss, rs):
        return pltpu.make_async_remote_copy(
            src_ref=ref, dst_ref=ref, send_sem=ss, recv_sem=rs, device_id=partner(0, 1), device_id_type=MESH)

    def arrivals(dst, n):
        for c in GROUPS:
            guard(c, lambda c=c: whole(dst[c], m_ss.at[n, c + 1], m_rs.at[n, c + 1]).wait_recv())

    def departures(dst, n):
        for c in GROUPS:
            guard(c, lambda c=c: whole(dst[c], m_ss.at[n, c + 1], m_rs.at[n, c + 1]).wait_send())

    def near_arrivals(near_of):
        for c in GROUPS:
            def act(c=c):
                for a, _ in near_group(c):
                    near_of(-a, -c).wait_recv()
            guard(c, act)

    def near_departures(near_of):
        for c in GROUPS:
            def act(c=c):
                for a, _ in near_group(c):
                    near_of(a, c).wait_send()
            guard(c, act)

    arrivals(m1g, 0)

    lane32 = lane_iota((32, 128))

    def gather_cols(own, ref, offsets, bases):
        def part(c, a, base, b):
            v = own[...] if (a, c) == (0, 0) else ref[c][slot_of(a, c)]
            s = (16 * b - base) % 128
            return pltpu.roll(v, s, 1) if s else v

        cols = []
        for lo, hi in bases:
            out = jnp.zeros((32, 128), f32)
            for b, a in enumerate(offsets):
                v = jnp.concatenate([part(-1, a, hi, b), part(0, a, lo, b), part(0, a, hi, b), part(1, a, lo, b)], axis=0)
                out = jnp.where((lane32 >= 16 * b) & (lane32 < 16 * b + 16), v, out)
            cols.append(out)
        return cols

    def gather_meta(offsets):
        out = jnp.zeros((8, 128), f32)
        for b, a in enumerate(offsets):
            v = m1s[...] if a == 0 else m1g[0][slot_of(a, 0)]
            out = jnp.where((lane8 >= 16 * b) & (lane8 < 16 * b + 16), pltpu.roll(v, 16 * b, 1) if b else v, out)
        return out

    bases1 = ((16, 48), (32, 64))
    bases2 = ((0, 64), (16, 80), (32, 96), (48, 112))
    near_off, far_off = (-1, 0, 1), (14, 15, 16, 17, 18)
    rot_n, sta_n = gather_cols(m1s, m1g, near_off, bases1)
    rot_f, sta_f = gather_cols(m1s, m1g, far_off, bases1)
    meta_n, meta_f = gather_meta(near_off), gather_meta(far_off)

    drift = off_s[0] - RI
    rows = row_iota((128, 128))
    lanes = lane_iota((128, 128))

    def weights(meta, base):
        w = meta[2:3, :]
        at = lanes + (drift + base) + meta[0:1, :].astype(jnp.int32)
        return jnp.where(rows == at, 1.0 - w, 0.0) + jnp.where(rows == at + 1, w, 0.0)

    w_n = weights(meta_n, 16)
    w_f = weights(meta_f, -16)

    def opposite(rn, sn, rf, sf):
        flux = jnp.dot(sf, w_n, precision=HI, preferred_element_type=f32) - rn
        fluxf = jnp.dot(sn, w_f, precision=HI, preferred_element_type=f32) - rf
        back = lax.dot_general(fluxf, w_f, (((1,), (1,)), ((), ())), precision=HI, preferred_element_type=f32)
        return flux, back

    def local_weights(meta):
        e, w = meta[1:2, :], meta[3:4, :]
        return (1.0 - e) * (1.0 - w), (1.0 - e) * w + e * (1.0 - w), e * w

    lw_n, lw_f = local_weights(meta_n), local_weights(meta_f)

    def spread(lw, v):
        return lw[0] * right(v) + lw[1] * v + lw[2] * left(v)

    def collect(lw, v):
        return left(lw[0] * v) + lw[1] * v + right(lw[2] * v)

    bl0, bl1 = meta_n[4:5, :], meta_n[5:6, :]
    eb = spread(lw_n, bl0)
    c0 = (1.0 - 2 * DIFF) * bl0 + DIFF * (left(bl0) + right(bl0)) - ADV * (bl0 - right(bl0)) + bl1
    r32 = row_iota((32, 128))
    for i, v in enumerate((bl0, bl1, c0, collect(lw_n, bl0), collect(lw_n, eb), eb)):
        picked = jnp.where(lane32 == r32 + 15, jnp.broadcast_to(v, (32, 128)), 0.0)
        bb[i] = jnp.broadcast_to(jnp.sum(picked, axis=1, keepdims=True), (32, 128))

    def coef(i, q):
        return bb[i, pl.ds(q, 1), :]

    def wide(v):
        return jnp.concatenate([v] * 4, axis=1)

    ri = lane_iota((1, R))
    edge = (ri == RI - 1) | (ri == RI)
    ctr = jnp.where(edge, 1.0 - 5 * DIFF - ADV, 1.0 - 6 * DIFF - ADV).astype(f32)
    up = jnp.where((ri == RI - 1) | (ri == R - 1), 0.0, DIFF).astype(f32)
    dn = jnp.where((ri == RI) | (ri == 0), 0.0, DIFF).astype(f32)

    def stencil(v, strong, weak, vz):
        return ctr * v + up * left(v) + dn * right(v) + DIFF * (vz + weak) + (DIFF + ADV) * strong

    def beside(v):
        return pltpu.roll(v, 1, 0) + pltpu.roll(v, v.shape[0] - 1, 0)

    def put(ref, idx, rows_, v, flux, back, k):
        ln = lane_iota(flux.shape)
        f = jnp.where(ln == 127, pltpu.roll(flux, 127 - k, 1), 0.0)
        b = jnp.where(ln == 0, pltpu.roll(back, lax.rem(128 - k, 128), 1), 0.0)
        ref[idx, rows_, 0:128] = v[:, 0:128]
        ref[idx, rows_, 128:256] = v[:, 128:256] + DIFF * f
        ref[idx, rows_, 256:384] = v[:, 256:384] - DIFF * b
        ref[idx, rows_, 384:512] = v[:, 384:512]

    def seal(ref, n):
        @pl.when(ax == 0)
        def _():
            ref[:, pl.ds(8 - n, n), :] = jnp.zeros((ref.shape[0], n, R), f32)

        @pl.when(ax == NX - 1)
        def _():
            ref[:, pl.ds(24, n), :] = jnp.zeros((ref.shape[0], n, R), f32)

    flux0, back0 = opposite(rot_n, sta_n, rot_f, sta_f)

    near_arrivals(near1)
    for c in (1, -1):
        def act(c=c):
            for copy in side(-c):
                copy.wait_recv()
        guard(c, act)
    seal(x0, 2)
    ally = slice(0, 32)

    def step_u1(q, _):
        v = x0[q + 1]
        new = stencil(v, x0[q], x0[q + 2], beside(v)) + wide(coef(0, q)) * prof[...]
        put(u1, q, ally, new, flux0, back0, q + 15)
        return 0

    lax.fori_loop(0, 18, step_u1, 0, unroll=3)
    seal(u1, 1)

    def take1(q, carry):
        rot, sta = carry
        a = pltpu.roll(u1[q, 8:24, 128:256], q + 16, 1)
        b = pltpu.roll(u1[q, 8:24, 256:384], q + 15, 1)
        return jnp.where(lane == q + 15, a, rot), jnp.where(lane == q + 15, b, sta)

    lane = lane_iota((Z, 128))
    zero = jnp.zeros((Z, 128), f32)
    rot1, sta1 = lax.fori_loop(0, 18, take1, (zero, zero), unroll=18)
    flux1 = spread(lw_n, sta1) - rot1
    back1 = collect(lw_n, flux1)

    centre = slice(8, 24)

    def step_u2(j, carry):
        ls, qs, ps, a1, a2, a3, cols = carry
        v = u1[j + 1]
        new = stencil(v[8:24], u1[j, 8:24, :], u1[j + 2, 8:24, :], beside(v)[8:24]) + wide(coef(1, j + 1)) * prof[8:24, :]
        put(fin, j, slice(0, 16), new, flux1, back1, j + 16)
        lam = fin[j] - tg[j]
        l2[j + 2, 8:24, :] = lam
        mid1, mid2 = lam[:, 128:256], lam[:, 256:384]
        for i, (t, l) in enumerate(((mid1, 126), (mid1, 127), (mid2, 0), (mid2, 1))):
            for h in range(2):
                k = j + bases2[i][h]
                cols = jnp.where(lane8 == k, pltpu.roll(t[8 * h : 8 * h + 8], lax.rem(k + 128 - l, 128), 1), cols)
        q = j + 1
        return (ls + lam * lam, qs + wide(coef(2, q)) * lam, ps + wide(coef(0, q)) * lam,
                a1 + coef(3, q) * mid2, a2 + coef(4, q) * mid2, a3 + coef(5, q) * mid1, cols)

    big = jnp.zeros((Z, R), f32)
    ls, qs, ps, a1, a2, a3, cols = lax.fori_loop(0, J, step_u2, (big, big, big, zero, zero, zero, jnp.zeros(tile, f32)), unroll=2)
    m2s[...] = cols

    def near2(a, c):
        return near_copy(l2.at[plane_own[a], row_own[c], :], l2, a, c, 1)

    for c in GROUPS:
        send_all(near2, m2s, m2g, 1, c)

    zr = row_iota((Z, R))
    pz = jnp.where(zr == 0, 0.0, pltpu.roll(ps, 1, 0)) + jnp.where(zr == Z - 1, 0.0, pltpu.roll(ps, Z - 1, 0))
    vv = qs + (ctr - (1.0 - 6 * DIFF - ADV) - 4 * DIFF) * ps + up * left(ps) + dn * right(ps) + DIFF * pz
    at255 = jnp.where(lane == 127, left(a1) - ps[:, 128:256], 0.0)
    at256 = jnp.where(lane == 0, a2 - right(a3), 0.0)
    vv = vv + DIFF * jnp.concatenate([zero, at255, -at256, zero], axis=1)
    top = jnp.where(ax == 0, 0.0, DIFF) * ps[0:1, :]
    bot = jnp.where(ax == NX - 1, 0.0, DIFF) * ps[15:16, :]

    def fold(v):
        v = v[:, 0:128] + v[:, 128:256] + v[:, 256:384] + v[:, 384:512]
        return jnp.sum(v, axis=0, keepdims=True)

    rowsum = []
    for m in range(M):
        rowsum.append(fold(bs[m] * vv) + fold(bh[0, m] * top + bh[1, m] * bot))
    rowsum.append(fold(ls))
    rowsum.append(jnp.zeros((7, 128), f32))
    stack = jnp.concatenate(rowsum, axis=0)
    stack = jnp.broadcast_to(jnp.sum(stack, axis=1, keepdims=True), (24, 128))
    rrs[...] = jnp.sum(jnp.where(row_iota((24, 128)) == lane_iota((24, 128)), stack, 0.0), axis=0, keepdims=True)

    pl.semaphore_wait(ready, len(GREETED))
    px, pz_, py, pc = (az >> 2) & 3, az & 3, (ax >> 1) * 2 + (az >> 4), ax & 1
    xs = [((px + d) & 3) << 2 for d in range(4)]
    zs = [(pz_ + d) & 3 for d in range(4)]
    ys = [(((py + d) & 1) << 4, (((py + d) >> 1) & 1) << 1) for d in range(4)]
    cs = [pc, 1 - pc]
    for x, y, z, c in OTHERS:
        pltpu.make_async_remote_copy(
            src_ref=rrs, dst_ref=rrr.at[OTHERS.index((-x % 4, -y % 4, -z % 4, c))], send_sem=rr_ss.at[0], recv_sem=rr_rs.at[0],
            device_id=(ys[y][0] + xs[x] + zs[z], ys[y][1] + cs[c]), device_id_type=MESH).start()

    arrivals(m2g, 1)
    zrow = row_iota((32, 128))
    inside = ((zrow >= 8) | (ax != 0)) & ((zrow < 24) | (ax != NX - 1))

    def adjoint_cols(cs, lw):
        c254, c255, c256, c257 = [jnp.where(inside, c, 0.0) for c in cs]
        flux = spread(lw, c256) - c255
        back = collect(lw, flux)

        def one(c, out, term):
            return (1.0 - 5 * DIFF - ADV) * c + DIFF * (out + right(c) + beside(c)) + (DIFF + ADV) * left(c) + DIFF * term

        return flux, back, one(c255, c254, flux), one(c256, c257, -back)

    flux_n, back_n, rot_n1, sta_n1 = adjoint_cols(gather_cols(m2s, m2g, near_off, bases2), lw_n)
    _, _, rot_f1, sta_f1 = adjoint_cols(gather_cols(m2s, m2g, far_off, bases2), lw_f)
    fluxa, backa = opposite(rot_n1[8:24], sta_n1[8:24], rot_f1[8:24], sta_f1[8:24])
    near_arrivals(near2)
    seal(l2, 2)

    def step_l1(q, _):
        v = l2[q + 1]
        new = stencil(v, l2[q + 2], l2[q], beside(v))
        put(l1, q, ally, new, flux_n, back_n, q + 15)
        return 0

    lax.fori_loop(0, 18, step_l1, 0, unroll=3)
    seal(l1, 1)

    def step_l0(j, _):
        v = l1[j + 1]
        new = stencil(v[8:24], l1[j + 2, 8:24, :], l1[j, 8:24, :], beside(v)[8:24])
        put(sen, j, slice(0, 16), new, fluxa, backa, j + 16)
        return 0

    lax.fori_loop(0, J, step_l0, 0, unroll=4)

    whole(rrr, rr_ss.at[0], rr_rs.at[0]).wait_recv()
    total = rrs[...] + jnp.sum(rrr[...], axis=0)
    tot[...] = jnp.broadcast_to(total, (8, 128))

    near_departures(near1)
    near_departures(near2)
    departures(m1g, 0)
    departures(m2g, 1)
    for c in (1, -1):
        def act(c=c):
            for copy in side(c):
                copy.wait_send()
        guard(c, act)
    whole(rrr, rr_ss.at[0], rr_rs.at[0]).wait_send()


def finish(fin, sen, tot, fin_o, sen_o, grad_o, loss_o, sems):
    a = pltpu.make_async_copy(fin, fin_o, sems.at[0])
    b = pltpu.make_async_copy(sen, sen_o, sems.at[1])
    a.start()
    b.start()
    row = tot[0:1, :]
    grad_o[...] = row[:, 0:M] * (1.0 / COLUMNS)
    loss_o[...] = row[:, M : M + 1] * (0.5 / (COLUMNS * R))
    a.wait()
    b.wait()


def on_device(initial, target, basis, coefficients, blade, offset, extra, frac):
    vm = pl.BlockSpec(memory_space=pltpu.VMEM)
    hbm = pl.BlockSpec(memory_space=pltpu.HBM)
    block = jax.ShapeDtypeStruct((J, Z, R), f32)
    dma = pltpu.SemaphoreType.DMA
    fin, sen, tot = pl.pallas_call(
        kernel,
        out_shape=(pltpu.VMEM((J, Z, R), f32), pltpu.VMEM((J, Z, R), f32), pltpu.VMEM((8, 128), f32)),
        in_specs=[hbm] * 8,
        out_specs=(vm, vm, vm),
        scratch_shapes=[
            pltpu.VMEM((20, 32, R), f32), pltpu.VMEM((18, 32, R), f32),
            pltpu.VMEM((20, 32, R), f32), pltpu.VMEM((18, 32, R), f32),
            pltpu.VMEM((J, Z, R), f32), pltpu.VMEM((M, Z, R), f32), pltpu.VMEM((2, M, 1, R), f32),
            pltpu.VMEM((32, R), f32),
            *[pltpu.VMEM((8, 128), f32), *[pltpu.VMEM((len(PARTNERS[c]), 8, 128), f32) for c in GROUPS]] * 2,
            pltpu.VMEM((1, 128), f32), pltpu.VMEM((NA * NX - 1, 1, 128), f32),
            pltpu.VMEM((6, 32, 128), f32),
            pltpu.VMEM((2, J), f32), pltpu.VMEM((2, J), jnp.int32), pltpu.VMEM((2, J), f32),
            pltpu.SMEM((M,), f32), pltpu.SMEM((2,), jnp.int32),
            dma((8,)), dma((2, 8)), dma((2, 8)), dma((2, 3)), dma((2, 3)), dma((2, 2)), dma((2, 2)), dma((1,)), dma((1,)),
            pltpu.SemaphoreType.REGULAR,
        ],
        compiler_params=pltpu.CompilerParams(collective_id=0, has_side_effects=True, vmem_limit_bytes=40 * 1024 * 1024),
    )(*(pltpu.with_memory_space_constraint(v, pltpu.HBM) for v in (initial, target, basis, coefficients, blade, offset, extra, frac)))
    fin, sen, grad, loss = pl.pallas_call(
        finish,
        out_shape=(block, block, jax.ShapeDtypeStruct((1, M), f32), jax.ShapeDtypeStruct((1, 1), f32)),
        in_specs=[vm] * 3,
        out_specs=(hbm, hbm, vm, vm),
        scratch_shapes=[dma((2,))],
    )(*(pltpu.with_memory_space_constraint(v, pltpu.VMEM) for v in (fin, sen, tot)))
    return fin, sen, grad.reshape(M), loss.reshape(())


def solution(mesh):
    block = P("az", "ax", None)
    row = P(None, "az")
    return jax.shard_map(
        on_device,
        mesh=mesh,
        in_specs=(block, block, P(None, "ax", None), P(), row, P(), row, row),
        out_specs=(block, block, P(), P()),
        check_vma=False,
    )
```

```python
import functools

import jax
import jax.numpy as jnp
from jax import lax
from jax.experimental import pallas as pl
from jax.experimental.pallas import tpu as pltpu
from jax.sharding import PartitionSpec as P

MESH = pl.DeviceIdType.MESH
f32 = jnp.float32
HI = lax.Precision.HIGHEST

NA, NX = 32, 4
J, Z, R, M = 16, 16, 512, 16
RI = 256
DIFF, ADV = 0.12, 0.2
COLUMNS = NA * J * NX * Z

NEAR = [(a, c) for a in (-1, 0, 1) for c in (-1, 0, 1) if (a, c) != (0, 0)]
FAR = [(a, c) for a in (14, 15, 16, 17, 18) for c in (-1, 0, 1)]
GROUPS = (0, 1, -1)
LATE, SAME, OPPOSITE = range(3)
PARTNERS = {
    (k, g): [(a, c) for a, c in NEAR + FAR if c == g and k == (OPPOSITE if a > 1 else LATE if a else SAME)]
    for k in range(3) for g in GROUPS if (k, g) != (SAME, 0)
}
GREETED = NEAR + FAR + [(6, 0), (6, 2), (-6, 0), (-6, 2)]
OTHERS = sorted(
    [(x, y, z, c) for x in range(4) for y in range(4) for z in range(4) for c in range(2) if x + y + z + c],
    key=lambda o: -(sum(v > 0 for v in o[:3]) * 8 + sum(v == 2 for v in o[:3])),
)


def slot_of(a, c):
    k = OPPOSITE if 1 < a % NA < NA - 1 else LATE if a else SAME
    return k, [x % NA for x, _ in PARTNERS[k, c]].index(a % NA)


def lane_iota(shape):
    return lax.broadcasted_iota(jnp.int32, shape, len(shape) - 1)


def row_iota(shape):
    return lax.broadcasted_iota(jnp.int32, shape, len(shape) - 2)


def left(v):
    return pltpu.roll(v, v.shape[-1] - 1, v.ndim - 1)


def right(v):
    return pltpu.roll(v, 1, v.ndim - 1)


def kernel(
    u_h, t_h, basis_h, coef_h, blade_h, off_h, extra_h, frac_h,
    fin, sen, tot,
    x0, u1, l2, l1, tg, bs, bh, prof, m1s, m1r, m2s, m2r, rrs, rrr, bb,
    blade_v, extra_v, frac_v, coef_s, off_s,
    loc, near_ss, near_rs, m_ss, m_rs, side_ss, side_rs, rr_ss, rr_rs, ready,
):
    az, ax = lax.axis_index("az"), lax.axis_index("ax")

    def partner(a, c):
        return ((az + a) & (NA - 1), (ax + c) & (NX - 1))

    def guard(c, act):
        if c == 0:
            act()
        else:
            pl.when((ax < NX - 1) if c > 0 else (ax > 0))(act)

    loads = [
        pltpu.make_async_copy(u_h, x0.at[2:18, 8:24, :], loc.at[0]),
        pltpu.make_async_copy(blade_h, blade_v, loc.at[1]),
        pltpu.make_async_copy(extra_h, extra_v, loc.at[2]),
        pltpu.make_async_copy(frac_h, frac_v, loc.at[3]),
        pltpu.make_async_copy(coef_h, coef_s, loc.at[4]),
        pltpu.make_async_copy(off_h, off_s, loc.at[5]),
        pltpu.make_async_copy(basis_h, bs, loc.at[6]),
        pltpu.make_async_copy(t_h, tg, loc.at[7]),
    ]
    loads[0].start()
    barrier = pltpu.get_barrier_semaphore()

    for a, c in GREETED:
        pl.semaphore_signal(barrier, inc=1, device_id=partner(a, c), device_id_type=MESH)
    for c in loads[1:]:
        c.start()

    loads[0].wait()
    tile = (8, 128)
    lane8 = lane_iota(tile)

    def take(j, acc):
        for i, (lo, k) in enumerate(((128, 1), (256, 0))):
            for h in range(2):
                at = 16 + 16 * i + 32 * h + j
                acc = jnp.where(lane8 == at, pltpu.roll(x0[j + 2, 8 + 8 * h : 16 + 8 * h, lo : lo + 128], lax.rem(at + k, 128), 1), acc)
        return acc

    taken = lax.fori_loop(0, J, take, jnp.zeros(tile, f32), unroll=True)
    for c in loads[1:4]:
        c.wait()
    m1s[...] = jnp.zeros(tile, f32)
    m1s[0:2, 0:16] = extra_v[...].astype(f32)
    m1s[2:4, 0:16] = frac_v[...]
    m1s[4:6, 0:16] = blade_v[...]
    m1s[...] = m1s[...] + taken

    pl.semaphore_wait(barrier, len(GREETED))
    plane_src = {-1: pl.ds(0, 2), 0: pl.ds(0, 16), 1: pl.ds(14, 2)}
    row_src = {-1: pl.ds(0, 2), 0: pl.ds(0, 16), 1: pl.ds(14, 2)}
    plane_dst = {-1: pl.ds(18, 2), 0: pl.ds(2, 16), 1: pl.ds(0, 2)}
    row_dst = {-1: pl.ds(24, 2), 0: pl.ds(8, 16), 1: pl.ds(6, 2)}
    plane_own = {-1: pl.ds(2, 2), 0: pl.ds(2, 16), 1: pl.ds(16, 2)}
    row_own = {-1: pl.ds(8, 2), 0: pl.ds(8, 16), 1: pl.ds(22, 2)}

    def near_copy(src, dst, a, c, n):
        i = NEAR.index((a, c))
        return pltpu.make_async_remote_copy(
            src_ref=src, dst_ref=dst.at[plane_dst[a], row_dst[c], :],
            send_sem=near_ss.at[n, i], recv_sem=near_rs.at[n, i],
            device_id=partner(a, c), device_id_type=MESH,
        )

    def message(src, dst, a, c, n):
        k, i = slot_of(-a, -c)
        return pltpu.make_async_remote_copy(
            src_ref=src, dst_ref=dst[k, -c].at[i],
            send_sem=m_ss.at[n, k, c + 1], recv_sem=m_rs.at[n, k, 1 - c],
            device_id=partner(a, c), device_id_type=MESH,
        )

    def near_group(k, c):
        return [n for n in NEAR if n[1] == c and (k == LATE) == (n[0] != 0)] if k != OPPOSITE else []

    def send_all(near_of, src, dst, n):
        for c in GROUPS:
            def act(c=c):
                for k in range(3):
                    for a, _ in near_group(k, c):
                        near_of(a, c).start()
                    for a, _ in PARTNERS.get((k, c), ()):
                        message(src, dst, a, c, n).start()
            guard(c, act)

    m1g = dict(zip(PARTNERS, m1r))
    m2g = dict(zip(PARTNERS, m2r))

    def near1(a, c):
        return near_copy(u_h.at[plane_src[a], row_src[c], :], x0, a, c, 0)

    send_all(near1, m1s, m1g, 0)

    for a, c in GREETED:
        pl.semaphore_signal(ready, inc=1, device_id=partner(a, c), device_id_type=MESH)

    for c in loads[4:]:
        c.wait()

    def mix(m, acc):
        return acc + coef_s[m] * bs[m]

    prof[8:24, :] = lax.fori_loop(0, M, mix, jnp.zeros((Z, R), f32), unroll=4)

    def side(c):
        i, src, dst = (0, 23, 7) if c > 0 else (1, 8, 24)
        return (
            pltpu.make_async_remote_copy(
                src_ref=prof.at[pl.ds(src, 1), :], dst_ref=prof.at[pl.ds(dst, 1), :],
                send_sem=side_ss.at[0, i], recv_sem=side_rs.at[0, i],
                device_id=partner(0, c), device_id_type=MESH),
            pltpu.make_async_remote_copy(
                src_ref=basis_h.at[:, pl.ds(src - 8, 1), :], dst_ref=bh.at[i],
                send_sem=side_ss.at[1, i], recv_sem=side_rs.at[1, i],
                device_id=partner(0, c), device_id_type=MESH),
        )

    for c in (1, -1):
        def act(c=c):
            for copy in side(c):
                copy.start()
        guard(c, act)

    def whole(ref, ss, rs):
        return pltpu.make_async_remote_copy(
            src_ref=ref, dst_ref=ref, send_sem=ss, recv_sem=rs, device_id=partner(0, 1), device_id_type=MESH)

    def arrivals(near_of, dst, n, k):
        for c in GROUPS:
            def act(c=c):
                if (k, c) in PARTNERS:
                    whole(dst[k, c], m_ss.at[n, k, c + 1], m_rs.at[n, k, c + 1]).wait_recv()
                for a, _ in near_group(k, c):
                    near_of(-a, -c).wait_recv()
            guard(c, act)

    def departures(near_of, dst, n):
        for c in GROUPS:
            def act(c=c):
                for k in range(3):
                    if (k, c) in PARTNERS:
                        whole(dst[k, c], m_ss.at[n, k, c + 1], m_rs.at[n, k, c + 1]).wait_send()
                    for a, _ in near_group(k, c):
                        near_of(a, c).wait_send()
            guard(c, act)

    arrivals(near1, m1g, 0, SAME)
    for c in (1, -1):
        def act(c=c):
            for copy in side(-c):
                copy.wait_recv()
        guard(c, act)
    lane32 = lane_iota((32, 128))

    near_off, far_off = (-1, 0, 1), (14, 15, 16, 17, 18)

    def gather_cols(own, ref, offsets, only, bases):
        def part(c, a, base, b):
            k, i = slot_of(a, c) if (a, c) != (0, 0) else (0, 0)
            v = own[...] if (a, c) == (0, 0) else ref[k, c][i]
            s = (16 * b - base) % 128
            return pltpu.roll(v, s, 1) if s else v

        cols = []
        for lo, hi in bases:
            out = jnp.zeros((32, 128), f32)
            for b, a in enumerate(offsets):
                if a not in only:
                    continue
                v = jnp.concatenate([part(-1, a, hi, b), part(0, a, lo, b), part(0, a, hi, b), part(1, a, lo, b)], axis=0)
                out = jnp.where((lane32 >= 16 * b) & (lane32 < 16 * b + 16), v, out)
            cols.append(out)
        return cols

    def gather_meta(offsets, only):
        out = jnp.zeros((8, 128), f32)
        for b, a in enumerate(offsets):
            if a not in only:
                continue
            k, i = slot_of(a, 0) if a else (0, 0)
            v = m1s[...] if a == 0 else m1g[k, 0][i]
            out = jnp.where((lane8 >= 16 * b) & (lane8 < 16 * b + 16), pltpu.roll(v, 16 * b, 1) if b else v, out)
        return out

    bases1 = ((16, 48), (32, 64))
    bases2 = ((0, 64), (16, 80), (32, 96), (48, 112))
    drift = off_s[0] - RI
    rows = row_iota((128, 128))
    lanes = lane_iota((128, 128))

    def weights(meta, base):
        w = meta[2:3, :]
        at = lanes + (drift + base) + meta[0:1, :].astype(jnp.int32)
        return jnp.where(rows == at, 1.0 - w, 0.0) + jnp.where(rows == at + 1, w, 0.0)

    def opposite(w_n, w_f, rn, sn, rf, sf):
        flux = jnp.dot(sf, w_n, precision=HI, preferred_element_type=f32) - rn
        fluxf = jnp.dot(sn, w_f, precision=HI, preferred_element_type=f32) - rf
        back = lax.dot_general(fluxf, w_f, (((1,), (1,)), ((), ())), precision=HI, preferred_element_type=f32)
        return flux, back

    def local_weights(meta):
        e, w = meta[1:2, :], meta[3:4, :]
        return (1.0 - e) * (1.0 - w), (1.0 - e) * w + e * (1.0 - w), e * w

    def spread(lw, v):
        return lw[0] * right(v) + lw[1] * v + lw[2] * left(v)

    def collect(lw, v):
        return left(lw[0] * v) + lw[1] * v + right(lw[2] * v)

    r32 = row_iota((32, 128))

    def c0_row(bl0, bl1):
        return (1.0 - 2 * DIFF) * bl0 + DIFF * (left(bl0) + right(bl0)) - ADV * (bl0 - right(bl0)) + bl1

    def plane_coefs(meta, lw):
        bl0, bl1 = meta[4:5, :], meta[5:6, :]
        eb = spread(lw, bl0)
        for i, v in enumerate((bl0, bl1, c0_row(bl0, bl1), collect(lw, bl0), collect(lw, eb), eb)):
            picked = jnp.where(lane32 == r32 + 15, jnp.broadcast_to(v, (32, 128)), 0.0)
            bb[i] = jnp.broadcast_to(jnp.sum(picked, axis=1, keepdims=True), (32, 128))

    def coef(i, q):
        return bb[i, pl.ds(q, 1), :]

    def wide(v):
        return jnp.concatenate([v] * 4, axis=1)

    ri = lane_iota((1, R))
    edge = (ri == RI - 1) | (ri == RI)
    ctr = jnp.where(edge, 1.0 - 5 * DIFF - ADV, 1.0 - 6 * DIFF - ADV).astype(f32)
    up = jnp.where((ri == RI - 1) | (ri == R - 1), 0.0, DIFF).astype(f32)
    dn = jnp.where((ri == RI) | (ri == 0), 0.0, DIFF).astype(f32)

    def stencil(v, strong, weak, vz):
        return ctr * v + up * left(v) + dn * right(v) + DIFF * (vz + weak) + (DIFF + ADV) * strong

    def beside(v):
        return pltpu.roll(v, 1, 0) + pltpu.roll(v, v.shape[0] - 1, 0)

    def columns_at(flux, back, k):
        ln = lane_iota(flux.shape)
        return (jnp.where(ln == 127, pltpu.roll(flux, (127 - k) & 127, 1), 0.0),
                jnp.where(ln == 0, pltpu.roll(back, (128 - k) & 127, 1), 0.0))

    def put(ref, idx, rows_, v, flux, back, k):
        f, b = columns_at(flux, back, k)
        ref[idx, rows_, 0:128] = v[:, 0:128]
        ref[idx, rows_, 128:256] = v[:, 128:256] + DIFF * f
        ref[idx, rows_, 256:384] = v[:, 256:384] - DIFF * b
        ref[idx, rows_, 384:512] = v[:, 384:512]

    def seal(ref, n, *parts):
        def clear(row):
            for lo, hi in parts:
                ref[lo:hi, pl.ds(row, n), :] = jnp.zeros((hi - lo, n, R), f32)

        pl.when(ax == 0)(lambda: clear(8 - n))
        pl.when(ax == NX - 1)(lambda: clear(24))

    ally, centre = slice(0, 32), slice(8, 24)
    lane = lane_iota((Z, 128))
    zero = jnp.zeros((Z, 128), f32)
    big = jnp.zeros((Z, R), f32)

    def step_u1(q):
        v = x0[q + 1]
        u1[q] = stencil(v, x0[q], x0[q + 2], beside(v)) + wide(coef(0, q)) * prof[...]

    def take1(q, rot, sta):
        a = pltpu.roll(u1[q, :, 128:256], (q + 16) & 127, 1)
        b = pltpu.roll(u1[q, :, 256:384], (q + 15) & 127, 1)
        return jnp.where(lane32 == q + 15, a, rot), jnp.where(lane32 == q + 15, b, sta)

    def step_u2(j, carry):
        ls, qs, ps, a1, a2, a3, cols = carry
        v = u1[j + 1]
        new = stencil(v[8:24], u1[j, 8:24, :], u1[j + 2, 8:24, :], beside(v)[8:24]) + wide(coef(1, j + 1)) * prof[8:24, :]
        fin[j] = new
        lam = new - tg[j]
        l2[j + 2, 8:24, :] = lam
        mid1, mid2 = lam[:, 128:256], lam[:, 256:384]
        for i, (t, l) in enumerate(((mid1, 126), (mid1, 127), (mid2, 0), (mid2, 1))):
            for h in range(2):
                k = j + bases2[i][h]
                cols = jnp.where(lane8 == k, pltpu.roll(t[8 * h : 8 * h + 8], (k + 128 - l) & 127, 1), cols)
        q = j + 1
        return (ls + lam * lam, qs + wide(coef(2, q)) * lam, ps + wide(coef(0, q)) * lam,
                a1 + coef(3, q) * mid2, a2 + coef(4, q) * mid2, a3 + coef(5, q) * mid1, cols)

    def local_flux(lw, rot, sta):
        flux = spread(lw, sta) - rot
        return flux, collect(lw, flux)

    meta_o = gather_meta(near_off, (0,))
    plane_coefs(meta_o, local_weights(meta_o))
    seal(x0, 2, (0, 20))

    def inner_u1(q, _):
        step_u1(q)
        return 0

    lax.fori_loop(2, 16, inner_u1, 0, unroll=2)
    seal(u1, 1, (2, 16))
    wide0 = jnp.zeros((32, 128), f32)
    rot1, sta1 = lax.fori_loop(2, 16, lambda q, c: take1(q, *c), (wide0, wide0), unroll=14)
    sums = lax.fori_loop(2, 14, step_u2, (big, big, big, zero, zero, zero, jnp.zeros(tile, f32)), unroll=2)

    arrivals(near1, m1g, 0, OPPOSITE)
    rot_f, sta_f = gather_cols(m1s, m1g, far_off, far_off, bases1)
    meta_f = gather_meta(far_off, far_off)
    w_f, lw_f = weights(meta_f, -16), local_weights(meta_f)
    rot_o, sta_o = gather_cols(m1s, m1g, near_off, (0,), bases1)

    arrivals(near1, m1g, 0, LATE)
    rot_e, sta_e = gather_cols(m1s, m1g, near_off, (-1, 1), bases1)
    rot_n, sta_n = rot_o + rot_e, sta_o + sta_e
    meta_n = meta_o + gather_meta(near_off, (-1, 1))
    lw_n, w_n = local_weights(meta_n), weights(meta_n, 16)
    flux0, back0 = opposite(w_n, w_f, rot_n, sta_n, rot_f, sta_f)
    plane_coefs(meta_n, lw_n)
    for q in (0, 1, 16, 17):
        step_u1(q)
    seal(u1, 1, (0, 2), (16, 18))
    for q in (0, 1, 16, 17):
        rot1, sta1 = take1(q, rot1, sta1)
    for j in (0, 1, 14, 15):
        sums = step_u2(j, sums)
    ls, qs, ps, a1, a2, a3, cols = sums

    zrow = row_iota((32, 128))
    inside = ((zrow >= 8) | (ax != 0)) & ((zrow < 24) | (ax != NX - 1))
    live = inside & (lane32 >= 15) & (lane32 <= 32)
    d255 = jnp.where(live, DIFF * flux0, 0.0)
    d256 = jnp.where(live, -DIFF * back0, 0.0)
    flux1, back1 = local_flux(lw_n, rot1 + d255, sta1 + d256)

    def pushed(d):
        return (1.0 - 5 * DIFF - ADV) * d + DIFF * (left(d) + beside(d)) + (DIFF + ADV) * right(d)

    own = (lane >= 16) & (lane < 32)
    adds = [jnp.where(own, v[8:24], 0.0)
            for v in (DIFF * d255, pushed(d255) + DIFF * flux1, pushed(d256) - DIFF * back1, DIFF * d256)]
    for j in (0, 1, 14, 15, *range(2, 14)):
        r = [pltpu.roll(v, (l - j - 16) & 127, 1) for v, l in zip(adds, (126, 127, 0, 1))]
        add1 = jnp.where(lane == 126, r[0], jnp.where(lane == 127, r[1], 0.0))
        add2 = jnp.where(lane == 0, r[2], jnp.where(lane == 1, r[3], 0.0))
        l2[j + 2, 8:24, 128:256] += add1
        l2[j + 2, 8:24, 256:384] += add2
        fin[j, :, 128:256] += add1
        fin[j, :, 256:384] += add2
    more = jnp.zeros(tile, f32)
    for i, v in enumerate(adds):
        for h in range(2):
            s = (bases2[i][h] - 16) & 127
            more = more + (pltpu.roll(v[8 * h : 8 * h + 8], s, 1) if s else v[8 * h : 8 * h + 8])
    m2s[...] = cols + more

    def near2(a, c):
        return near_copy(l2.at[plane_own[a], row_own[c], :], l2, a, c, 1)

    send_all(near2, m2s, m2g, 1)

    bl0, bl1 = meta_n[4:5, :], meta_n[5:6, :]
    eb = spread(lw_n, bl0)

    def along(row, v):
        return jnp.sum(row * v, axis=1, keepdims=True)

    crow = c0_row(bl0, bl1)
    for_q, for_p = [[along(r, v) for v in adds] for r in (crow, bl0)]

    def fix(v, parts):
        one, two = v[:, 128:256], v[:, 256:384]
        one = one + jnp.where(lane == 126, parts[0], 0.0) + jnp.where(lane == 127, parts[1], 0.0)
        two = two + jnp.where(lane == 0, parts[2], 0.0) + jnp.where(lane == 1, parts[3], 0.0)
        return jnp.concatenate([v[:, 0:128], one, two, v[:, 384:512]], axis=1)

    qs, ps = fix(qs, for_q), fix(ps, for_p)
    a1 = a1 + along(collect(lw_n, bl0), adds[2])
    a2 = a2 + along(collect(lw_n, eb), adds[2])
    a3 = a3 + along(eb, adds[1])
    zr = row_iota((Z, R))
    pz = jnp.where(zr == 0, 0.0, pltpu.roll(ps, 1, 0)) + jnp.where(zr == Z - 1, 0.0, pltpu.roll(ps, Z - 1, 0))
    vv = qs + (ctr - (1.0 - 6 * DIFF - ADV) - 4 * DIFF) * ps + up * left(ps) + dn * right(ps) + DIFF * pz
    at255 = jnp.where(lane == 127, left(a1) - ps[:, 128:256], 0.0)
    at256 = jnp.where(lane == 0, a2 - right(a3), 0.0)
    vv = vv + DIFF * jnp.concatenate([zero, at255, -at256, zero], axis=1)
    top = jnp.where(ax == 0, 0.0, DIFF) * ps[0:1, :]
    bot = jnp.where(ax == NX - 1, 0.0, DIFF) * ps[15:16, :]

    def fold(v):
        v = v[:, 0:128] + v[:, 128:256] + v[:, 256:384] + v[:, 384:512]
        return jnp.sum(v, axis=0, keepdims=True)

    rowsum = []
    for m in range(M):
        rowsum.append(fold(bs[m] * vv) + fold(bh[0, m] * top + bh[1, m] * bot))
    rowsum.append(fold(ls) + jnp.sum(more * (2.0 * cols + more), axis=0, keepdims=True))
    rowsum.append(jnp.zeros((7, 128), f32))
    stack = jnp.concatenate(rowsum, axis=0)
    stack = jnp.broadcast_to(jnp.sum(stack, axis=1, keepdims=True), (24, 128))
    rrs[...] = jnp.sum(jnp.where(row_iota((24, 128)) == lane_iota((24, 128)), stack, 0.0), axis=0, keepdims=True)

    pl.semaphore_wait(ready, len(GREETED))
    px, pz_, py, pc = (az >> 2) & 3, az & 3, (ax >> 1) * 2 + (az >> 4), ax & 1
    xs = [((px + d) & 3) << 2 for d in range(4)]
    zs = [(pz_ + d) & 3 for d in range(4)]
    ys = [(((py + d) & 1) << 4, (((py + d) >> 1) & 1) << 1) for d in range(4)]
    cs = [pc, 1 - pc]
    for x, y, z, c in OTHERS:
        pltpu.make_async_remote_copy(
            src_ref=rrs, dst_ref=rrr.at[OTHERS.index((-x % 4, -y % 4, -z % 4, c))], send_sem=rr_ss.at[0], recv_sem=rr_rs.at[0],
            device_id=(ys[y][0] + xs[x] + zs[z], ys[y][1] + cs[c]), device_id_type=MESH).start()

    def misfit_cols(offsets, only):
        return [jnp.where(inside, c, 0.0) for c in gather_cols(m2s, m2g, offsets, only, bases2)]

    def adjoint_cols(cs, lw):
        c254, c255, c256, c257 = cs
        flux, back = local_flux(lw, c255, c256)

        def one(c, out, term):
            return (1.0 - 5 * DIFF - ADV) * c + DIFF * (out + right(c) + beside(c)) + (DIFF + ADV) * left(c) + DIFF * term

        return flux, back, one(c255, c254, flux)[8:24], one(c256, c257, -back)[8:24]

    def step_l1(q, flux, back):
        v = l2[q + 1]
        new = stencil(v, l2[q + 2], l2[q], beside(v))
        put(l1, q, ally, new, flux, back, q + 15)

    def step_l0(j):
        v = l1[j + 1]
        sen[j] = stencil(v[8:24], l1[j + 2, 8:24, :], l1[j, 8:24, :], beside(v)[8:24])

    arrivals(near2, m2g, 1, SAME)
    seal(l2, 2, (0, 20))
    cols_o = misfit_cols(near_off, (0,))
    flux_n, back_n = local_flux(lw_n, cols_o[1], cols_o[2])

    def inner_l1(q, _):
        step_l1(q, flux_n, back_n)
        return 0

    def inner_l0(j, _):
        step_l0(j)
        return 0

    lax.fori_loop(3, 15, inner_l1, 0, unroll=2)
    seal(l1, 1, (3, 15))
    lax.fori_loop(3, 13, inner_l0, 0, unroll=2)
    arrivals(near2, m2g, 1, OPPOSITE)
    _, _, rot_f1, sta_f1 = adjoint_cols(misfit_cols(far_off, far_off), lw_f)

    arrivals(near2, m2g, 1, LATE)
    flux_n, back_n, rot_n1, sta_n1 = adjoint_cols([o + e for o, e in zip(cols_o, misfit_cols(near_off, (-1, 1)))], lw_n)
    fluxa, backa = opposite(w_n, w_f, rot_n1, sta_n1, rot_f1, sta_f1)
    for q in (0, 1, 2, 15, 16, 17):
        step_l1(q, flux_n, back_n)
    seal(l1, 1, (0, 3), (15, 18))
    for j in (0, 1, 2, 13, 14, 15):
        step_l0(j)
    for j in range(J):
        f, b = columns_at(fluxa, backa, j + 16)
        sen[j, :, 128:256] += DIFF * f
        sen[j, :, 256:384] -= DIFF * b

    whole(rrr, rr_ss.at[0], rr_rs.at[0]).wait_recv()
    total = rrs[...] + jnp.sum(rrr[...], axis=0)
    tot[...] = jnp.broadcast_to(total, (8, 128))

    departures(near1, m1g, 0)
    departures(near2, m2g, 1)
    for c in (1, -1):
        def act(c=c):
            for copy in side(c):
                copy.wait_send()
        guard(c, act)
    whole(rrr, rr_ss.at[0], rr_rs.at[0]).wait_send()


def finish(fin, sen, tot, fin_o, sen_o, grad_o, loss_o, sems):
    a = pltpu.make_async_copy(fin, fin_o, sems.at[0])
    b = pltpu.make_async_copy(sen, sen_o, sems.at[1])
    a.start()
    b.start()
    row = tot[0:1, :]
    grad_o[...] = row[:, 0:M] * (1.0 / COLUMNS)
    loss_o[...] = row[:, M : M + 1] * (0.5 / (COLUMNS * R))
    a.wait()
    b.wait()


def on_device(initial, target, basis, coefficients, blade, offset, extra, frac):
    vm = pl.BlockSpec(memory_space=pltpu.VMEM)
    hbm = pl.BlockSpec(memory_space=pltpu.HBM)
    block = jax.ShapeDtypeStruct((J, Z, R), f32)
    dma = pltpu.SemaphoreType.DMA
    fin, sen, tot = pl.pallas_call(
        kernel,
        out_shape=(pltpu.VMEM((J, Z, R), f32), pltpu.VMEM((J, Z, R), f32), pltpu.VMEM((8, 128), f32)),
        in_specs=[hbm] * 8,
        out_specs=(vm, vm, vm),
        scratch_shapes=[
            pltpu.VMEM((20, 32, R), f32), pltpu.VMEM((18, 32, R), f32),
            pltpu.VMEM((20, 32, R), f32), pltpu.VMEM((18, 32, R), f32),
            pltpu.VMEM((J, Z, R), f32), pltpu.VMEM((M, Z, R), f32), pltpu.VMEM((2, M, 1, R), f32),
            pltpu.VMEM((32, R), f32),
            *[pltpu.VMEM((8, 128), f32), [pltpu.VMEM((len(p), 8, 128), f32) for p in PARTNERS.values()]] * 2,
            pltpu.VMEM((1, 128), f32), pltpu.VMEM((NA * NX - 1, 1, 128), f32),
            pltpu.VMEM((6, 32, 128), f32),
            pltpu.VMEM((2, J), f32), pltpu.VMEM((2, J), jnp.int32), pltpu.VMEM((2, J), f32),
            pltpu.SMEM((M,), f32), pltpu.SMEM((2,), jnp.int32),
            dma((8,)), dma((2, 8)), dma((2, 8)), dma((2, 3, 3)), dma((2, 3, 3)), dma((2, 2)), dma((2, 2)), dma((1,)), dma((1,)),
            pltpu.SemaphoreType.REGULAR,
        ],
        compiler_params=pltpu.CompilerParams(collective_id=0, has_side_effects=True, vmem_limit_bytes=40 * 1024 * 1024),
    )(*(pltpu.with_memory_space_constraint(v, pltpu.HBM) for v in (initial, target, basis, coefficients, blade, offset, extra, frac)))
    fin, sen, grad, loss = pl.pallas_call(
        finish,
        out_shape=(block, block, jax.ShapeDtypeStruct((1, M), f32), jax.ShapeDtypeStruct((1, 1), f32)),
        in_specs=[vm] * 3,
        out_specs=(hbm, hbm, vm, vm),
        scratch_shapes=[dma((2,))],
    )(*(pltpu.with_memory_space_constraint(v, pltpu.VMEM) for v in (fin, sen, tot)))
    return fin, sen, grad.reshape(M), loss.reshape(())


def solution(mesh):
    block = P("az", "ax", None)
    row = P(None, "az")
    return jax.shard_map(
        on_device,
        mesh=mesh,
        in_specs=(block, block, P(None, "ax", None), P(), row, P(), row, row),
        out_specs=(block, block, P(), P()),
        check_vma=False,
    )
```

```python
import functools

import jax
import jax.numpy as jnp
from jax import lax
from jax.experimental import pallas as pl
from jax.experimental.pallas import tpu as pltpu
from jax.sharding import PartitionSpec as P

MESH = pl.DeviceIdType.MESH
f32 = jnp.float32
HI = lax.Precision.HIGHEST

NA, NX = 32, 4
J, Z, R, M = 16, 16, 512, 16
RI = 256
DIFF, ADV = 0.12, 0.2
COLUMNS = NA * J * NX * Z

NEAR = [(a, c) for a in (-1, 0, 1) for c in (-1, 0, 1) if (a, c) != (0, 0)]
FAR = [(a, c) for a in (14, 15, 16, 17, 18) for c in (-1, 0, 1)]
GROUPS = (0, 1, -1)
LATE, SAME, OPPOSITE = range(3)
PARTNERS = {
    (k, g): [(a, c) for a, c in NEAR + FAR if c == g and k == (OPPOSITE if a > 1 else LATE if a else SAME)]
    for k in range(3) for g in GROUPS if (k, g) != (SAME, 0)
}
GREETED = NEAR + FAR + [(6, 0), (6, 2), (-6, 0), (-6, 2)]
OTHERS = sorted(
    [(x, y, z, c) for x in range(4) for y in range(4) for z in range(4) for c in range(2) if x + y + z + c],
    key=lambda o: -(sum(v > 0 for v in o[:3]) * 8 + sum(v == 2 for v in o[:3])),
)


def slot_of(a, c):
    k = OPPOSITE if 1 < a % NA < NA - 1 else LATE if a else SAME
    return k, [x % NA for x, _ in PARTNERS[k, c]].index(a % NA)


def lane_iota(shape):
    return lax.broadcasted_iota(jnp.int32, shape, len(shape) - 1)


def row_iota(shape):
    return lax.broadcasted_iota(jnp.int32, shape, len(shape) - 2)


def left(v):
    return pltpu.roll(v, v.shape[-1] - 1, v.ndim - 1)


def right(v):
    return pltpu.roll(v, 1, v.ndim - 1)


def kernel(
    u_h, t_h, basis_h, coef_h, blade_h, off_h, extra_h, frac_h,
    fin, sen, tot,
    x0, u1, l2, l1, tg, bs, bh, prof, m1s, m1r, m2s, m2r, rrs, rrr, bb,
    blade_v, extra_v, frac_v, coef_s, off_s,
    loc, near_ss, near_rs, m_ss, m_rs, side_ss, side_rs, rr_ss, rr_rs, ready,
):
    az, ax = lax.axis_index("az"), lax.axis_index("ax")

    def partner(a, c):
        return ((az + a) & (NA - 1), (ax + c) & (NX - 1))

    def guard(c, act):
        if c == 0:
            act()
        else:
            pl.when((ax < NX - 1) if c > 0 else (ax > 0))(act)

    loads = [
        pltpu.make_async_copy(u_h, x0.at[2:18, 8:24, :], loc.at[0]),
        pltpu.make_async_copy(blade_h, blade_v, loc.at[1]),
        pltpu.make_async_copy(extra_h, extra_v, loc.at[2]),
        pltpu.make_async_copy(frac_h, frac_v, loc.at[3]),
        pltpu.make_async_copy(coef_h, coef_s, loc.at[4]),
        pltpu.make_async_copy(off_h, off_s, loc.at[5]),
        pltpu.make_async_copy(basis_h, bs, loc.at[6]),
        pltpu.make_async_copy(t_h, tg, loc.at[7]),
    ]
    loads[0].start()
    barrier = pltpu.get_barrier_semaphore()

    for a, c in GREETED:
        pl.semaphore_signal(barrier, inc=1, device_id=partner(a, c), device_id_type=MESH)
    for c in loads[1:]:
        c.start()

    loads[0].wait()
    tile = (8, 128)
    lane8 = lane_iota(tile)

    def take(j, acc):
        for i, (lo, k) in enumerate(((128, 1), (256, 0))):
            for h in range(2):
                at = 16 + 16 * i + 32 * h + j
                acc = jnp.where(lane8 == at, pltpu.roll(x0[j + 2, 8 + 8 * h : 16 + 8 * h, lo : lo + 128], lax.rem(at + k, 128), 1), acc)
        return acc

    taken = lax.fori_loop(0, J, take, jnp.zeros(tile, f32), unroll=True)
    for c in loads[1:4]:
        c.wait()
    m1s[...] = jnp.zeros(tile, f32)
    m1s[0:2, 0:16] = extra_v[...].astype(f32)
    m1s[2:4, 0:16] = frac_v[...]
    m1s[4:6, 0:16] = blade_v[...]
    m1s[...] = m1s[...] + taken

    pl.semaphore_wait(barrier, len(GREETED))
    plane_src = {-1: pl.ds(0, 2), 0: pl.ds(0, 16), 1: pl.ds(14, 2)}
    row_src = {-1: pl.ds(0, 2), 0: pl.ds(0, 16), 1: pl.ds(14, 2)}
    plane_dst = {-1: pl.ds(18, 2), 0: pl.ds(2, 16), 1: pl.ds(0, 2)}
    row_dst = {-1: pl.ds(24, 2), 0: pl.ds(8, 16), 1: pl.ds(6, 2)}
    plane_own = {-1: pl.ds(2, 2), 0: pl.ds(2, 16), 1: pl.ds(16, 2)}
    row_own = {-1: pl.ds(8, 2), 0: pl.ds(8, 16), 1: pl.ds(22, 2)}

    def near_copy(src, dst, a, c, n):
        i = NEAR.index((a, c))
        return pltpu.make_async_remote_copy(
            src_ref=src, dst_ref=dst.at[plane_dst[a], row_dst[c], :],
            send_sem=near_ss.at[n, i], recv_sem=near_rs.at[n, i],
            device_id=partner(a, c), device_id_type=MESH,
        )

    def message(src, dst, a, c, n):
        k, i = slot_of(-a, -c)
        return pltpu.make_async_remote_copy(
            src_ref=src, dst_ref=dst[k, -c].at[i],
            send_sem=m_ss.at[n, k, c + 1], recv_sem=m_rs.at[n, k, 1 - c],
            device_id=partner(a, c), device_id_type=MESH,
        )

    def near_group(k, c):
        return [n for n in NEAR if n[1] == c and (k == LATE) == (n[0] != 0)] if k != OPPOSITE else []

    def send_all(near_of, src, dst, n):
        for c in (1, -1, 0):
            def act(c=c):
                for k in (SAME, LATE, OPPOSITE):
                    for a, _ in near_group(k, c):
                        near_of(a, c).start()
                    for a, _ in PARTNERS.get((k, c), ()):
                        message(src, dst, a, c, n).start()
            guard(c, act)

    m1g = dict(zip(PARTNERS, m1r))
    m2g = dict(zip(PARTNERS, m2r))

    def near1(a, c):
        return near_copy(u_h.at[plane_src[a], row_src[c], :], x0, a, c, 0)

    send_all(near1, m1s, m1g, 0)

    for a, c in GREETED:
        pl.semaphore_signal(ready, inc=1, device_id=partner(a, c), device_id_type=MESH)

    for c in loads[4:]:
        c.wait()

    def mix(m, acc):
        return acc + coef_s[m] * bs[m]

    prof[8:24, :] = lax.fori_loop(0, M, mix, jnp.zeros((Z, R), f32), unroll=4)

    def side(c):
        i, src, dst = (0, 23, 7) if c > 0 else (1, 8, 24)
        return (
            pltpu.make_async_remote_copy(
                src_ref=prof.at[pl.ds(src, 1), :], dst_ref=prof.at[pl.ds(dst, 1), :],
                send_sem=side_ss.at[0, i], recv_sem=side_rs.at[0, i],
                device_id=partner(0, c), device_id_type=MESH),
            pltpu.make_async_remote_copy(
                src_ref=basis_h.at[:, pl.ds(src - 8, 1), :], dst_ref=bh.at[i],
                send_sem=side_ss.at[1, i], recv_sem=side_rs.at[1, i],
                device_id=partner(0, c), device_id_type=MESH),
        )

    for c in (1, -1):
        def act(c=c):
            for copy in side(c):
                copy.start()
        guard(c, act)

    def whole(ref, ss, rs):
        return pltpu.make_async_remote_copy(
            src_ref=ref, dst_ref=ref, send_sem=ss, recv_sem=rs, device_id=partner(0, 1), device_id_type=MESH)

    def arrivals(near_of, dst, n, k):
        for c in GROUPS:
            def act(c=c):
                if (k, c) in PARTNERS:
                    whole(dst[k, c], m_ss.at[n, k, c + 1], m_rs.at[n, k, c + 1]).wait_recv()
                for a, _ in near_group(k, c):
                    near_of(-a, -c).wait_recv()
            guard(c, act)

    def departures(near_of, dst, n):
        for c in GROUPS:
            def act(c=c):
                for k in range(3):
                    if (k, c) in PARTNERS:
                        whole(dst[k, c], m_ss.at[n, k, c + 1], m_rs.at[n, k, c + 1]).wait_send()
                    for a, _ in near_group(k, c):
                        near_of(a, c).wait_send()
            guard(c, act)

    arrivals(near1, m1g, 0, SAME)
    for c in (1, -1):
        def act(c=c):
            for copy in side(-c):
                copy.wait_recv()
        guard(c, act)
    lane32 = lane_iota((32, 128))

    near_off, far_off = (-1, 0, 1), (14, 15, 16, 17, 18)

    def gather_cols(own, ref, offsets, only, bases):
        def part(c, a, base, b):
            k, i = slot_of(a, c) if (a, c) != (0, 0) else (0, 0)
            v = own[...] if (a, c) == (0, 0) else ref[k, c][i]
            s = (16 * b - base) % 128
            return pltpu.roll(v, s, 1) if s else v

        cols = []
        for lo, hi in bases:
            out = jnp.zeros((32, 128), f32)
            for b, a in enumerate(offsets):
                if a not in only:
                    continue
                v = jnp.concatenate([part(-1, a, hi, b), part(0, a, lo, b), part(0, a, hi, b), part(1, a, lo, b)], axis=0)
                out = jnp.where((lane32 >= 16 * b) & (lane32 < 16 * b + 16), v, out)
            cols.append(out)
        return cols

    def gather_meta(offsets, only):
        out = jnp.zeros((8, 128), f32)
        for b, a in enumerate(offsets):
            if a not in only:
                continue
            k, i = slot_of(a, 0) if a else (0, 0)
            v = m1s[...] if a == 0 else m1g[k, 0][i]
            out = jnp.where((lane8 >= 16 * b) & (lane8 < 16 * b + 16), pltpu.roll(v, 16 * b, 1) if b else v, out)
        return out

    bases1 = ((16, 48), (32, 64))
    bases2 = ((0, 64), (16, 80), (32, 96), (48, 112))
    drift = off_s[0] - RI
    rows = row_iota((128, 128))
    lanes = lane_iota((128, 128))

    def weights(meta, base):
        w = meta[2:3, :]
        at = lanes + (drift + base) + meta[0:1, :].astype(jnp.int32)
        return jnp.where(rows == at, 1.0 - w, 0.0) + jnp.where(rows == at + 1, w, 0.0)

    def opposite(w_n, w_f, rn, sn, rf, sf):
        flux = jnp.dot(sf, w_n, precision=HI, preferred_element_type=f32) - rn
        fluxf = jnp.dot(sn, w_f, precision=HI, preferred_element_type=f32) - rf
        back = lax.dot_general(fluxf, w_f, (((1,), (1,)), ((), ())), precision=HI, preferred_element_type=f32)
        return flux, back

    def local_weights(meta):
        e, w = meta[1:2, :], meta[3:4, :]
        return (1.0 - e) * (1.0 - w), (1.0 - e) * w + e * (1.0 - w), e * w

    def spread(lw, v):
        return lw[0] * right(v) + lw[1] * v + lw[2] * left(v)

    def collect(lw, v):
        return left(lw[0] * v) + lw[1] * v + right(lw[2] * v)

    r32 = row_iota((32, 128))

    def c0_row(bl0, bl1):
        return (1.0 - 2 * DIFF) * bl0 + DIFF * (left(bl0) + right(bl0)) - ADV * (bl0 - right(bl0)) + bl1

    def plane_coefs(meta, lw):
        bl0, bl1 = meta[4:5, :], meta[5:6, :]
        eb = spread(lw, bl0)
        for i, v in enumerate((bl0, bl1, c0_row(bl0, bl1), collect(lw, bl0), collect(lw, eb), eb)):
            picked = jnp.where(lane32 == r32 + 15, jnp.broadcast_to(v, (32, 128)), 0.0)
            bb[i] = jnp.broadcast_to(jnp.sum(picked, axis=1, keepdims=True), (32, 128))

    def coef(i, q):
        return bb[i, pl.ds(q, 1), :]

    def wide(v):
        return jnp.concatenate([v] * 4, axis=1)

    ri = lane_iota((1, R))
    edge = (ri == RI - 1) | (ri == RI)
    ctr = jnp.where(edge, 1.0 - 5 * DIFF - ADV, 1.0 - 6 * DIFF - ADV).astype(f32)
    up = jnp.where((ri == RI - 1) | (ri == R - 1), 0.0, DIFF).astype(f32)
    dn = jnp.where((ri == RI) | (ri == 0), 0.0, DIFF).astype(f32)

    def stencil(v, strong, weak, vz):
        return ctr * v + up * left(v) + dn * right(v) + DIFF * (vz + weak) + (DIFF + ADV) * strong

    def beside(v):
        return pltpu.roll(v, 1, 0) + pltpu.roll(v, v.shape[0] - 1, 0)

    def columns_at(flux, back, k):
        ln = lane_iota(flux.shape)
        return (jnp.where(ln == 127, pltpu.roll(flux, (127 - k) & 127, 1), 0.0),
                jnp.where(ln == 0, pltpu.roll(back, (128 - k) & 127, 1), 0.0))

    def put(ref, idx, rows_, v, flux, back, k):
        f, b = columns_at(flux, back, k)
        ref[idx, rows_, 0:128] = v[:, 0:128]
        ref[idx, rows_, 128:256] = v[:, 128:256] + DIFF * f
        ref[idx, rows_, 256:384] = v[:, 256:384] - DIFF * b
        ref[idx, rows_, 384:512] = v[:, 384:512]

    def seal(ref, n, *parts):
        def clear(row):
            for lo, hi in parts:
                ref[lo:hi, pl.ds(row, n), :] = jnp.zeros((hi - lo, n, R), f32)

        pl.when(ax == 0)(lambda: clear(8 - n))
        pl.when(ax == NX - 1)(lambda: clear(24))

    ally, centre = slice(0, 32), slice(8, 24)
    lane = lane_iota((Z, 128))
    zero = jnp.zeros((Z, 128), f32)
    big = jnp.zeros((Z, R), f32)

    def step_u1(q):
        v = x0[q + 1]
        u1[q] = stencil(v, x0[q], x0[q + 2], beside(v)) + wide(coef(0, q)) * prof[...]

    def take1(q, rot, sta):
        a = pltpu.roll(u1[q, :, 128:256], (q + 16) & 127, 1)
        b = pltpu.roll(u1[q, :, 256:384], (q + 15) & 127, 1)
        return jnp.where(lane32 == q + 15, a, rot), jnp.where(lane32 == q + 15, b, sta)

    def step_u2(j, carry):
        ls, qs, ps, a1, a2, a3, cols = carry
        v = u1[j + 1]
        new = stencil(v[8:24], u1[j, 8:24, :], u1[j + 2, 8:24, :], beside(v)[8:24]) + wide(coef(1, j + 1)) * prof[8:24, :]
        fin[j] = new
        lam = new - tg[j]
        l2[j + 2, 8:24, :] = lam
        mid1, mid2 = lam[:, 128:256], lam[:, 256:384]
        for i, (t, l) in enumerate(((mid1, 126), (mid1, 127), (mid2, 0), (mid2, 1))):
            for h in range(2):
                k = j + bases2[i][h]
                cols = jnp.where(lane8 == k, pltpu.roll(t[8 * h : 8 * h + 8], (k + 128 - l) & 127, 1), cols)
        q = j + 1
        return (ls + lam * lam, qs + wide(coef(2, q)) * lam, ps + wide(coef(0, q)) * lam,
                a1 + coef(3, q) * mid2, a2 + coef(4, q) * mid2, a3 + coef(5, q) * mid1, cols)

    def local_flux(lw, rot, sta):
        flux = spread(lw, sta) - rot
        return flux, collect(lw, flux)

    meta_o = gather_meta(near_off, (0,))
    plane_coefs(meta_o, local_weights(meta_o))
    seal(x0, 2, (0, 20))

    def inner_u1(q, _):
        step_u1(q)
        return 0

    lax.fori_loop(2, 16, inner_u1, 0, unroll=7)
    seal(u1, 1, (2, 16))
    wide0 = jnp.zeros((32, 128), f32)
    rot1, sta1 = lax.fori_loop(2, 16, lambda q, c: take1(q, *c), (wide0, wide0), unroll=14)
    sums = lax.fori_loop(2, 14, step_u2, (big, big, big, zero, zero, zero, jnp.zeros(tile, f32)), unroll=4)

    arrivals(near1, m1g, 0, OPPOSITE)
    rot_f, sta_f = gather_cols(m1s, m1g, far_off, far_off, bases1)
    meta_f = gather_meta(far_off, far_off)
    w_f, lw_f = weights(meta_f, -16), local_weights(meta_f)
    rot_o, sta_o = gather_cols(m1s, m1g, near_off, (0,), bases1)

    arrivals(near1, m1g, 0, LATE)
    rot_e, sta_e = gather_cols(m1s, m1g, near_off, (-1, 1), bases1)
    rot_n, sta_n = rot_o + rot_e, sta_o + sta_e
    meta_n = meta_o + gather_meta(near_off, (-1, 1))
    lw_n, w_n = local_weights(meta_n), weights(meta_n, 16)
    flux0, back0 = opposite(w_n, w_f, rot_n, sta_n, rot_f, sta_f)
    plane_coefs(meta_n, lw_n)
    for q in (0, 1, 16, 17):
        step_u1(q)
    seal(u1, 1, (0, 2), (16, 18))
    for q in (0, 1, 16, 17):
        rot1, sta1 = take1(q, rot1, sta1)
    for j in (0, 1, 14, 15):
        sums = step_u2(j, sums)
    ls, qs, ps, a1, a2, a3, cols = sums

    zrow = row_iota((32, 128))
    inside = ((zrow >= 8) | (ax != 0)) & ((zrow < 24) | (ax != NX - 1))
    live = inside & (lane32 >= 15) & (lane32 <= 32)
    d255 = jnp.where(live, DIFF * flux0, 0.0)
    d256 = jnp.where(live, -DIFF * back0, 0.0)
    flux1, back1 = local_flux(lw_n, rot1 + d255, sta1 + d256)

    def pushed(d):
        return (1.0 - 5 * DIFF - ADV) * d + DIFF * (left(d) + beside(d)) + (DIFF + ADV) * right(d)

    own = (lane >= 16) & (lane < 32)
    adds = [jnp.where(own, v[8:24], 0.0)
            for v in (DIFF * d255, pushed(d255) + DIFF * flux1, pushed(d256) - DIFF * back1, DIFF * d256)]
    for j in (0, 1, 14, 15, *range(2, 14)):
        r = [pltpu.roll(v, (l - j - 16) & 127, 1) for v, l in zip(adds, (126, 127, 0, 1))]
        add1 = jnp.where(lane == 126, r[0], jnp.where(lane == 127, r[1], 0.0))
        add2 = jnp.where(lane == 0, r[2], jnp.where(lane == 1, r[3], 0.0))
        l2[j + 2, 8:24, 128:256] += add1
        l2[j + 2, 8:24, 256:384] += add2
        fin[j, :, 128:256] += add1
        fin[j, :, 256:384] += add2
    more = jnp.zeros(tile, f32)
    for i, v in enumerate(adds):
        for h in range(2):
            s = (bases2[i][h] - 16) & 127
            more = more + (pltpu.roll(v[8 * h : 8 * h + 8], s, 1) if s else v[8 * h : 8 * h + 8])
    m2s[...] = cols + more

    def near2(a, c):
        return near_copy(l2.at[plane_own[a], row_own[c], :], l2, a, c, 1)

    send_all(near2, m2s, m2g, 1)

    bl0, bl1 = meta_n[4:5, :], meta_n[5:6, :]
    eb = spread(lw_n, bl0)

    def along(row, v):
        return jnp.sum(row * v, axis=1, keepdims=True)

    crow = c0_row(bl0, bl1)
    for_q, for_p = [[along(r, v) for v in adds] for r in (crow, bl0)]

    def fix(v, parts):
        one, two = v[:, 128:256], v[:, 256:384]
        one = one + jnp.where(lane == 126, parts[0], 0.0) + jnp.where(lane == 127, parts[1], 0.0)
        two = two + jnp.where(lane == 0, parts[2], 0.0) + jnp.where(lane == 1, parts[3], 0.0)
        return jnp.concatenate([v[:, 0:128], one, two, v[:, 384:512]], axis=1)

    qs, ps = fix(qs, for_q), fix(ps, for_p)
    a1 = a1 + along(collect(lw_n, bl0), adds[2])
    a2 = a2 + along(collect(lw_n, eb), adds[2])
    a3 = a3 + along(eb, adds[1])
    zr = row_iota((Z, R))
    pz = jnp.where(zr == 0, 0.0, pltpu.roll(ps, 1, 0)) + jnp.where(zr == Z - 1, 0.0, pltpu.roll(ps, Z - 1, 0))
    vv = qs + (ctr - (1.0 - 6 * DIFF - ADV) - 4 * DIFF) * ps + up * left(ps) + dn * right(ps) + DIFF * pz
    at255 = jnp.where(lane == 127, left(a1) - ps[:, 128:256], 0.0)
    at256 = jnp.where(lane == 0, a2 - right(a3), 0.0)
    vv = vv + DIFF * jnp.concatenate([zero, at255, -at256, zero], axis=1)
    top = jnp.where(ax == 0, 0.0, DIFF) * ps[0:1, :]
    bot = jnp.where(ax == NX - 1, 0.0, DIFF) * ps[15:16, :]

    def fold(v):
        v = v[:, 0:128] + v[:, 128:256] + v[:, 256:384] + v[:, 384:512]
        return jnp.sum(v, axis=0, keepdims=True)

    rowsum = []
    for m in range(M):
        rowsum.append(fold(bs[m] * vv) + fold(bh[0, m] * top + bh[1, m] * bot))
    rowsum.append(fold(ls) + jnp.sum(more * (2.0 * cols + more), axis=0, keepdims=True))
    rowsum.append(jnp.zeros((7, 128), f32))
    stack = jnp.concatenate(rowsum, axis=0)
    stack = jnp.broadcast_to(jnp.sum(stack, axis=1, keepdims=True), (24, 128))
    rrs[...] = jnp.sum(jnp.where(row_iota((24, 128)) == lane_iota((24, 128)), stack, 0.0), axis=0, keepdims=True)

    pl.semaphore_wait(ready, len(GREETED))
    px, pz_, py, pc = (az >> 2) & 3, az & 3, (ax >> 1) * 2 + (az >> 4), ax & 1
    xs = [((px + d) & 3) << 2 for d in range(4)]
    zs = [(pz_ + d) & 3 for d in range(4)]
    ys = [(((py + d) & 1) << 4, (((py + d) >> 1) & 1) << 1) for d in range(4)]
    cs = [pc, 1 - pc]
    for x, y, z, c in OTHERS:
        pltpu.make_async_remote_copy(
            src_ref=rrs, dst_ref=rrr.at[OTHERS.index((-x % 4, -y % 4, -z % 4, c))], send_sem=rr_ss.at[0], recv_sem=rr_rs.at[0],
            device_id=(ys[y][0] + xs[x] + zs[z], ys[y][1] + cs[c]), device_id_type=MESH).start()

    def misfit_cols(offsets, only):
        return [jnp.where(inside, c, 0.0) for c in gather_cols(m2s, m2g, offsets, only, bases2)]

    def adjoint_cols(cs, lw):
        c254, c255, c256, c257 = cs
        flux, back = local_flux(lw, c255, c256)

        def one(c, out, term):
            return (1.0 - 5 * DIFF - ADV) * c + DIFF * (out + right(c) + beside(c)) + (DIFF + ADV) * left(c) + DIFF * term

        return flux, back, one(c255, c254, flux)[8:24], one(c256, c257, -back)[8:24]

    def step_l1(q, flux, back):
        v = l2[q + 1]
        new = stencil(v, l2[q + 2], l2[q], beside(v))
        put(l1, q, ally, new, flux, back, q + 15)

    def step_l0(j):
        v = l1[j + 1]
        sen[j] = stencil(v[8:24], l1[j + 2, 8:24, :], l1[j, 8:24, :], beside(v)[8:24])

    arrivals(near2, m2g, 1, SAME)
    seal(l2, 2, (0, 20))
    cols_o = misfit_cols(near_off, (0,))
    flux_n, back_n = local_flux(lw_n, cols_o[1], cols_o[2])

    def inner_l1(q, _):
        step_l1(q, flux_n, back_n)
        return 0

    def inner_l0(j, _):
        step_l0(j)
        return 0

    lax.fori_loop(3, 15, inner_l1, 0, unroll=4)
    seal(l1, 1, (3, 15))
    lax.fori_loop(3, 13, inner_l0, 0, unroll=5)
    arrivals(near2, m2g, 1, OPPOSITE)
    _, _, rot_f1, sta_f1 = adjoint_cols(misfit_cols(far_off, far_off), lw_f)

    arrivals(near2, m2g, 1, LATE)
    flux_n, back_n, rot_n1, sta_n1 = adjoint_cols([o + e for o, e in zip(cols_o, misfit_cols(near_off, (-1, 1)))], lw_n)
    fluxa, backa = opposite(w_n, w_f, rot_n1, sta_n1, rot_f1, sta_f1)
    for q in (0, 1, 2, 15, 16, 17):
        step_l1(q, flux_n, back_n)
    seal(l1, 1, (0, 3), (15, 18))
    for j in (0, 1, 2, 13, 14, 15):
        step_l0(j)
    for j in range(J):
        f, b = columns_at(fluxa, backa, j + 16)
        sen[j, :, 128:256] += DIFF * f
        sen[j, :, 256:384] -= DIFF * b

    whole(rrr, rr_ss.at[0], rr_rs.at[0]).wait_recv()
    total = rrs[...] + jnp.sum(rrr[...], axis=0)
    tot[...] = jnp.broadcast_to(total, (8, 128))

    departures(near1, m1g, 0)
    departures(near2, m2g, 1)
    for c in (1, -1):
        def act(c=c):
            for copy in side(c):
                copy.wait_send()
        guard(c, act)
    whole(rrr, rr_ss.at[0], rr_rs.at[0]).wait_send()


def finish(fin, sen, tot, fin_o, sen_o, grad_o, loss_o, sems):
    a = pltpu.make_async_copy(fin, fin_o, sems.at[0])
    b = pltpu.make_async_copy(sen, sen_o, sems.at[1])
    a.start()
    b.start()
    row = tot[0:1, :]
    grad_o[...] = row[:, 0:M] * (1.0 / COLUMNS)
    loss_o[...] = row[:, M : M + 1] * (0.5 / (COLUMNS * R))
    a.wait()
    b.wait()


def on_device(initial, target, basis, coefficients, blade, offset, extra, frac):
    vm = pl.BlockSpec(memory_space=pltpu.VMEM)
    hbm = pl.BlockSpec(memory_space=pltpu.HBM)
    block = jax.ShapeDtypeStruct((J, Z, R), f32)
    dma = pltpu.SemaphoreType.DMA
    fin, sen, tot = pl.pallas_call(
        kernel,
        out_shape=(pltpu.VMEM((J, Z, R), f32), pltpu.VMEM((J, Z, R), f32), pltpu.VMEM((8, 128), f32)),
        in_specs=[hbm] * 8,
        out_specs=(vm, vm, vm),
        scratch_shapes=[
            pltpu.VMEM((20, 32, R), f32), pltpu.VMEM((18, 32, R), f32),
            pltpu.VMEM((20, 32, R), f32), pltpu.VMEM((18, 32, R), f32),
            pltpu.VMEM((J, Z, R), f32), pltpu.VMEM((M, Z, R), f32), pltpu.VMEM((2, M, 1, R), f32),
            pltpu.VMEM((32, R), f32),
            *[pltpu.VMEM((8, 128), f32), [pltpu.VMEM((len(p), 8, 128), f32) for p in PARTNERS.values()]] * 2,
            pltpu.VMEM((1, 128), f32), pltpu.VMEM((NA * NX - 1, 1, 128), f32),
            pltpu.VMEM((6, 32, 128), f32),
            pltpu.VMEM((2, J), f32), pltpu.VMEM((2, J), jnp.int32), pltpu.VMEM((2, J), f32),
            pltpu.SMEM((M,), f32), pltpu.SMEM((2,), jnp.int32),
            dma((8,)), dma((2, 8)), dma((2, 8)), dma((2, 3, 3)), dma((2, 3, 3)), dma((2, 2)), dma((2, 2)), dma((1,)), dma((1,)),
            pltpu.SemaphoreType.REGULAR,
        ],
        compiler_params=pltpu.CompilerParams(collective_id=0, has_side_effects=True, vmem_limit_bytes=40 * 1024 * 1024),
    )(*(pltpu.with_memory_space_constraint(v, pltpu.HBM) for v in (initial, target, basis, coefficients, blade, offset, extra, frac)))
    fin, sen, grad, loss = pl.pallas_call(
        finish,
        out_shape=(block, block, jax.ShapeDtypeStruct((1, M), f32), jax.ShapeDtypeStruct((1, 1), f32)),
        in_specs=[vm] * 3,
        out_specs=(hbm, hbm, vm, vm),
        scratch_shapes=[dma((2,))],
    )(*(pltpu.with_memory_space_constraint(v, pltpu.VMEM) for v in (fin, sen, tot)))
    return fin, sen, grad.reshape(M), loss.reshape(())


def solution(mesh):
    block = P("az", "ax", None)
    row = P(None, "az")
    return jax.shard_map(
        on_device,
        mesh=mesh,
        in_specs=(block, block, P(None, "ax", None), P(), row, P(), row, row),
        out_specs=(block, block, P(), P()),
        check_vma=False,
    )
```

```python
import functools

import jax
import jax.numpy as jnp
from jax import lax
from jax.experimental import pallas as pl
from jax.experimental.pallas import tpu as pltpu
from jax.sharding import PartitionSpec as P

MESH = pl.DeviceIdType.MESH
f32 = jnp.float32
HI = lax.Precision.HIGHEST

NA, NX = 32, 4
J, Z, R, M = 16, 16, 512, 16
RI = 256
DIFF, ADV = 0.12, 0.2
COLUMNS = NA * J * NX * Z

NEAR = [(a, c) for a in (-1, 0, 1) for c in (-1, 0, 1) if (a, c) != (0, 0)]
FAR = [(a, c) for a in (14, 15, 16, 17, 18) for c in (-1, 0, 1)]
GROUPS = (0, 1, -1)
LATE, SAME, OPPOSITE = range(3)
PARTNERS = {
    (k, g): [(a, c) for a, c in NEAR + FAR if c == g and k == (OPPOSITE if a > 1 else LATE if a else SAME)]
    for k in range(3) for g in GROUPS if (k, g) != (SAME, 0)
}
GREETED = NEAR + FAR + [(6, 0), (6, 2), (-6, 0), (-6, 2)]
OTHERS = sorted(
    [(x, y, z, c) for x in range(4) for y in range(4) for z in range(4) for c in range(2) if x + y + z + c],
    key=lambda o: -(sum(v > 0 for v in o[:3]) * 8 + sum(v == 2 for v in o[:3])),
)


def slot_of(a, c):
    k = OPPOSITE if 1 < a % NA < NA - 1 else LATE if a else SAME
    return k, [x % NA for x, _ in PARTNERS[k, c]].index(a % NA)


def lane_iota(shape):
    return lax.broadcasted_iota(jnp.int32, shape, len(shape) - 1)


def row_iota(shape):
    return lax.broadcasted_iota(jnp.int32, shape, len(shape) - 2)


def left(v):
    return pltpu.roll(v, v.shape[-1] - 1, v.ndim - 1)


def right(v):
    return pltpu.roll(v, 1, v.ndim - 1)


def kernel(
    u_h, t_h, basis_h, coef_h, blade_h, off_h, extra_h, frac_h,
    fin, sen, tot,
    x0, u1, l2, l1, tg, bs, bh, prof, m1s, m1r, m2s, m2r, rrs, rrr, bb,
    blade_v, extra_v, frac_v, coef_s, off_s,
    loc, near_ss, near_rs, m_ss, m_rs, side_ss, side_rs, rr_ss, rr_rs, ready,
):
    az, ax = lax.axis_index("az"), lax.axis_index("ax")

    def partner(a, c):
        return ((az + a) & (NA - 1), (ax + c) & (NX - 1))

    def guard(c, act):
        if c == 0:
            act()
        else:
            pl.when((ax < NX - 1) if c > 0 else (ax > 0))(act)

    loads = [
        pltpu.make_async_copy(u_h, x0.at[2:18, 8:24, :], loc.at[0]),
        pltpu.make_async_copy(blade_h, blade_v, loc.at[1]),
        pltpu.make_async_copy(extra_h, extra_v, loc.at[2]),
        pltpu.make_async_copy(frac_h, frac_v, loc.at[3]),
        pltpu.make_async_copy(coef_h, coef_s, loc.at[4]),
        pltpu.make_async_copy(off_h, off_s, loc.at[5]),
        pltpu.make_async_copy(basis_h, bs, loc.at[6]),
        pltpu.make_async_copy(t_h, tg, loc.at[7]),
    ]
    loads[0].start()
    barrier = pltpu.get_barrier_semaphore()

    for a, c in GREETED:
        pl.semaphore_signal(barrier, inc=1, device_id=partner(a, c), device_id_type=MESH)
    for c in loads[1:]:
        c.start()

    loads[0].wait()
    tile = (8, 128)
    lane8 = lane_iota(tile)

    def take(j, acc):
        for i, (lo, k) in enumerate(((128, 1), (256, 0))):
            for h in range(2):
                at = 16 + 16 * i + 32 * h + j
                acc = jnp.where(lane8 == at, pltpu.roll(x0[j + 2, 8 + 8 * h : 16 + 8 * h, lo : lo + 128], lax.rem(at + k, 128), 1), acc)
        return acc

    taken = lax.fori_loop(0, J, take, jnp.zeros(tile, f32), unroll=True)
    for c in loads[1:4]:
        c.wait()
    m1s[...] = jnp.zeros(tile, f32)
    m1s[0:2, 0:16] = extra_v[...].astype(f32)
    m1s[2:4, 0:16] = frac_v[...]
    m1s[4:6, 0:16] = blade_v[...]
    m1s[...] = m1s[...] + taken

    for i in (4, 6):
        loads[i].wait()

    def mix(m, acc):
        return acc + coef_s[m] * bs[m]

    prof[8:24, :] = lax.fori_loop(0, M, mix, jnp.zeros((Z, R), f32), unroll=4)

    pl.semaphore_wait(barrier, len(GREETED))
    plane_dst = {-1: pl.ds(18, 2), 0: pl.ds(2, 16), 1: pl.ds(0, 2)}
    row_dst = {-1: pl.ds(24, 2), 0: pl.ds(8, 16), 1: pl.ds(6, 2)}
    plane_own = {-1: pl.ds(2, 2), 0: pl.ds(2, 16), 1: pl.ds(16, 2)}
    row_own = {-1: pl.ds(8, 2), 0: pl.ds(8, 16), 1: pl.ds(22, 2)}

    def near_copy(src, dst, a, c, n):
        i = NEAR.index((a, c))
        return pltpu.make_async_remote_copy(
            src_ref=src, dst_ref=dst.at[plane_dst[a], row_dst[c], :],
            send_sem=near_ss.at[n, i], recv_sem=near_rs.at[n, i],
            device_id=partner(a, c), device_id_type=MESH,
        )

    def message(src, dst, a, c, n):
        k, i = slot_of(-a, -c)
        return pltpu.make_async_remote_copy(
            src_ref=src, dst_ref=dst[k, -c].at[i],
            send_sem=m_ss.at[n, k, c + 1], recv_sem=m_rs.at[n, k, 1 - c],
            device_id=partner(a, c), device_id_type=MESH,
        )

    def near_group(k, c):
        return [n for n in NEAR if n[1] == c and (k == LATE) == (n[0] != 0)] if k != OPPOSITE else []

    def send_all(near_of, src, dst, n):
        for c in (1, -1, 0):
            def act(c=c):
                for k in (SAME, LATE, OPPOSITE):
                    for a, _ in near_group(k, c):
                        near_of(a, c).start()
                    for a, _ in PARTNERS.get((k, c), ()):
                        message(src, dst, a, c, n).start()
            guard(c, act)

    m1g = dict(zip(PARTNERS, m1r))
    m2g = dict(zip(PARTNERS, m2r))

    def near1(a, c):
        return near_copy(x0.at[plane_own[a], row_own[c], :], x0, a, c, 0)

    def side(c):
        i, src, dst = (0, 23, 7) if c > 0 else (1, 8, 24)
        return (
            pltpu.make_async_remote_copy(
                src_ref=prof.at[pl.ds(src, 1), :], dst_ref=prof.at[pl.ds(dst, 1), :],
                send_sem=side_ss.at[0, i], recv_sem=side_rs.at[0, i],
                device_id=partner(0, c), device_id_type=MESH),
            pltpu.make_async_remote_copy(
                src_ref=bs.at[:, pl.ds(src - 8, 1), :], dst_ref=bh.at[i],
                send_sem=side_ss.at[1, i], recv_sem=side_rs.at[1, i],
                device_id=partner(0, c), device_id_type=MESH),
        )

    for c in (1, -1):
        guard(c, lambda c=c: side(c)[0].start() and None)

    send_all(near1, m1s, m1g, 0)
    for c in (1, -1):
        guard(c, lambda c=c: side(c)[1].start() and None)


    for a, c in GREETED:
        pl.semaphore_signal(ready, inc=1, device_id=partner(a, c), device_id_type=MESH)

    for i in (5, 7):
        loads[i].wait()

    def whole(ref, ss, rs):
        return pltpu.make_async_remote_copy(
            src_ref=ref, dst_ref=ref, send_sem=ss, recv_sem=rs, device_id=partner(0, 1), device_id_type=MESH)

    def arrivals(near_of, dst, n, k):
        for c in GROUPS:
            def act(c=c):
                if (k, c) in PARTNERS:
                    whole(dst[k, c], m_ss.at[n, k, c + 1], m_rs.at[n, k, c + 1]).wait_recv()
                for a, _ in near_group(k, c):
                    near_of(-a, -c).wait_recv()
            guard(c, act)

    def departures(near_of, dst, n):
        for c in GROUPS:
            def act(c=c):
                for k in range(3):
                    if (k, c) in PARTNERS:
                        whole(dst[k, c], m_ss.at[n, k, c + 1], m_rs.at[n, k, c + 1]).wait_send()
                    for a, _ in near_group(k, c):
                        near_of(a, c).wait_send()
            guard(c, act)

    arrivals(near1, m1g, 0, SAME)
    for c in (1, -1):
        guard(c, lambda c=c: side(-c)[0].wait_recv() and None)
    lane32 = lane_iota((32, 128))

    near_off, far_off = (-1, 0, 1), (14, 15, 16, 17, 18)

    def gather_cols(own, ref, offsets, only, bases):
        def part(c, a, base, b):
            k, i = slot_of(a, c) if (a, c) != (0, 0) else (0, 0)
            v = own[...] if (a, c) == (0, 0) else ref[k, c][i]
            s = (16 * b - base) % 128
            return pltpu.roll(v, s, 1) if s else v

        cols = []
        for lo, hi in bases:
            out = jnp.zeros((32, 128), f32)
            for b, a in enumerate(offsets):
                if a not in only:
                    continue
                v = jnp.concatenate([part(-1, a, hi, b), part(0, a, lo, b), part(0, a, hi, b), part(1, a, lo, b)], axis=0)
                out = jnp.where((lane32 >= 16 * b) & (lane32 < 16 * b + 16), v, out)
            cols.append(out)
        return cols

    def gather_meta(offsets, only):
        out = jnp.zeros((8, 128), f32)
        for b, a in enumerate(offsets):
            if a not in only:
                continue
            k, i = slot_of(a, 0) if a else (0, 0)
            v = m1s[...] if a == 0 else m1g[k, 0][i]
            out = jnp.where((lane8 >= 16 * b) & (lane8 < 16 * b + 16), pltpu.roll(v, 16 * b, 1) if b else v, out)
        return out

    bases1 = ((16, 48), (32, 64))
    bases2 = ((0, 64), (16, 80), (32, 96), (48, 112))
    drift = off_s[0] - RI
    rows = row_iota((128, 128))
    lanes = lane_iota((128, 128))

    def weights(meta, base):
        w = meta[2:3, :]
        at = lanes + (drift + base) + meta[0:1, :].astype(jnp.int32)
        return jnp.where(rows == at, 1.0 - w, 0.0) + jnp.where(rows == at + 1, w, 0.0)

    def opposite(w_n, w_f, rn, sn, rf, sf):
        flux = jnp.dot(sf, w_n, precision=HI, preferred_element_type=f32) - rn
        fluxf = jnp.dot(sn, w_f, precision=HI, preferred_element_type=f32) - rf
        back = lax.dot_general(fluxf, w_f, (((1,), (1,)), ((), ())), precision=HI, preferred_element_type=f32)
        return flux, back

    def local_weights(meta):
        e, w = meta[1:2, :], meta[3:4, :]
        return (1.0 - e) * (1.0 - w), (1.0 - e) * w + e * (1.0 - w), e * w

    def spread(lw, v):
        return lw[0] * right(v) + lw[1] * v + lw[2] * left(v)

    def collect(lw, v):
        return left(lw[0] * v) + lw[1] * v + right(lw[2] * v)

    r32 = row_iota((32, 128))

    def c0_row(bl0, bl1):
        return (1.0 - 2 * DIFF) * bl0 + DIFF * (left(bl0) + right(bl0)) - ADV * (bl0 - right(bl0)) + bl1

    def plane_coefs(meta, lw):
        bl0, bl1 = meta[4:5, :], meta[5:6, :]
        eb = spread(lw, bl0)
        for i, v in enumerate((bl0, bl1, c0_row(bl0, bl1), collect(lw, bl0), collect(lw, eb), eb)):
            picked = jnp.where(lane32 == r32 + 15, jnp.broadcast_to(v, (32, 128)), 0.0)
            bb[i] = jnp.broadcast_to(jnp.sum(picked, axis=1, keepdims=True), (32, 128))

    def coef(i, q):
        return bb[i, pl.ds(q, 1), :]

    def wide(v):
        return jnp.concatenate([v] * 4, axis=1)

    ri = lane_iota((1, R))
    edge = (ri == RI - 1) | (ri == RI)
    ctr = jnp.where(edge, 1.0 - 5 * DIFF - ADV, 1.0 - 6 * DIFF - ADV).astype(f32)
    up = jnp.where((ri == RI - 1) | (ri == R - 1), 0.0, DIFF).astype(f32)
    dn = jnp.where((ri == RI) | (ri == 0), 0.0, DIFF).astype(f32)

    def stencil(v, strong, weak, vz):
        return ctr * v + up * left(v) + dn * right(v) + DIFF * (vz + weak) + (DIFF + ADV) * strong

    def beside(v):
        return pltpu.roll(v, 1, 0) + pltpu.roll(v, v.shape[0] - 1, 0)

    def columns_at(flux, back, k):
        ln = lane_iota(flux.shape)
        return (jnp.where(ln == 127, pltpu.roll(flux, (127 - k) & 127, 1), 0.0),
                jnp.where(ln == 0, pltpu.roll(back, (128 - k) & 127, 1), 0.0))

    def put(ref, idx, rows_, v, flux, back, k):
        f, b = columns_at(flux, back, k)
        ref[idx, rows_, 0:128] = v[:, 0:128]
        ref[idx, rows_, 128:256] = v[:, 128:256] + DIFF * f
        ref[idx, rows_, 256:384] = v[:, 256:384] - DIFF * b
        ref[idx, rows_, 384:512] = v[:, 384:512]

    def seal(ref, n, *parts):
        def clear(row):
            for lo, hi in parts:
                ref[lo:hi, pl.ds(row, n), :] = jnp.zeros((hi - lo, n, R), f32)

        pl.when(ax == 0)(lambda: clear(8 - n))
        pl.when(ax == NX - 1)(lambda: clear(24))

    ally, centre = slice(0, 32), slice(8, 24)
    lane = lane_iota((Z, 128))
    zero = jnp.zeros((Z, 128), f32)
    big = jnp.zeros((Z, R), f32)

    def step_u1(q):
        v = x0[q + 1]
        u1[q] = stencil(v, x0[q], x0[q + 2], beside(v)) + wide(coef(0, q)) * prof[...]

    def take1(q, rot, sta):
        a = pltpu.roll(u1[q, :, 128:256], (q + 16) & 127, 1)
        b = pltpu.roll(u1[q, :, 256:384], (q + 15) & 127, 1)
        return jnp.where(lane32 == q + 15, a, rot), jnp.where(lane32 == q + 15, b, sta)

    def step_u2(j, carry):
        ls, qs, ps, a1, a2, a3, cols = carry
        v = u1[j + 1]
        new = stencil(v[8:24], u1[j, 8:24, :], u1[j + 2, 8:24, :], beside(v)[8:24]) + wide(coef(1, j + 1)) * prof[8:24, :]
        fin[j] = new
        lam = new - tg[j]
        l2[j + 2, 8:24, :] = lam
        mid1, mid2 = lam[:, 128:256], lam[:, 256:384]
        for i, (t, l) in enumerate(((mid1, 126), (mid1, 127), (mid2, 0), (mid2, 1))):
            for h in range(2):
                k = j + bases2[i][h]
                cols = jnp.where(lane8 == k, pltpu.roll(t[8 * h : 8 * h + 8], (k + 128 - l) & 127, 1), cols)
        q = j + 1
        return (ls + lam * lam, qs + wide(coef(2, q)) * lam, ps + wide(coef(0, q)) * lam,
                a1 + coef(3, q) * mid2, a2 + coef(4, q) * mid2, a3 + coef(5, q) * mid1, cols)

    def local_flux(lw, rot, sta):
        flux = spread(lw, sta) - rot
        return flux, collect(lw, flux)

    meta_o = gather_meta(near_off, (0,))
    plane_coefs(meta_o, local_weights(meta_o))
    seal(x0, 2, (0, 20))

    def inner_u1(q, _):
        step_u1(q)
        return 0

    lax.fori_loop(2, 16, inner_u1, 0, unroll=7)
    seal(u1, 1, (2, 16))
    wide0 = jnp.zeros((32, 128), f32)
    rot1, sta1 = lax.fori_loop(2, 16, lambda q, c: take1(q, *c), (wide0, wide0), unroll=14)
    sums = lax.fori_loop(2, 14, step_u2, (big, big, big, zero, zero, zero, jnp.zeros(tile, f32)), unroll=4)

    arrivals(near1, m1g, 0, OPPOSITE)
    rot_f, sta_f = gather_cols(m1s, m1g, far_off, far_off, bases1)
    meta_f = gather_meta(far_off, far_off)
    w_f, lw_f = weights(meta_f, -16), local_weights(meta_f)
    rot_o, sta_o = gather_cols(m1s, m1g, near_off, (0,), bases1)

    arrivals(near1, m1g, 0, LATE)
    rot_e, sta_e = gather_cols(m1s, m1g, near_off, (-1, 1), bases1)
    rot_n, sta_n = rot_o + rot_e, sta_o + sta_e
    meta_n = meta_o + gather_meta(near_off, (-1, 1))
    lw_n, w_n = local_weights(meta_n), weights(meta_n, 16)
    flux0, back0 = opposite(w_n, w_f, rot_n, sta_n, rot_f, sta_f)
    plane_coefs(meta_n, lw_n)
    for q in (0, 1, 16, 17):
        step_u1(q)
    seal(u1, 1, (0, 2), (16, 18))
    for q in (0, 1, 16, 17):
        rot1, sta1 = take1(q, rot1, sta1)
    for j in (0, 1, 14, 15):
        sums = step_u2(j, sums)
    ls, qs, ps, a1, a2, a3, cols = sums

    zrow = row_iota((32, 128))
    inside = ((zrow >= 8) | (ax != 0)) & ((zrow < 24) | (ax != NX - 1))
    live = inside & (lane32 >= 15) & (lane32 <= 32)
    d255 = jnp.where(live, DIFF * flux0, 0.0)
    d256 = jnp.where(live, -DIFF * back0, 0.0)
    flux1, back1 = local_flux(lw_n, rot1 + d255, sta1 + d256)

    def pushed(d):
        return (1.0 - 5 * DIFF - ADV) * d + DIFF * (left(d) + beside(d)) + (DIFF + ADV) * right(d)

    own = (lane >= 16) & (lane < 32)
    adds = [jnp.where(own, v[8:24], 0.0)
            for v in (DIFF * d255, pushed(d255) + DIFF * flux1, pushed(d256) - DIFF * back1, DIFF * d256)]
    for j in (0, 1, 14, 15, *range(2, 14)):
        r = [pltpu.roll(v, (l - j - 16) & 127, 1) for v, l in zip(adds, (126, 127, 0, 1))]
        add1 = jnp.where(lane == 126, r[0], jnp.where(lane == 127, r[1], 0.0))
        add2 = jnp.where(lane == 0, r[2], jnp.where(lane == 1, r[3], 0.0))
        l2[j + 2, 8:24, 128:256] += add1
        l2[j + 2, 8:24, 256:384] += add2
        fin[j, :, 128:256] += add1
        fin[j, :, 256:384] += add2
    more = jnp.zeros(tile, f32)
    for i, v in enumerate(adds):
        for h in range(2):
            s = (bases2[i][h] - 16) & 127
            more = more + (pltpu.roll(v[8 * h : 8 * h + 8], s, 1) if s else v[8 * h : 8 * h + 8])
    m2s[...] = cols + more

    def near2(a, c):
        return near_copy(l2.at[plane_own[a], row_own[c], :], l2, a, c, 1)

    send_all(near2, m2s, m2g, 1)

    for c in (1, -1):
        guard(c, lambda c=c: side(-c)[1].wait_recv() and None)

    bl0, bl1 = meta_n[4:5, :], meta_n[5:6, :]
    eb = spread(lw_n, bl0)

    def along(row, v):
        return jnp.sum(row * v, axis=1, keepdims=True)

    crow = c0_row(bl0, bl1)
    for_q, for_p = [[along(r, v) for v in adds] for r in (crow, bl0)]

    def fix(v, parts):
        one, two = v[:, 128:256], v[:, 256:384]
        one = one + jnp.where(lane == 126, parts[0], 0.0) + jnp.where(lane == 127, parts[1], 0.0)
        two = two + jnp.where(lane == 0, parts[2], 0.0) + jnp.where(lane == 1, parts[3], 0.0)
        return jnp.concatenate([v[:, 0:128], one, two, v[:, 384:512]], axis=1)

    qs, ps = fix(qs, for_q), fix(ps, for_p)
    a1 = a1 + along(collect(lw_n, bl0), adds[2])
    a2 = a2 + along(collect(lw_n, eb), adds[2])
    a3 = a3 + along(eb, adds[1])
    zr = row_iota((Z, R))
    pz = jnp.where(zr == 0, 0.0, pltpu.roll(ps, 1, 0)) + jnp.where(zr == Z - 1, 0.0, pltpu.roll(ps, Z - 1, 0))
    vv = qs + (ctr - (1.0 - 6 * DIFF - ADV) - 4 * DIFF) * ps + up * left(ps) + dn * right(ps) + DIFF * pz
    at255 = jnp.where(lane == 127, left(a1) - ps[:, 128:256], 0.0)
    at256 = jnp.where(lane == 0, a2 - right(a3), 0.0)
    vv = vv + DIFF * jnp.concatenate([zero, at255, -at256, zero], axis=1)
    top = jnp.where(ax == 0, 0.0, DIFF) * ps[0:1, :]
    bot = jnp.where(ax == NX - 1, 0.0, DIFF) * ps[15:16, :]

    def fold(v):
        v = v[:, 0:128] + v[:, 128:256] + v[:, 256:384] + v[:, 384:512]
        return jnp.sum(v, axis=0, keepdims=True)

    rowsum = []
    for m in range(M):
        rowsum.append(fold(bs[m] * vv) + fold(bh[0, m] * top + bh[1, m] * bot))
    rowsum.append(fold(ls) + jnp.sum(more * (2.0 * cols + more), axis=0, keepdims=True))
    rowsum.append(jnp.zeros((7, 128), f32))
    stack = jnp.concatenate(rowsum, axis=0)
    stack = jnp.broadcast_to(jnp.sum(stack, axis=1, keepdims=True), (24, 128))
    rrs[...] = jnp.sum(jnp.where(row_iota((24, 128)) == lane_iota((24, 128)), stack, 0.0), axis=0, keepdims=True)

    pl.semaphore_wait(ready, len(GREETED))
    px, pz_, py, pc = (az >> 2) & 3, az & 3, (ax >> 1) * 2 + (az >> 4), ax & 1
    xs = [((px + d) & 3) << 2 for d in range(4)]
    zs = [(pz_ + d) & 3 for d in range(4)]
    ys = [(((py + d) & 1) << 4, (((py + d) >> 1) & 1) << 1) for d in range(4)]
    cs = [pc, 1 - pc]
    for x, y, z, c in OTHERS:
        pltpu.make_async_remote_copy(
            src_ref=rrs, dst_ref=rrr.at[OTHERS.index((-x % 4, -y % 4, -z % 4, c))], send_sem=rr_ss.at[0], recv_sem=rr_rs.at[0],
            device_id=(ys[y][0] + xs[x] + zs[z], ys[y][1] + cs[c]), device_id_type=MESH).start()

    def misfit_cols(offsets, only):
        return [jnp.where(inside, c, 0.0) for c in gather_cols(m2s, m2g, offsets, only, bases2)]

    def adjoint_cols(cs, lw):
        c254, c255, c256, c257 = cs
        flux, back = local_flux(lw, c255, c256)

        def one(c, out, term):
            return (1.0 - 5 * DIFF - ADV) * c + DIFF * (out + right(c) + beside(c)) + (DIFF + ADV) * left(c) + DIFF * term

        return flux, back, one(c255, c254, flux)[8:24], one(c256, c257, -back)[8:24]

    def step_l1(q, flux, back):
        v = l2[q + 1]
        new = stencil(v, l2[q + 2], l2[q], beside(v))
        put(l1, q, ally, new, flux, back, q + 15)

    def step_l0(j):
        v = l1[j + 1]
        sen[j] = stencil(v[8:24], l1[j + 2, 8:24, :], l1[j, 8:24, :], beside(v)[8:24])

    arrivals(near2, m2g, 1, SAME)
    seal(l2, 2, (0, 20))
    cols_o = misfit_cols(near_off, (0,))
    flux_n, back_n = local_flux(lw_n, cols_o[1], cols_o[2])

    def inner_l1(q, _):
        step_l1(q, flux_n, back_n)
        return 0

    def inner_l0(j, _):
        step_l0(j)
        return 0

    lax.fori_loop(3, 15, inner_l1, 0, unroll=4)
    seal(l1, 1, (3, 15))
    lax.fori_loop(3, 13, inner_l0, 0, unroll=5)
    arrivals(near2, m2g, 1, OPPOSITE)
    _, _, rot_f1, sta_f1 = adjoint_cols(misfit_cols(far_off, far_off), lw_f)

    arrivals(near2, m2g, 1, LATE)
    flux_n, back_n, rot_n1, sta_n1 = adjoint_cols([o + e for o, e in zip(cols_o, misfit_cols(near_off, (-1, 1)))], lw_n)
    fluxa, backa = opposite(w_n, w_f, rot_n1, sta_n1, rot_f1, sta_f1)
    for q in (0, 1, 2, 15, 16, 17):
        step_l1(q, flux_n, back_n)
    seal(l1, 1, (0, 3), (15, 18))
    for j in (0, 1, 2, 13, 14, 15):
        step_l0(j)
    for j in range(J):
        f, b = columns_at(fluxa, backa, j + 16)
        sen[j, :, 128:256] += DIFF * f
        sen[j, :, 256:384] -= DIFF * b

    whole(rrr, rr_ss.at[0], rr_rs.at[0]).wait_recv()
    total = rrs[...] + jnp.sum(rrr[...], axis=0)
    tot[...] = jnp.broadcast_to(total, (8, 128))

    departures(near1, m1g, 0)
    departures(near2, m2g, 1)
    for c in (1, -1):
        def act(c=c):
            for copy in side(c):
                copy.wait_send()
        guard(c, act)
    whole(rrr, rr_ss.at[0], rr_rs.at[0]).wait_send()


def finish(fin, sen, tot, fin_o, sen_o, grad_o, loss_o, sems):
    a = pltpu.make_async_copy(fin, fin_o, sems.at[0])
    b = pltpu.make_async_copy(sen, sen_o, sems.at[1])
    a.start()
    b.start()
    row = tot[0:1, :]
    grad_o[...] = row[:, 0:M] * (1.0 / COLUMNS)
    loss_o[...] = row[:, M : M + 1] * (0.5 / (COLUMNS * R))
    a.wait()
    b.wait()


def on_device(initial, target, basis, coefficients, blade, offset, extra, frac):
    vm = pl.BlockSpec(memory_space=pltpu.VMEM)
    hbm = pl.BlockSpec(memory_space=pltpu.HBM)
    block = jax.ShapeDtypeStruct((J, Z, R), f32)
    dma = pltpu.SemaphoreType.DMA
    fin, sen, tot = pl.pallas_call(
        kernel,
        out_shape=(pltpu.VMEM((J, Z, R), f32), pltpu.VMEM((J, Z, R), f32), pltpu.VMEM((8, 128), f32)),
        in_specs=[hbm] * 8,
        out_specs=(vm, vm, vm),
        scratch_shapes=[
            pltpu.VMEM((20, 32, R), f32), pltpu.VMEM((18, 32, R), f32),
            pltpu.VMEM((20, 32, R), f32), pltpu.VMEM((18, 32, R), f32),
            pltpu.VMEM((J, Z, R), f32), pltpu.VMEM((M, Z, R), f32), pltpu.VMEM((2, M, 1, R), f32),
            pltpu.VMEM((32, R), f32),
            *[pltpu.VMEM((8, 128), f32), [pltpu.VMEM((len(p), 8, 128), f32) for p in PARTNERS.values()]] * 2,
            pltpu.VMEM((1, 128), f32), pltpu.VMEM((NA * NX - 1, 1, 128), f32),
            pltpu.VMEM((6, 32, 128), f32),
            pltpu.VMEM((2, J), f32), pltpu.VMEM((2, J), jnp.int32), pltpu.VMEM((2, J), f32),
            pltpu.SMEM((M,), f32), pltpu.SMEM((2,), jnp.int32),
            dma((8,)), dma((2, 8)), dma((2, 8)), dma((2, 3, 3)), dma((2, 3, 3)), dma((2, 2)), dma((2, 2)), dma((1,)), dma((1,)),
            pltpu.SemaphoreType.REGULAR,
        ],
        compiler_params=pltpu.CompilerParams(collective_id=0, has_side_effects=True, vmem_limit_bytes=40 * 1024 * 1024),
    )(*(pltpu.with_memory_space_constraint(v, pltpu.HBM) for v in (initial, target, basis, coefficients, blade, offset, extra, frac)))
    fin, sen, grad, loss = pl.pallas_call(
        finish,
        out_shape=(block, block, jax.ShapeDtypeStruct((1, M), f32), jax.ShapeDtypeStruct((1, 1), f32)),
        in_specs=[vm] * 3,
        out_specs=(hbm, hbm, vm, vm),
        scratch_shapes=[dma((2,))],
    )(*(pltpu.with_memory_space_constraint(v, pltpu.VMEM) for v in (fin, sen, tot)))
    return fin, sen, grad.reshape(M), loss.reshape(())


def solution(mesh):
    block = P("az", "ax", None)
    row = P(None, "az")
    return jax.shard_map(
        on_device,
        mesh=mesh,
        in_specs=(block, block, P(None, "ax", None), P(), row, P(), row, row),
        out_specs=(block, block, P(), P()),
        check_vma=False,
    )
```

```python
import functools

import jax
import jax.numpy as jnp
from jax import lax
from jax.experimental import pallas as pl
from jax.experimental.pallas import tpu as pltpu
from jax.sharding import PartitionSpec as P

MESH = pl.DeviceIdType.MESH
f32 = jnp.float32
HI = lax.Precision.HIGHEST

NA, NX = 32, 4
J, Z, R, M = 16, 16, 512, 16
RI = 256
DIFF, ADV = 0.12, 0.2
COLUMNS = NA * J * NX * Z

NEAR = [(a, c) for a in (-1, 0, 1) for c in (-1, 0, 1) if (a, c) != (0, 0)]
FAR = [(a, c) for a in (14, 15, 16, 17, 18) for c in (-1, 0, 1)]
GROUPS = (0, 1, -1)
LATE, SAME, OPPOSITE = range(3)
PARTNERS = {
    (k, g): [(a, c) for a, c in NEAR + FAR if c == g and k == (OPPOSITE if a > 1 else LATE if a else SAME)]
    for k in range(3) for g in GROUPS if (k, g) != (SAME, 0)
}
ALWAYS = [(-1, 0), (1, 0), (0, -1), (0, 1)] + [(a, 0) for a in range(14, 19)] + [(16, -1), (16, 1)]
ALWAYS += [(a, c) for a in (-8, -4, 4, 8) for c in (0, 2)]
INSIDE = [-1, 1, 14, 15, 17, 18]
AROUND = [-4, 4]
OTHERS = sorted(
    [(x, y, z, c) for x in range(4) for y in range(4) for z in range(4) for c in range(2) if x + y + z + c],
    key=lambda o: -(sum(v > 0 for v in o[:3]) * 8 + sum(v == 2 for v in o[:3])),
)


def slot_of(a, c):
    k = OPPOSITE if 1 < a % NA < NA - 1 else LATE if a else SAME
    return k, [x % NA for x, _ in PARTNERS[k, c]].index(a % NA)


def lane_iota(shape):
    return lax.broadcasted_iota(jnp.int32, shape, len(shape) - 1)


def row_iota(shape):
    return lax.broadcasted_iota(jnp.int32, shape, len(shape) - 2)


def left(v):
    return pltpu.roll(v, v.shape[-1] - 1, v.ndim - 1)


def right(v):
    return pltpu.roll(v, 1, v.ndim - 1)


def kernel(
    u_h, t_h, basis_h, coef_h, blade_h, off_h, extra_h, frac_h,
    fin, sen, tot,
    x0, u1, l2, l1, tg, bs, bh, prof, m1s, m1r, m2s, m2r, rrs, rrr, bb,
    blade_v, extra_v, frac_v, coef_s, off_s,
    loc, near_ss, near_rs, m_ss, m_rs, side_ss, side_rs, rr_ss, rr_rs, ready,
):
    az, ax = lax.axis_index("az"), lax.axis_index("ax")

    def partner(a, c):
        return ((az + a) & (NA - 1), (ax + c) & (NX - 1))

    def guard(c, act):
        if c == 0:
            act()
        else:
            pl.when((ax < NX - 1) if c > 0 else (ax > 0))(act)

    loads = [
        pltpu.make_async_copy(u_h, x0.at[2:18, 8:24, :], loc.at[0]),
        pltpu.make_async_copy(blade_h, blade_v, loc.at[1]),
        pltpu.make_async_copy(extra_h, extra_v, loc.at[2]),
        pltpu.make_async_copy(frac_h, frac_v, loc.at[3]),
        pltpu.make_async_copy(coef_h, coef_s, loc.at[4]),
        pltpu.make_async_copy(off_h, off_s, loc.at[5]),
        pltpu.make_async_copy(basis_h, bs, loc.at[6]),
        pltpu.make_async_copy(t_h, tg, loc.at[7]),
    ]
    loads[0].start()
    barrier = pltpu.get_barrier_semaphore()

    def greet(sem):
        def signal(a, c):
            pl.semaphore_signal(sem, inc=1, device_id=partner(a, c), device_id_type=MESH)

        for a, c in ALWAYS:
            signal(a, c)
        for c in (1, -1):
            at_end = ax == (NX - 1 if c > 0 else 0)

            @pl.when(at_end)
            def _(c=c):
                for a in AROUND:
                    signal(a, c)

            @pl.when(jnp.logical_not(at_end))
            def _(c=c):
                for a in INSIDE:
                    signal(a, c)

    greeted = len(ALWAYS) + 2 * len(INSIDE) - jnp.where((ax == 0) | (ax == NX - 1), len(INSIDE) - len(AROUND), 0)
    greet(barrier)
    for c in loads[1:]:
        c.start()

    loads[0].wait()
    tile = (8, 128)
    lane8 = lane_iota(tile)

    def take(j, acc):
        for i, (lo, k) in enumerate(((128, 1), (256, 0))):
            for h in range(2):
                at = 16 + 16 * i + 32 * h + j
                acc = jnp.where(lane8 == at, pltpu.roll(x0[j + 2, 8 + 8 * h : 16 + 8 * h, lo : lo + 128], lax.rem(at + k, 128), 1), acc)
        return acc

    taken = lax.fori_loop(0, J, take, jnp.zeros(tile, f32), unroll=True)
    for c in loads[1:4]:
        c.wait()
    m1s[...] = jnp.zeros(tile, f32)
    m1s[0:2, 0:16] = extra_v[...].astype(f32)
    m1s[2:4, 0:16] = frac_v[...]
    m1s[4:6, 0:16] = blade_v[...]
    m1s[...] = m1s[...] + taken

    for i in (4, 6):
        loads[i].wait()

    def mix(m, acc):
        return acc + coef_s[m] * bs[m]

    prof[8:24, :] = lax.fori_loop(0, M, mix, jnp.zeros((Z, R), f32), unroll=4)

    pl.semaphore_wait(barrier, greeted)
    plane_dst = {-1: pl.ds(18, 2), 0: pl.ds(2, 16), 1: pl.ds(0, 2)}
    row_dst = {-1: pl.ds(24, 2), 0: pl.ds(8, 16), 1: pl.ds(6, 2)}
    plane_own = {-1: pl.ds(2, 2), 0: pl.ds(2, 16), 1: pl.ds(16, 2)}
    row_own = {-1: pl.ds(8, 2), 0: pl.ds(8, 16), 1: pl.ds(22, 2)}

    def near_copy(src, dst, a, c, n):
        i = NEAR.index((a, c))
        return pltpu.make_async_remote_copy(
            src_ref=src, dst_ref=dst.at[plane_dst[a], row_dst[c], :],
            send_sem=near_ss.at[n, i], recv_sem=near_rs.at[n, i],
            device_id=partner(a, c), device_id_type=MESH,
        )

    def message(src, dst, a, c, n):
        k, i = slot_of(-a, -c)
        return pltpu.make_async_remote_copy(
            src_ref=src, dst_ref=dst[k, -c].at[i],
            send_sem=m_ss.at[n, k, c + 1], recv_sem=m_rs.at[n, k, 1 - c],
            device_id=partner(a, c), device_id_type=MESH,
        )

    def near_group(k, c):
        return [n for n in NEAR if n[1] == c and (k == LATE) == (n[0] != 0)] if k != OPPOSITE else []

    def send_all(near_of, src, dst, n):
        for c in (1, -1, 0):
            def act(c=c):
                for k in (SAME, LATE, OPPOSITE):
                    for a, _ in near_group(k, c):
                        near_of(a, c).start()
                    for a, _ in PARTNERS.get((k, c), ()):
                        message(src, dst, a, c, n).start()
            guard(c, act)

    m1g = dict(zip(PARTNERS, m1r))
    m2g = dict(zip(PARTNERS, m2r))

    def near1(a, c):
        return near_copy(x0.at[plane_own[a], row_own[c], :], x0, a, c, 0)

    def side(c):
        i, src, dst = (0, 23, 7) if c > 0 else (1, 8, 24)
        return (
            pltpu.make_async_remote_copy(
                src_ref=prof.at[pl.ds(src, 1), :], dst_ref=prof.at[pl.ds(dst, 1), :],
                send_sem=side_ss.at[0, i], recv_sem=side_rs.at[0, i],
                device_id=partner(0, c), device_id_type=MESH),
            pltpu.make_async_remote_copy(
                src_ref=bs.at[:, pl.ds(src - 8, 1), :], dst_ref=bh.at[i],
                send_sem=side_ss.at[1, i], recv_sem=side_rs.at[1, i],
                device_id=partner(0, c), device_id_type=MESH),
        )

    for c in (1, -1):
        guard(c, lambda c=c: side(c)[0].start() and None)

    send_all(near1, m1s, m1g, 0)
    for c in (1, -1):
        guard(c, lambda c=c: side(c)[1].start() and None)


    greet(ready)

    for i in (5, 7):
        loads[i].wait()

    def whole(ref, ss, rs):
        return pltpu.make_async_remote_copy(
            src_ref=ref, dst_ref=ref, send_sem=ss, recv_sem=rs, device_id=partner(0, 1), device_id_type=MESH)

    def arrivals(near_of, dst, n, k):
        for c in GROUPS:
            def act(c=c):
                if (k, c) in PARTNERS:
                    whole(dst[k, c], m_ss.at[n, k, c + 1], m_rs.at[n, k, c + 1]).wait_recv()
                for a, _ in near_group(k, c):
                    near_of(-a, -c).wait_recv()
            guard(c, act)

    def departures(near_of, dst, n):
        for c in GROUPS:
            def act(c=c):
                for k in range(3):
                    if (k, c) in PARTNERS:
                        whole(dst[k, c], m_ss.at[n, k, c + 1], m_rs.at[n, k, c + 1]).wait_send()
                    for a, _ in near_group(k, c):
                        near_of(a, c).wait_send()
            guard(c, act)

    arrivals(near1, m1g, 0, SAME)
    for c in (1, -1):
        guard(c, lambda c=c: side(-c)[0].wait_recv() and None)
    lane32 = lane_iota((32, 128))

    near_off, far_off = (-1, 0, 1), (14, 15, 16, 17, 18)

    def gather_cols(own, ref, offsets, only, bases):
        def part(c, a, base, b):
            k, i = slot_of(a, c) if (a, c) != (0, 0) else (0, 0)
            v = own[...] if (a, c) == (0, 0) else ref[k, c][i]
            s = (16 * b - base) % 128
            return pltpu.roll(v, s, 1) if s else v

        cols = []
        for lo, hi in bases:
            out = jnp.zeros((32, 128), f32)
            for b, a in enumerate(offsets):
                if a not in only:
                    continue
                v = jnp.concatenate([part(-1, a, hi, b), part(0, a, lo, b), part(0, a, hi, b), part(1, a, lo, b)], axis=0)
                out = jnp.where((lane32 >= 16 * b) & (lane32 < 16 * b + 16), v, out)
            cols.append(out)
        return cols

    def gather_meta(offsets, only):
        out = jnp.zeros((8, 128), f32)
        for b, a in enumerate(offsets):
            if a not in only:
                continue
            k, i = slot_of(a, 0) if a else (0, 0)
            v = m1s[...] if a == 0 else m1g[k, 0][i]
            out = jnp.where((lane8 >= 16 * b) & (lane8 < 16 * b + 16), pltpu.roll(v, 16 * b, 1) if b else v, out)
        return out

    bases1 = ((16, 48), (32, 64))
    bases2 = ((0, 64), (16, 80), (32, 96), (48, 112))
    drift = off_s[0] - RI
    rows = row_iota((128, 128))
    lanes = lane_iota((128, 128))

    def weights(meta, base):
        w = meta[2:3, :]
        at = lanes + (drift + base) + meta[0:1, :].astype(jnp.int32)
        return jnp.where(rows == at, 1.0 - w, 0.0) + jnp.where(rows == at + 1, w, 0.0)

    def opposite(w_n, w_f, rn, sn, rf, sf):
        flux = jnp.dot(sf, w_n, precision=HI, preferred_element_type=f32) - rn
        fluxf = jnp.dot(sn, w_f, precision=HI, preferred_element_type=f32) - rf
        back = lax.dot_general(fluxf, w_f, (((1,), (1,)), ((), ())), precision=HI, preferred_element_type=f32)
        return flux, back

    def local_weights(meta):
        e, w = meta[1:2, :], meta[3:4, :]
        return (1.0 - e) * (1.0 - w), (1.0 - e) * w + e * (1.0 - w), e * w

    def spread(lw, v):
        return lw[0] * right(v) + lw[1] * v + lw[2] * left(v)

    def collect(lw, v):
        return left(lw[0] * v) + lw[1] * v + right(lw[2] * v)

    r32 = row_iota((32, 128))

    def c0_row(bl0, bl1):
        return (1.0 - 2 * DIFF) * bl0 + DIFF * (left(bl0) + right(bl0)) - ADV * (bl0 - right(bl0)) + bl1

    def plane_coefs(meta, lw):
        bl0, bl1 = meta[4:5, :], meta[5:6, :]
        eb = spread(lw, bl0)
        for i, v in enumerate((bl0, bl1, c0_row(bl0, bl1), collect(lw, bl0), collect(lw, eb), eb)):
            picked = jnp.where(lane32 == r32 + 15, jnp.broadcast_to(v, (32, 128)), 0.0)
            bb[i] = jnp.broadcast_to(jnp.sum(picked, axis=1, keepdims=True), (32, 128))

    def coef(i, q):
        return bb[i, pl.ds(q, 1), :]

    def wide(v):
        return jnp.concatenate([v] * 4, axis=1)

    ri = lane_iota((1, R))
    edge = (ri == RI - 1) | (ri == RI)
    ctr = jnp.where(edge, 1.0 - 5 * DIFF - ADV, 1.0 - 6 * DIFF - ADV).astype(f32)
    up = jnp.where((ri == RI - 1) | (ri == R - 1), 0.0, DIFF).astype(f32)
    dn = jnp.where((ri == RI) | (ri == 0), 0.0, DIFF).astype(f32)

    def stencil(v, strong, weak, vz):
        return ctr * v + up * left(v) + dn * right(v) + DIFF * (vz + weak) + (DIFF + ADV) * strong

    def beside(v):
        return pltpu.roll(v, 1, 0) + pltpu.roll(v, v.shape[0] - 1, 0)

    def columns_at(flux, back, k):
        ln = lane_iota(flux.shape)
        return (jnp.where(ln == 127, pltpu.roll(flux, (127 - k) & 127, 1), 0.0),
                jnp.where(ln == 0, pltpu.roll(back, (128 - k) & 127, 1), 0.0))

    def put(ref, idx, rows_, v, flux, back, k):
        f, b = columns_at(flux, back, k)
        ref[idx, rows_, 0:128] = v[:, 0:128]
        ref[idx, rows_, 128:256] = v[:, 128:256] + DIFF * f
        ref[idx, rows_, 256:384] = v[:, 256:384] - DIFF * b
        ref[idx, rows_, 384:512] = v[:, 384:512]

    def seal(ref, n, *parts):
        def clear(row):
            for lo, hi in parts:
                ref[lo:hi, pl.ds(row, n), :] = jnp.zeros((hi - lo, n, R), f32)

        pl.when(ax == 0)(lambda: clear(8 - n))
        pl.when(ax == NX - 1)(lambda: clear(24))

    ally, centre = slice(0, 32), slice(8, 24)
    lane = lane_iota((Z, 128))
    zero = jnp.zeros((Z, 128), f32)
    big = jnp.zeros((Z, R), f32)

    def step_u1(q):
        v = x0[q + 1]
        u1[q] = stencil(v, x0[q], x0[q + 2], beside(v)) + wide(coef(0, q)) * prof[...]

    def take1(q, rot, sta):
        a = pltpu.roll(u1[q, :, 128:256], (q + 16) & 127, 1)
        b = pltpu.roll(u1[q, :, 256:384], (q + 15) & 127, 1)
        return jnp.where(lane32 == q + 15, a, rot), jnp.where(lane32 == q + 15, b, sta)

    def step_u2(j, carry):
        ls, qs, ps, a1, a2, a3, cols = carry
        v = u1[j + 1]
        new = stencil(v[8:24], u1[j, 8:24, :], u1[j + 2, 8:24, :], beside(v)[8:24]) + wide(coef(1, j + 1)) * prof[8:24, :]
        fin[j] = new
        lam = new - tg[j]
        l2[j + 2, 8:24, :] = lam
        mid1, mid2 = lam[:, 128:256], lam[:, 256:384]
        for i, (t, l) in enumerate(((mid1, 126), (mid1, 127), (mid2, 0), (mid2, 1))):
            for h in range(2):
                k = j + bases2[i][h]
                cols = jnp.where(lane8 == k, pltpu.roll(t[8 * h : 8 * h + 8], (k + 128 - l) & 127, 1), cols)
        q = j + 1
        return (ls + lam * lam, qs + wide(coef(2, q)) * lam, ps + wide(coef(0, q)) * lam,
                a1 + coef(3, q) * mid2, a2 + coef(4, q) * mid2, a3 + coef(5, q) * mid1, cols)

    def local_flux(lw, rot, sta):
        flux = spread(lw, sta) - rot
        return flux, collect(lw, flux)

    meta_o = gather_meta(near_off, (0,))
    plane_coefs(meta_o, local_weights(meta_o))
    seal(x0, 2, (0, 20))

    def inner_u1(q, _):
        step_u1(q)
        return 0

    lax.fori_loop(2, 16, inner_u1, 0, unroll=7)
    seal(u1, 1, (2, 16))
    wide0 = jnp.zeros((32, 128), f32)
    rot1, sta1 = lax.fori_loop(2, 16, lambda q, c: take1(q, *c), (wide0, wide0), unroll=14)
    sums = lax.fori_loop(2, 14, step_u2, (big, big, big, zero, zero, zero, jnp.zeros(tile, f32)), unroll=4)

    arrivals(near1, m1g, 0, OPPOSITE)
    rot_f, sta_f = gather_cols(m1s, m1g, far_off, far_off, bases1)
    meta_f = gather_meta(far_off, far_off)
    w_f, lw_f = weights(meta_f, -16), local_weights(meta_f)
    rot_o, sta_o = gather_cols(m1s, m1g, near_off, (0,), bases1)

    arrivals(near1, m1g, 0, LATE)
    rot_e, sta_e = gather_cols(m1s, m1g, near_off, (-1, 1), bases1)
    rot_n, sta_n = rot_o + rot_e, sta_o + sta_e
    meta_n = meta_o + gather_meta(near_off, (-1, 1))
    lw_n, w_n = local_weights(meta_n), weights(meta_n, 16)
    flux0, back0 = opposite(w_n, w_f, rot_n, sta_n, rot_f, sta_f)
    plane_coefs(meta_n, lw_n)
    for q in (0, 1, 16, 17):
        step_u1(q)
    seal(u1, 1, (0, 2), (16, 18))
    for q in (0, 1, 16, 17):
        rot1, sta1 = take1(q, rot1, sta1)
    for j in (0, 1, 14, 15):
        sums = step_u2(j, sums)
    ls, qs, ps, a1, a2, a3, cols = sums

    zrow = row_iota((32, 128))
    inside = ((zrow >= 8) | (ax != 0)) & ((zrow < 24) | (ax != NX - 1))
    live = inside & (lane32 >= 15) & (lane32 <= 32)
    d255 = jnp.where(live, DIFF * flux0, 0.0)
    d256 = jnp.where(live, -DIFF * back0, 0.0)
    flux1, back1 = local_flux(lw_n, rot1 + d255, sta1 + d256)

    def pushed(d):
        return (1.0 - 5 * DIFF - ADV) * d + DIFF * (left(d) + beside(d)) + (DIFF + ADV) * right(d)

    own = (lane >= 16) & (lane < 32)
    adds = [jnp.where(own, v[8:24], 0.0)
            for v in (DIFF * d255, pushed(d255) + DIFF * flux1, pushed(d256) - DIFF * back1, DIFF * d256)]
    for j in (0, 1, 14, 15, *range(2, 14)):
        r = [pltpu.roll(v, (l - j - 16) & 127, 1) for v, l in zip(adds, (126, 127, 0, 1))]
        add1 = jnp.where(lane == 126, r[0], jnp.where(lane == 127, r[1], 0.0))
        add2 = jnp.where(lane == 0, r[2], jnp.where(lane == 1, r[3], 0.0))
        l2[j + 2, 8:24, 128:256] += add1
        l2[j + 2, 8:24, 256:384] += add2
        fin[j, :, 128:256] += add1
        fin[j, :, 256:384] += add2
    more = jnp.zeros(tile, f32)
    for i, v in enumerate(adds):
        for h in range(2):
            s = (bases2[i][h] - 16) & 127
            more = more + (pltpu.roll(v[8 * h : 8 * h + 8], s, 1) if s else v[8 * h : 8 * h + 8])
    m2s[...] = cols + more

    def near2(a, c):
        return near_copy(l2.at[plane_own[a], row_own[c], :], l2, a, c, 1)

    send_all(near2, m2s, m2g, 1)

    for c in (1, -1):
        guard(c, lambda c=c: side(-c)[1].wait_recv() and None)

    bl0, bl1 = meta_n[4:5, :], meta_n[5:6, :]
    eb = spread(lw_n, bl0)

    def along(row, v):
        return jnp.sum(row * v, axis=1, keepdims=True)

    crow = c0_row(bl0, bl1)
    for_q, for_p = [[along(r, v) for v in adds] for r in (crow, bl0)]

    def fix(v, parts):
        one, two = v[:, 128:256], v[:, 256:384]
        one = one + jnp.where(lane == 126, parts[0], 0.0) + jnp.where(lane == 127, parts[1], 0.0)
        two = two + jnp.where(lane == 0, parts[2], 0.0) + jnp.where(lane == 1, parts[3], 0.0)
        return jnp.concatenate([v[:, 0:128], one, two, v[:, 384:512]], axis=1)

    qs, ps = fix(qs, for_q), fix(ps, for_p)
    a1 = a1 + along(collect(lw_n, bl0), adds[2])
    a2 = a2 + along(collect(lw_n, eb), adds[2])
    a3 = a3 + along(eb, adds[1])
    zr = row_iota((Z, R))
    pz = jnp.where(zr == 0, 0.0, pltpu.roll(ps, 1, 0)) + jnp.where(zr == Z - 1, 0.0, pltpu.roll(ps, Z - 1, 0))
    vv = qs + (ctr - (1.0 - 6 * DIFF - ADV) - 4 * DIFF) * ps + up * left(ps) + dn * right(ps) + DIFF * pz
    at255 = jnp.where(lane == 127, left(a1) - ps[:, 128:256], 0.0)
    at256 = jnp.where(lane == 0, a2 - right(a3), 0.0)
    vv = vv + DIFF * jnp.concatenate([zero, at255, -at256, zero], axis=1)
    top = jnp.where(ax == 0, 0.0, DIFF) * ps[0:1, :]
    bot = jnp.where(ax == NX - 1, 0.0, DIFF) * ps[15:16, :]

    def fold(v):
        v = v[:, 0:128] + v[:, 128:256] + v[:, 256:384] + v[:, 384:512]
        return jnp.sum(v, axis=0, keepdims=True)

    rowsum = []
    for m in range(M):
        rowsum.append(fold(bs[m] * vv) + fold(bh[0, m] * top + bh[1, m] * bot))
    rowsum.append(fold(ls) + jnp.sum(more * (2.0 * cols + more), axis=0, keepdims=True))
    rowsum.append(jnp.zeros((7, 128), f32))
    stack = jnp.concatenate(rowsum, axis=0)
    stack = jnp.broadcast_to(jnp.sum(stack, axis=1, keepdims=True), (24, 128))
    rrs[...] = jnp.sum(jnp.where(row_iota((24, 128)) == lane_iota((24, 128)), stack, 0.0), axis=0, keepdims=True)

    pl.semaphore_wait(ready, greeted)
    px, pz_, py, pc = (az >> 2) & 3, az & 3, (ax >> 1) * 2 + (az >> 4), ax & 1
    xs = [((px + d) & 3) << 2 for d in range(4)]
    zs = [(pz_ + d) & 3 for d in range(4)]
    ys = [(((py + d) & 1) << 4, (((py + d) >> 1) & 1) << 1) for d in range(4)]
    cs = [pc, 1 - pc]
    for x, y, z, c in OTHERS:
        pltpu.make_async_remote_copy(
            src_ref=rrs, dst_ref=rrr.at[OTHERS.index((-x % 4, -y % 4, -z % 4, c))], send_sem=rr_ss.at[0], recv_sem=rr_rs.at[0],
            device_id=(ys[y][0] + xs[x] + zs[z], ys[y][1] + cs[c]), device_id_type=MESH).start()

    def misfit_cols(offsets, only):
        return [jnp.where(inside, c, 0.0) for c in gather_cols(m2s, m2g, offsets, only, bases2)]

    def adjoint_cols(cs, lw):
        c254, c255, c256, c257 = cs
        flux, back = local_flux(lw, c255, c256)

        def one(c, out, term):
            return (1.0 - 5 * DIFF - ADV) * c + DIFF * (out + right(c) + beside(c)) + (DIFF + ADV) * left(c) + DIFF * term

        return flux, back, one(c255, c254, flux)[8:24], one(c256, c257, -back)[8:24]

    def step_l1(q, flux, back):
        v = l2[q + 1]
        new = stencil(v, l2[q + 2], l2[q], beside(v))
        put(l1, q, ally, new, flux, back, q + 15)

    def step_l0(j):
        v = l1[j + 1]
        sen[j] = stencil(v[8:24], l1[j + 2, 8:24, :], l1[j, 8:24, :], beside(v)[8:24])

    arrivals(near2, m2g, 1, SAME)
    seal(l2, 2, (0, 20))
    cols_o = misfit_cols(near_off, (0,))
    flux_n, back_n = local_flux(lw_n, cols_o[1], cols_o[2])

    def inner_l1(q, _):
        step_l1(q, flux_n, back_n)
        return 0

    def inner_l0(j, _):
        step_l0(j)
        return 0

    lax.fori_loop(3, 15, inner_l1, 0, unroll=4)
    seal(l1, 1, (3, 15))
    lax.fori_loop(3, 13, inner_l0, 0, unroll=5)
    arrivals(near2, m2g, 1, OPPOSITE)
    _, _, rot_f1, sta_f1 = adjoint_cols(misfit_cols(far_off, far_off), lw_f)

    arrivals(near2, m2g, 1, LATE)
    flux_n, back_n, rot_n1, sta_n1 = adjoint_cols([o + e for o, e in zip(cols_o, misfit_cols(near_off, (-1, 1)))], lw_n)
    fluxa, backa = opposite(w_n, w_f, rot_n1, sta_n1, rot_f1, sta_f1)
    for q in (0, 1, 2, 15, 16, 17):
        step_l1(q, flux_n, back_n)
    seal(l1, 1, (0, 3), (15, 18))
    for j in (0, 1, 2, 13, 14, 15):
        step_l0(j)
    for j in range(J):
        f, b = columns_at(fluxa, backa, j + 16)
        sen[j, :, 128:256] += DIFF * f
        sen[j, :, 256:384] -= DIFF * b

    whole(rrr, rr_ss.at[0], rr_rs.at[0]).wait_recv()
    total = rrs[...] + jnp.sum(rrr[...], axis=0)
    tot[...] = jnp.broadcast_to(total, (8, 128))

    departures(near1, m1g, 0)
    departures(near2, m2g, 1)
    for c in (1, -1):
        def act(c=c):
            for copy in side(c):
                copy.wait_send()
        guard(c, act)
    whole(rrr, rr_ss.at[0], rr_rs.at[0]).wait_send()


def finish(fin, sen, tot, fin_o, sen_o, grad_o, loss_o, sems):
    a = pltpu.make_async_copy(fin, fin_o, sems.at[0])
    b = pltpu.make_async_copy(sen, sen_o, sems.at[1])
    a.start()
    b.start()
    row = tot[0:1, :]
    grad_o[...] = row[:, 0:M] * (1.0 / COLUMNS)
    loss_o[...] = row[:, M : M + 1] * (0.5 / (COLUMNS * R))
    a.wait()
    b.wait()


def on_device(initial, target, basis, coefficients, blade, offset, extra, frac):
    vm = pl.BlockSpec(memory_space=pltpu.VMEM)
    hbm = pl.BlockSpec(memory_space=pltpu.HBM)
    block = jax.ShapeDtypeStruct((J, Z, R), f32)
    dma = pltpu.SemaphoreType.DMA
    fin, sen, tot = pl.pallas_call(
        kernel,
        out_shape=(pltpu.VMEM((J, Z, R), f32), pltpu.VMEM((J, Z, R), f32), pltpu.VMEM((8, 128), f32)),
        in_specs=[hbm] * 8,
        out_specs=(vm, vm, vm),
        scratch_shapes=[
            pltpu.VMEM((20, 32, R), f32), pltpu.VMEM((18, 32, R), f32),
            pltpu.VMEM((20, 32, R), f32), pltpu.VMEM((18, 32, R), f32),
            pltpu.VMEM((J, Z, R), f32), pltpu.VMEM((M, Z, R), f32), pltpu.VMEM((2, M, 1, R), f32),
            pltpu.VMEM((32, R), f32),
            *[pltpu.VMEM((8, 128), f32), [pltpu.VMEM((len(p), 8, 128), f32) for p in PARTNERS.values()]] * 2,
            pltpu.VMEM((1, 128), f32), pltpu.VMEM((NA * NX - 1, 1, 128), f32),
            pltpu.VMEM((6, 32, 128), f32),
            pltpu.VMEM((2, J), f32), pltpu.VMEM((2, J), jnp.int32), pltpu.VMEM((2, J), f32),
            pltpu.SMEM((M,), f32), pltpu.SMEM((2,), jnp.int32),
            dma((8,)), dma((2, 8)), dma((2, 8)), dma((2, 3, 3)), dma((2, 3, 3)), dma((2, 2)), dma((2, 2)), dma((1,)), dma((1,)),
            pltpu.SemaphoreType.REGULAR,
        ],
        compiler_params=pltpu.CompilerParams(collective_id=0, has_side_effects=True, vmem_limit_bytes=40 * 1024 * 1024),
    )(*(pltpu.with_memory_space_constraint(v, pltpu.HBM) for v in (initial, target, basis, coefficients, blade, offset, extra, frac)))
    fin, sen, grad, loss = pl.pallas_call(
        finish,
        out_shape=(block, block, jax.ShapeDtypeStruct((1, M), f32), jax.ShapeDtypeStruct((1, 1), f32)),
        in_specs=[vm] * 3,
        out_specs=(hbm, hbm, vm, vm),
        scratch_shapes=[dma((2,))],
    )(*(pltpu.with_memory_space_constraint(v, pltpu.VMEM) for v in (fin, sen, tot)))
    return fin, sen, grad.reshape(M), loss.reshape(())


def solution(mesh):
    block = P("az", "ax", None)
    row = P(None, "az")
    return jax.shard_map(
        on_device,
        mesh=mesh,
        in_specs=(block, block, P(None, "ax", None), P(), row, P(), row, row),
        out_specs=(block, block, P(), P()),
        check_vma=False,
    )
```

```python
import functools

import jax
import jax.numpy as jnp
from jax import lax
from jax.experimental import pallas as pl
from jax.experimental.pallas import tpu as pltpu
from jax.sharding import PartitionSpec as P

MESH = pl.DeviceIdType.MESH
f32 = jnp.float32
HI = lax.Precision.HIGHEST

NA, NX = 32, 4
J, Z, R, M = 16, 16, 512, 16
RI = 256
DIFF, ADV = 0.12, 0.2
COLUMNS = NA * J * NX * Z

NEAR = [(a, c) for a in (-1, 0, 1) for c in (-1, 0, 1) if (a, c) != (0, 0)]
FAR = [(a, c) for a in (14, 15, 16, 17, 18) for c in (-1, 0, 1)]
GROUPS = (0, 1, -1)
LATE, SAME, OPPOSITE = range(3)
PARTNERS = {
    (k, g): [(a, c) for a, c in NEAR + FAR if c == g and k == (OPPOSITE if a > 1 else LATE if a else SAME)]
    for k in range(3) for g in GROUPS if (k, g) != (SAME, 0)
}
ALWAYS = [(-1, 0), (1, 0), (0, -1), (0, 1)] + [(a, 0) for a in range(14, 19)] + [(16, -1), (16, 1)]
ALWAYS += [(a, c) for a in (-8, -4, 4, 8) for c in (0, 2)]
INSIDE = [-1, 1, 14, 15, 17, 18]
AROUND = [-4, 4]
def hops(t):
    az, ax = t // NX, t % NX
    at = ((az >> 2) & 3, az & 3, (ax >> 1) * 2 + (az >> 4))
    return sum(v > 0 for v in at) * 4 + sum(min(v, 4 - v) for v in at), t


TARGETS = sorted(range(NA * NX), key=hops)


def slot_of(a, c):
    k = OPPOSITE if 1 < a % NA < NA - 1 else LATE if a else SAME
    return k, [x % NA for x, _ in PARTNERS[k, c]].index(a % NA)


def lane_iota(shape):
    return lax.broadcasted_iota(jnp.int32, shape, len(shape) - 1)


def row_iota(shape):
    return lax.broadcasted_iota(jnp.int32, shape, len(shape) - 2)


def left(v):
    return pltpu.roll(v, v.shape[-1] - 1, v.ndim - 1)


def right(v):
    return pltpu.roll(v, 1, v.ndim - 1)


def kernel(
    u_h, t_h, basis_h, coef_h, blade_h, off_h, extra_h, frac_h,
    fin, sen, tot,
    x0, u1, l2, l1, tg, bs, bh, prof, m1s, m1r, m2s, m2r, rrs, rrr, bb,
    blade_v, extra_v, frac_v, coef_s, off_s,
    loc, near_ss, near_rs, m_ss, m_rs, side_ss, side_rs, rr_ss, rr_rs, ready,
):
    az, ax = lax.axis_index("az"), lax.axis_index("ax")

    def partner(a, c):
        return ((az + a) & (NA - 1), (ax + c) & (NX - 1))

    def guard(c, act):
        if c == 0:
            act()
        else:
            pl.when((ax < NX - 1) if c > 0 else (ax > 0))(act)

    loads = [
        pltpu.make_async_copy(u_h, x0.at[2:18, 8:24, :], loc.at[0]),
        pltpu.make_async_copy(blade_h, blade_v, loc.at[1]),
        pltpu.make_async_copy(extra_h, extra_v, loc.at[2]),
        pltpu.make_async_copy(frac_h, frac_v, loc.at[3]),
        pltpu.make_async_copy(coef_h, coef_s, loc.at[4]),
        pltpu.make_async_copy(off_h, off_s, loc.at[5]),
        pltpu.make_async_copy(basis_h, bs, loc.at[6]),
        pltpu.make_async_copy(t_h, tg, loc.at[7]),
    ]
    loads[0].start()
    barrier = pltpu.get_barrier_semaphore()

    def greet(sem):
        def signal(a, c):
            pl.semaphore_signal(sem, inc=1, device_id=partner(a, c), device_id_type=MESH)

        for a, c in ALWAYS:
            signal(a, c)
        for c in (1, -1):
            at_end = ax == (NX - 1 if c > 0 else 0)

            @pl.when(at_end)
            def _(c=c):
                for a in AROUND:
                    signal(a, c)

            @pl.when(jnp.logical_not(at_end))
            def _(c=c):
                for a in INSIDE:
                    signal(a, c)

    greeted = len(ALWAYS) + 2 * len(INSIDE) - jnp.where((ax == 0) | (ax == NX - 1), len(INSIDE) - len(AROUND), 0)
    greet(barrier)
    for c in loads[1:]:
        c.start()

    loads[0].wait()
    tile = (8, 128)
    lane8 = lane_iota(tile)

    def take(j, acc):
        for i, (lo, k) in enumerate(((128, 1), (256, 0))):
            for h in range(2):
                at = 16 + 16 * i + 32 * h + j
                acc = jnp.where(lane8 == at, pltpu.roll(x0[j + 2, 8 + 8 * h : 16 + 8 * h, lo : lo + 128], lax.rem(at + k, 128), 1), acc)
        return acc

    taken = lax.fori_loop(0, J, take, jnp.zeros(tile, f32), unroll=True)
    for c in loads[1:4]:
        c.wait()
    m1s[...] = jnp.zeros(tile, f32)
    m1s[0:2, 0:16] = extra_v[...].astype(f32)
    m1s[2:4, 0:16] = frac_v[...]
    m1s[4:6, 0:16] = blade_v[...]
    m1s[...] = m1s[...] + taken

    for i in (4, 6):
        loads[i].wait()

    def mix(m, acc):
        return acc + coef_s[m] * bs[m]

    prof[8:24, :] = lax.fori_loop(0, M, mix, jnp.zeros((Z, R), f32), unroll=4)

    pl.semaphore_wait(barrier, greeted)
    plane_dst = {-1: pl.ds(18, 2), 0: pl.ds(2, 16), 1: pl.ds(0, 2)}
    row_dst = {-1: pl.ds(24, 2), 0: pl.ds(8, 16), 1: pl.ds(6, 2)}
    plane_own = {-1: pl.ds(2, 2), 0: pl.ds(2, 16), 1: pl.ds(16, 2)}
    row_own = {-1: pl.ds(8, 2), 0: pl.ds(8, 16), 1: pl.ds(22, 2)}

    def near_copy(src, dst, a, c, n):
        i = NEAR.index((a, c))
        return pltpu.make_async_remote_copy(
            src_ref=src, dst_ref=dst.at[plane_dst[a], row_dst[c], :],
            send_sem=near_ss.at[n, i], recv_sem=near_rs.at[n, i],
            device_id=partner(a, c), device_id_type=MESH,
        )

    def message(src, dst, a, c, n):
        k, i = slot_of(-a, -c)
        return pltpu.make_async_remote_copy(
            src_ref=src, dst_ref=dst[k, -c].at[i],
            send_sem=m_ss.at[n, k, c + 1], recv_sem=m_rs.at[n, k, 1 - c],
            device_id=partner(a, c), device_id_type=MESH,
        )

    def near_group(k, c):
        return [n for n in NEAR if n[1] == c and (k == LATE) == (n[0] != 0)] if k != OPPOSITE else []

    def send_all(near_of, src, dst, n):
        for c in (1, -1, 0):
            def act(c=c):
                for k in (SAME, LATE, OPPOSITE):
                    for a, _ in near_group(k, c):
                        near_of(a, c).start()
                    for a, _ in PARTNERS.get((k, c), ()):
                        message(src, dst, a, c, n).start()
            guard(c, act)

    m1g = dict(zip(PARTNERS, m1r))
    m2g = dict(zip(PARTNERS, m2r))

    def near1(a, c):
        return near_copy(x0.at[plane_own[a], row_own[c], :], x0, a, c, 0)

    def side(c):
        i, src, dst = (0, 23, 7) if c > 0 else (1, 8, 24)
        return (
            pltpu.make_async_remote_copy(
                src_ref=prof.at[pl.ds(src, 1), :], dst_ref=prof.at[pl.ds(dst, 1), :],
                send_sem=side_ss.at[0, i], recv_sem=side_rs.at[0, i],
                device_id=partner(0, c), device_id_type=MESH),
            pltpu.make_async_remote_copy(
                src_ref=bs.at[:, pl.ds(src - 8, 1), :], dst_ref=bh.at[i],
                send_sem=side_ss.at[1, i], recv_sem=side_rs.at[1, i],
                device_id=partner(0, c), device_id_type=MESH),
        )

    for c in (1, -1):
        guard(c, lambda c=c: side(c)[0].start() and None)

    send_all(near1, m1s, m1g, 0)
    for c in (1, -1):
        guard(c, lambda c=c: side(c)[1].start() and None)


    greet(ready)

    for i in (5, 7):
        loads[i].wait()

    def whole(ref, ss, rs):
        return pltpu.make_async_remote_copy(
            src_ref=ref, dst_ref=ref, send_sem=ss, recv_sem=rs, device_id=partner(0, 1), device_id_type=MESH)

    def arrivals(near_of, dst, n, k):
        for c in GROUPS:
            def act(c=c):
                if (k, c) in PARTNERS:
                    whole(dst[k, c], m_ss.at[n, k, c + 1], m_rs.at[n, k, c + 1]).wait_recv()
                for a, _ in near_group(k, c):
                    near_of(-a, -c).wait_recv()
            guard(c, act)

    def departures(near_of, dst, n):
        for c in GROUPS:
            def act(c=c):
                for k in range(3):
                    if (k, c) in PARTNERS:
                        whole(dst[k, c], m_ss.at[n, k, c + 1], m_rs.at[n, k, c + 1]).wait_send()
                    for a, _ in near_group(k, c):
                        near_of(a, c).wait_send()
            guard(c, act)

    arrivals(near1, m1g, 0, SAME)
    for c in (1, -1):
        guard(c, lambda c=c: side(-c)[0].wait_recv() and None)
    lane32 = lane_iota((32, 128))

    near_off, far_off = (-1, 0, 1), (14, 15, 16, 17, 18)

    def gather_cols(own, ref, offsets, only, bases):
        def part(c, a, base, b):
            k, i = slot_of(a, c) if (a, c) != (0, 0) else (0, 0)
            v = own[...] if (a, c) == (0, 0) else ref[k, c][i]
            s = (16 * b - base) % 128
            return pltpu.roll(v, s, 1) if s else v

        cols = []
        for lo, hi in bases:
            out = jnp.zeros((32, 128), f32)
            for b, a in enumerate(offsets):
                if a not in only:
                    continue
                v = jnp.concatenate([part(-1, a, hi, b), part(0, a, lo, b), part(0, a, hi, b), part(1, a, lo, b)], axis=0)
                out = jnp.where((lane32 >= 16 * b) & (lane32 < 16 * b + 16), v, out)
            cols.append(out)
        return cols

    def gather_meta(offsets, only):
        out = jnp.zeros((8, 128), f32)
        for b, a in enumerate(offsets):
            if a not in only:
                continue
            k, i = slot_of(a, 0) if a else (0, 0)
            v = m1s[...] if a == 0 else m1g[k, 0][i]
            out = jnp.where((lane8 >= 16 * b) & (lane8 < 16 * b + 16), pltpu.roll(v, 16 * b, 1) if b else v, out)
        return out

    bases1 = ((16, 48), (32, 64))
    bases2 = ((0, 64), (16, 80), (32, 96), (48, 112))
    drift = off_s[0] - RI
    rows = row_iota((128, 128))
    lanes = lane_iota((128, 128))

    def weights(meta, base):
        w = meta[2:3, :]
        at = lanes + (drift + base) + meta[0:1, :].astype(jnp.int32)
        return jnp.where(rows == at, 1.0 - w, 0.0) + jnp.where(rows == at + 1, w, 0.0)

    def opposite(w_n, w_f, rn, sn, rf, sf):
        flux = jnp.dot(sf, w_n, precision=HI, preferred_element_type=f32) - rn
        fluxf = jnp.dot(sn, w_f, precision=HI, preferred_element_type=f32) - rf
        back = lax.dot_general(fluxf, w_f, (((1,), (1,)), ((), ())), precision=HI, preferred_element_type=f32)
        return flux, back

    def local_weights(meta):
        e, w = meta[1:2, :], meta[3:4, :]
        return (1.0 - e) * (1.0 - w), (1.0 - e) * w + e * (1.0 - w), e * w

    def spread(lw, v):
        return lw[0] * right(v) + lw[1] * v + lw[2] * left(v)

    def collect(lw, v):
        return left(lw[0] * v) + lw[1] * v + right(lw[2] * v)

    r32 = row_iota((32, 128))

    def c0_row(bl0, bl1):
        return (1.0 - 2 * DIFF) * bl0 + DIFF * (left(bl0) + right(bl0)) - ADV * (bl0 - right(bl0)) + bl1

    def plane_coefs(meta, lw):
        bl0, bl1 = meta[4:5, :], meta[5:6, :]
        eb = spread(lw, bl0)
        for i, v in enumerate((bl0, bl1, c0_row(bl0, bl1), collect(lw, bl0), collect(lw, eb), eb)):
            picked = jnp.where(lane32 == r32 + 15, jnp.broadcast_to(v, (32, 128)), 0.0)
            bb[i] = jnp.broadcast_to(jnp.sum(picked, axis=1, keepdims=True), (32, 128))

    def coef(i, q):
        return bb[i, pl.ds(q, 1), :]

    def wide(v):
        return jnp.concatenate([v] * 4, axis=1)

    ri = lane_iota((1, R))
    edge = (ri == RI - 1) | (ri == RI)
    ctr = jnp.where(edge, 1.0 - 5 * DIFF - ADV, 1.0 - 6 * DIFF - ADV).astype(f32)
    up = jnp.where((ri == RI - 1) | (ri == R - 1), 0.0, DIFF).astype(f32)
    dn = jnp.where((ri == RI) | (ri == 0), 0.0, DIFF).astype(f32)

    def stencil(v, strong, weak, vz):
        return ctr * v + up * left(v) + dn * right(v) + DIFF * (vz + weak) + (DIFF + ADV) * strong

    def beside(v):
        return pltpu.roll(v, 1, 0) + pltpu.roll(v, v.shape[0] - 1, 0)

    def columns_at(flux, back, k):
        ln = lane_iota(flux.shape)
        return (jnp.where(ln == 127, pltpu.roll(flux, (127 - k) & 127, 1), 0.0),
                jnp.where(ln == 0, pltpu.roll(back, (128 - k) & 127, 1), 0.0))

    def put(ref, idx, rows_, v, flux, back, k):
        f, b = columns_at(flux, back, k)
        ref[idx, rows_, 0:128] = v[:, 0:128]
        ref[idx, rows_, 128:256] = v[:, 128:256] + DIFF * f
        ref[idx, rows_, 256:384] = v[:, 256:384] - DIFF * b
        ref[idx, rows_, 384:512] = v[:, 384:512]

    def seal(ref, n, *parts):
        def clear(row):
            for lo, hi in parts:
                ref[lo:hi, pl.ds(row, n), :] = jnp.zeros((hi - lo, n, R), f32)

        pl.when(ax == 0)(lambda: clear(8 - n))
        pl.when(ax == NX - 1)(lambda: clear(24))

    ally, centre = slice(0, 32), slice(8, 24)
    lane = lane_iota((Z, 128))
    zero = jnp.zeros((Z, 128), f32)
    big = jnp.zeros((Z, R), f32)

    def step_u1(q):
        v = x0[q + 1]
        u1[q] = stencil(v, x0[q], x0[q + 2], beside(v)) + wide(coef(0, q)) * prof[...]

    def take1(q, rot, sta):
        a = pltpu.roll(u1[q, :, 128:256], (q + 16) & 127, 1)
        b = pltpu.roll(u1[q, :, 256:384], (q + 15) & 127, 1)
        return jnp.where(lane32 == q + 15, a, rot), jnp.where(lane32 == q + 15, b, sta)

    def step_u2(j, carry):
        ls, qs, ps, a1, a2, a3, cols = carry
        v = u1[j + 1]
        new = stencil(v[8:24], u1[j, 8:24, :], u1[j + 2, 8:24, :], beside(v)[8:24]) + wide(coef(1, j + 1)) * prof[8:24, :]
        fin[j] = new
        lam = new - tg[j]
        l2[j + 2, 8:24, :] = lam
        mid1, mid2 = lam[:, 128:256], lam[:, 256:384]
        for i, (t, l) in enumerate(((mid1, 126), (mid1, 127), (mid2, 0), (mid2, 1))):
            for h in range(2):
                k = j + bases2[i][h]
                cols = jnp.where(lane8 == k, pltpu.roll(t[8 * h : 8 * h + 8], (k + 128 - l) & 127, 1), cols)
        q = j + 1
        return (ls + lam * lam, qs + wide(coef(2, q)) * lam, ps + wide(coef(0, q)) * lam,
                a1 + coef(3, q) * mid2, a2 + coef(4, q) * mid2, a3 + coef(5, q) * mid1, cols)

    def local_flux(lw, rot, sta):
        flux = spread(lw, sta) - rot
        return flux, collect(lw, flux)

    meta_o = gather_meta(near_off, (0,))
    plane_coefs(meta_o, local_weights(meta_o))
    seal(x0, 2, (0, 20))

    def inner_u1(q, _):
        step_u1(q)
        return 0

    lax.fori_loop(2, 16, inner_u1, 0, unroll=14)
    seal(u1, 1, (2, 16))
    wide0 = jnp.zeros((32, 128), f32)
    rot1, sta1 = lax.fori_loop(2, 16, lambda q, c: take1(q, *c), (wide0, wide0), unroll=14)
    sums = lax.fori_loop(2, 14, step_u2, (big, big, big, zero, zero, zero, jnp.zeros(tile, f32)), unroll=6)

    arrivals(near1, m1g, 0, OPPOSITE)
    rot_f, sta_f = gather_cols(m1s, m1g, far_off, far_off, bases1)
    meta_f = gather_meta(far_off, far_off)
    w_f, lw_f = weights(meta_f, -16), local_weights(meta_f)
    rot_o, sta_o = gather_cols(m1s, m1g, near_off, (0,), bases1)

    arrivals(near1, m1g, 0, LATE)
    rot_e, sta_e = gather_cols(m1s, m1g, near_off, (-1, 1), bases1)
    rot_n, sta_n = rot_o + rot_e, sta_o + sta_e
    meta_n = meta_o + gather_meta(near_off, (-1, 1))
    lw_n, w_n = local_weights(meta_n), weights(meta_n, 16)
    flux0, back0 = opposite(w_n, w_f, rot_n, sta_n, rot_f, sta_f)
    plane_coefs(meta_n, lw_n)
    for q in (0, 1, 16, 17):
        step_u1(q)
    seal(u1, 1, (0, 2), (16, 18))
    for q in (0, 1, 16, 17):
        rot1, sta1 = take1(q, rot1, sta1)
    for j in (0, 1, 14, 15):
        sums = step_u2(j, sums)
    ls, qs, ps, a1, a2, a3, cols = sums

    zrow = row_iota((32, 128))
    inside = ((zrow >= 8) | (ax != 0)) & ((zrow < 24) | (ax != NX - 1))
    live = inside & (lane32 >= 15) & (lane32 <= 32)
    d255 = jnp.where(live, DIFF * flux0, 0.0)
    d256 = jnp.where(live, -DIFF * back0, 0.0)
    flux1, back1 = local_flux(lw_n, rot1 + d255, sta1 + d256)

    def pushed(d):
        return (1.0 - 5 * DIFF - ADV) * d + DIFF * (left(d) + beside(d)) + (DIFF + ADV) * right(d)

    own = (lane >= 16) & (lane < 32)
    adds = [jnp.where(own, v[8:24], 0.0)
            for v in (DIFF * d255, pushed(d255) + DIFF * flux1, pushed(d256) - DIFF * back1, DIFF * d256)]
    for j in (0, 1, 14, 15, *range(2, 14)):
        r = [pltpu.roll(v, (l - j - 16) & 127, 1) for v, l in zip(adds, (126, 127, 0, 1))]
        add1 = jnp.where(lane == 126, r[0], jnp.where(lane == 127, r[1], 0.0))
        add2 = jnp.where(lane == 0, r[2], jnp.where(lane == 1, r[3], 0.0))
        l2[j + 2, 8:24, 128:256] += add1
        l2[j + 2, 8:24, 256:384] += add2
        fin[j, :, 128:256] += add1
        fin[j, :, 256:384] += add2
    more = jnp.zeros(tile, f32)
    for i, v in enumerate(adds):
        for h in range(2):
            s = (bases2[i][h] - 16) & 127
            more = more + (pltpu.roll(v[8 * h : 8 * h + 8], s, 1) if s else v[8 * h : 8 * h + 8])
    m2s[...] = cols + more

    def near2(a, c):
        return near_copy(l2.at[plane_own[a], row_own[c], :], l2, a, c, 1)

    send_all(near2, m2s, m2g, 1)

    for c in (1, -1):
        guard(c, lambda c=c: side(-c)[1].wait_recv() and None)

    bl0, bl1 = meta_n[4:5, :], meta_n[5:6, :]
    eb = spread(lw_n, bl0)

    def along(row, v):
        return jnp.sum(row * v, axis=1, keepdims=True)

    crow = c0_row(bl0, bl1)
    for_q, for_p = [[along(r, v) for v in adds] for r in (crow, bl0)]

    def fix(v, parts):
        one, two = v[:, 128:256], v[:, 256:384]
        one = one + jnp.where(lane == 126, parts[0], 0.0) + jnp.where(lane == 127, parts[1], 0.0)
        two = two + jnp.where(lane == 0, parts[2], 0.0) + jnp.where(lane == 1, parts[3], 0.0)
        return jnp.concatenate([v[:, 0:128], one, two, v[:, 384:512]], axis=1)

    qs, ps = fix(qs, for_q), fix(ps, for_p)
    a1 = a1 + along(collect(lw_n, bl0), adds[2])
    a2 = a2 + along(collect(lw_n, eb), adds[2])
    a3 = a3 + along(eb, adds[1])
    zr = row_iota((Z, R))
    pz = jnp.where(zr == 0, 0.0, pltpu.roll(ps, 1, 0)) + jnp.where(zr == Z - 1, 0.0, pltpu.roll(ps, Z - 1, 0))
    vv = qs + (ctr - (1.0 - 6 * DIFF - ADV) - 4 * DIFF) * ps + up * left(ps) + dn * right(ps) + DIFF * pz
    at255 = jnp.where(lane == 127, left(a1) - ps[:, 128:256], 0.0)
    at256 = jnp.where(lane == 0, a2 - right(a3), 0.0)
    vv = vv + DIFF * jnp.concatenate([zero, at255, -at256, zero], axis=1)
    top = jnp.where(ax == 0, 0.0, DIFF) * ps[0:1, :]
    bot = jnp.where(ax == NX - 1, 0.0, DIFF) * ps[15:16, :]

    def fold(v):
        v = v[:, 0:128] + v[:, 128:256] + v[:, 256:384] + v[:, 384:512]
        return jnp.sum(v, axis=0, keepdims=True)

    rowsum = []
    for m in range(M):
        rowsum.append(fold(bs[m] * vv) + fold(bh[0, m] * top + bh[1, m] * bot))
    rowsum.append(fold(ls) + jnp.sum(more * (2.0 * cols + more), axis=0, keepdims=True))
    rowsum.append(jnp.zeros((7, 128), f32))
    stack = jnp.concatenate(rowsum, axis=0)
    stack = jnp.broadcast_to(jnp.sum(stack, axis=1, keepdims=True), (24, 128))
    rrs[...] = jnp.sum(jnp.where(row_iota((24, 128)) == lane_iota((24, 128)), stack, 0.0), axis=0, keepdims=True)

    pl.semaphore_wait(ready, greeted)
    me = az * NX + ax
    rrr[me] = rrs[...]
    for t in TARGETS:
        @pl.when(me != t)
        def _(t=t):
            pltpu.make_async_remote_copy(
                src_ref=rrs, dst_ref=rrr.at[me], send_sem=rr_ss.at[0], recv_sem=rr_rs.at[0],
                device_id=(t // NX, t % NX), device_id_type=MESH).start()

    def misfit_cols(offsets, only):
        return [jnp.where(inside, c, 0.0) for c in gather_cols(m2s, m2g, offsets, only, bases2)]

    def adjoint_cols(cs, lw):
        c254, c255, c256, c257 = cs
        flux, back = local_flux(lw, c255, c256)

        def one(c, out, term):
            return (1.0 - 5 * DIFF - ADV) * c + DIFF * (out + right(c) + beside(c)) + (DIFF + ADV) * left(c) + DIFF * term

        return flux, back, one(c255, c254, flux)[8:24], one(c256, c257, -back)[8:24]

    def step_l1(q, flux, back):
        v = l2[q + 1]
        new = stencil(v, l2[q + 2], l2[q], beside(v))
        put(l1, q, ally, new, flux, back, q + 15)

    def step_l0(j):
        v = l1[j + 1]
        sen[j] = stencil(v[8:24], l1[j + 2, 8:24, :], l1[j, 8:24, :], beside(v)[8:24])

    arrivals(near2, m2g, 1, SAME)
    seal(l2, 2, (0, 20))
    cols_o = misfit_cols(near_off, (0,))
    flux_n, back_n = local_flux(lw_n, cols_o[1], cols_o[2])

    def inner_l1(q, _):
        step_l1(q, flux_n, back_n)
        return 0

    def inner_l0(j, _):
        step_l0(j)
        return 0

    lax.fori_loop(3, 15, inner_l1, 0, unroll=4)
    seal(l1, 1, (3, 15))
    lax.fori_loop(3, 13, inner_l0, 0, unroll=5)
    arrivals(near2, m2g, 1, OPPOSITE)
    _, _, rot_f1, sta_f1 = adjoint_cols(misfit_cols(far_off, far_off), lw_f)

    arrivals(near2, m2g, 1, LATE)
    flux_n, back_n, rot_n1, sta_n1 = adjoint_cols([o + e for o, e in zip(cols_o, misfit_cols(near_off, (-1, 1)))], lw_n)
    fluxa, backa = opposite(w_n, w_f, rot_n1, sta_n1, rot_f1, sta_f1)
    for q in (0, 1, 2, 15, 16, 17):
        step_l1(q, flux_n, back_n)
    seal(l1, 1, (0, 3), (15, 18))
    for j in (0, 1, 2, 13, 14, 15):
        step_l0(j)
    for j in range(J):
        f, b = columns_at(fluxa, backa, j + 16)
        sen[j, :, 128:256] += DIFF * f
        sen[j, :, 256:384] -= DIFF * b

    others = rrr.at[pl.ds(0, NA * NX - 1)]
    whole(others, rr_ss.at[0], rr_rs.at[0]).wait_recv()
    total = jnp.sum(rrr[...], axis=0)
    tot[...] = jnp.broadcast_to(total, (8, 128))

    departures(near1, m1g, 0)
    departures(near2, m2g, 1)
    for c in (1, -1):
        def act(c=c):
            for copy in side(c):
                copy.wait_send()
        guard(c, act)
    whole(others, rr_ss.at[0], rr_rs.at[0]).wait_send()


def finish(fin, sen, tot, fin_o, sen_o, grad_o, loss_o, sems):
    a = pltpu.make_async_copy(fin, fin_o, sems.at[0])
    b = pltpu.make_async_copy(sen, sen_o, sems.at[1])
    a.start()
    b.start()
    row = tot[0:1, :]
    grad_o[...] = row[:, 0:M] * (1.0 / COLUMNS)
    loss_o[...] = row[:, M : M + 1] * (0.5 / (COLUMNS * R))
    a.wait()
    b.wait()


def on_device(initial, target, basis, coefficients, blade, offset, extra, frac):
    vm = pl.BlockSpec(memory_space=pltpu.VMEM)
    hbm = pl.BlockSpec(memory_space=pltpu.HBM)
    block = jax.ShapeDtypeStruct((J, Z, R), f32)
    dma = pltpu.SemaphoreType.DMA
    fin, sen, tot = pl.pallas_call(
        kernel,
        out_shape=(pltpu.VMEM((J, Z, R), f32), pltpu.VMEM((J, Z, R), f32), pltpu.VMEM((8, 128), f32)),
        in_specs=[hbm] * 8,
        out_specs=(vm, vm, vm),
        scratch_shapes=[
            pltpu.VMEM((20, 32, R), f32), pltpu.VMEM((18, 32, R), f32),
            pltpu.VMEM((20, 32, R), f32), pltpu.VMEM((18, 32, R), f32),
            pltpu.VMEM((J, Z, R), f32), pltpu.VMEM((M, Z, R), f32), pltpu.VMEM((2, M, 1, R), f32),
            pltpu.VMEM((32, R), f32),
            *[pltpu.VMEM((8, 128), f32), [pltpu.VMEM((len(p), 8, 128), f32) for p in PARTNERS.values()]] * 2,
            pltpu.VMEM((1, 128), f32), pltpu.VMEM((NA * NX, 1, 128), f32),
            pltpu.VMEM((6, 32, 128), f32),
            pltpu.VMEM((2, J), f32), pltpu.VMEM((2, J), jnp.int32), pltpu.VMEM((2, J), f32),
            pltpu.SMEM((M,), f32), pltpu.SMEM((2,), jnp.int32),
            dma((8,)), dma((2, 8)), dma((2, 8)), dma((2, 3, 3)), dma((2, 3, 3)), dma((2, 2)), dma((2, 2)), dma((1,)), dma((1,)),
            pltpu.SemaphoreType.REGULAR,
        ],
        compiler_params=pltpu.CompilerParams(collective_id=0, has_side_effects=True, vmem_limit_bytes=40 * 1024 * 1024),
    )(*(pltpu.with_memory_space_constraint(v, pltpu.HBM) for v in (initial, target, basis, coefficients, blade, offset, extra, frac)))
    fin, sen, grad, loss = pl.pallas_call(
        finish,
        out_shape=(block, block, jax.ShapeDtypeStruct((1, M), f32), jax.ShapeDtypeStruct((1, 1), f32)),
        in_specs=[vm] * 3,
        out_specs=(hbm, hbm, vm, vm),
        scratch_shapes=[dma((2,))],
    )(*(pltpu.with_memory_space_constraint(v, pltpu.VMEM) for v in (fin, sen, tot)))
    return fin, sen, grad.reshape(M), loss.reshape(())


def solution(mesh):
    block = P("az", "ax", None)
    row = P(None, "az")
    return jax.shard_map(
        on_device,
        mesh=mesh,
        in_specs=(block, block, P(None, "ax", None), P(), row, P(), row, row),
        out_specs=(block, block, P(), P()),
        check_vma=False,
    )
```
